32 devices in a mesh: rep: 2 (over core), shard: 16 (over z, y, x).
Axes of the slice: x: 2, y: 2, z: 4, core: 2. Of those that a mesh axis runs over, the one named last changes fastest.
Arguments:
- region_features: bfloat16 [16384, 768], P(('rep', 'shard')), may hold values from -3000 to 3000, as said below
- text_ids: int32 [16384], P(('rep', 'shard')), may hold values from 0 to 15359
- boxes: int32 [16384, 4], P(('rep', 'shard')), may hold values from 0 to 1023
- segment_ids: int32 [16384], P(('rep', 'shard')), may hold values from 0 to 511
- document_lengths: int32 [32, 4], P(('rep', 'shard')), may hold values from 0 to 512, as said below
- cotangent: bfloat16 [16384, 768], P(('rep', 'shard')), may hold values from -6 to 6
- batch_gain: bfloat16 [768], P('shard'), may hold values from 0.5 to 2
- batch_bias: bfloat16 [768], P('shard'), may hold values from -3 to 3
- text_table: bfloat16 [15360, 768], P('shard'), may hold values from -6 to 6
- side_table: bfloat16 [2560, 768], P('shard'), may hold values from -3 to 3
- embed_gain: bfloat16 [768], P('shard'), may hold values from 0.5 to 2
- embed_bias: bfloat16 [768], P('shard'), may hold values from -3 to 3
- in_weight: bfloat16 [768, 2304], P('shard'), may hold values from -0.21875 to 0.21875
- in_bias: bfloat16 [1536], P('shard'), may hold values from -3 to 3
- out_weight: bfloat16 [768, 768], P('shard'), may hold values from -0.875 to 0.875
- out_bias: bfloat16 [768], P('shard'), may hold values from -3 to 3
- first_gain: bfloat16 [768], P('shard'), may hold values from 0.5 to 2
- first_bias: bfloat16 [768], P('shard'), may hold values from -3 to 3
- up_weight: bfloat16 [768, 3072], P('shard'), may hold values from -0.21875 to 0.21875
- up_bias: bfloat16 [3072], P('shard'), may hold values from -3 to 3
- down_weight: bfloat16 [3072, 768], P('shard'), may hold values from -0.109375 to 0.109375
- down_bias: bfloat16 [768], P('shard'), may hold values from -3 to 3
- second_gain: bfloat16 [768], P('shard'), may hold values from 0.5 to 2
- second_bias: bfloat16 [768], P('shard'), may hold values from -3 to 3
Outputs:
- out_rows: bfloat16 [16384, 768], P(('rep', 'shard'))
- feature_grad: bfloat16 [16384, 768], P(('rep', 'shard'))
- batch_gain_grad: float32 [768], P('shard')
- batch_bias_grad: float32 [768], P('shard')
- text_table_grad: float32 [15360, 768], P('shard')
- side_table_grad: float32 [2560, 768], P('shard')
- embed_gain_grad: float32 [768], P('shard')
- embed_bias_grad: float32 [768], P('shard')
- in_weight_grad: float32 [768, 2304], P('shard')
- in_bias_grad: float32 [1536], P('shard')
- out_weight_grad: float32 [768, 768], P('shard')
- out_bias_grad: float32 [768], P('shard')
- first_gain_grad: float32 [768], P('shard')
- first_bias_grad: float32 [768], P('shard')
- up_weight_grad: float32 [768, 3072], P('shard')
- up_bias_grad: float32 [3072], P('shard')
- down_weight_grad: float32 [3072, 768], P('shard')
- down_bias_grad: float32 [768], P('shard')
- second_gain_grad: float32 [768], P('shard')
- second_bias_grad: float32 [768], P('shard')
The draws below stay inside these ranges and needn't reach their ends.
Inputs may be any that keep to these rules, and one draw needn't show every extreme that they name: `document_lengths`: each row lists, in order from the block's start, the lengths of the 1 to 4 documents packed into one block of 512 rows, zeros after the last; each document has 30 to 512 rows, they fill at least half of the block, and the rest of the block is padding. Some block holds a single document of 512 rows. `region_features`: visual features of the tokens' regions, one row a token.
All inputs are finite; a program needn't handle non-finite values.
Results may differ from the reference program's by a relative error of at most 0.015.
Values may be sent and summed in bfloat16 or wider, within the bound.
A program may use at most 192 MiB of HBM per device.

```python
import math
import jax
import jax.numpy as jnp
import numpy as np
from jax import lax

D = 768
HEADS = 12
HEAD = 64
FF = 3072
VOCAB = 15360
BINS = 1024
SEGMENTS = 512
SIDE = 2560
BLOCK = 512
SLOTS = 4
MIN_DOC = 30
BLOCKS = 32
ROWS = 16384


def draw_region_features(key, part):
    key = jax.random.fold_in(key, 11)
    keys = jax.random.split(key, 4)
    place = (jnp.arange(ROWS) // BLOCK).astype(jnp.float32) / (BLOCKS - 1)
    rise = 1.0 + 2.0 * place
    offset = jax.random.uniform(keys[0], (D,), minval=-1.0, maxval=1.0)
    column_scale = jnp.exp(jax.random.uniform(keys[1], (D,), minval=jnp.log(0.3), maxval=jnp.log(3.0)))
    noise = jax.random.truncated_normal(keys[2], -4.0, 4.0, (ROWS, D))
    row_scale = jnp.exp(jax.random.uniform(keys[3], (ROWS, 1), minval=0.0, maxval=jnp.log(10.0)))
    values = (offset[None, :] + noise) * column_scale[None, :] * row_scale * rise[:, None]
    return values.astype(jnp.bfloat16)


def draw_document_lengths(key, part):
    key = jax.random.fold_in(key, 23)
    keys = jax.random.split(key, 4)
    filled = jax.random.randint(keys[0], (BLOCKS, 1), BLOCK // 2, BLOCK + 1)
    docs = jax.random.randint(keys[1], (BLOCKS, 1), 1, SLOTS + 1)
    spare = filled - docs * MIN_DOC
    cuts = jnp.sort(jax.random.randint(keys[2], (BLOCKS, SLOTS - 1), 0, BLOCK + 1) % (spare + 1), axis=1)
    slot = jnp.arange(SLOTS - 1)[None, :]
    bounds = jnp.where(slot < docs - 1, cuts, spare)
    edges = jnp.concatenate([jnp.zeros((BLOCKS, 1), jnp.int32), bounds, spare], axis=1)
    pieces = edges[:, 1:] - edges[:, :-1]
    every = jnp.arange(SLOTS)[None, :]
    lengths = jnp.where(every < docs, MIN_DOC + pieces, 0)
    chosen = jax.random.randint(keys[3], (), 0, BLOCKS)
    single = jnp.where(every == 0, BLOCK, 0)
    lengths = jnp.where((jnp.arange(BLOCKS) == chosen)[:, None], single, lengths)
    return lengths.astype(jnp.int32)


def with_ends(values, rng, low, top_value):
    extent = values.shape
    index_at = [jax.random.randint(jax.random.fold_in(rng, axis), (), 0, extent[axis]) for axis in range(len(extent))]
    values = values.at[tuple(index_at)].set(low)
    longest = extent.index(max(extent))
    index_at[longest] = (index_at[longest] + 1) % extent[longest]
    return values.at[tuple(index_at)].set(top_value)


def steps_of(key, shape, shards, least, top_value):
    loudness = 1.0
    for position, shards_of in shards:
        draws = jax.random.uniform(jax.random.fold_in(jax.random.fold_in(key, 6), position), (shards_of,), jnp.float32, least / len(shards), top_value / len(shards))
        loudness = loudness * jnp.repeat(jnp.exp(draws), shape[position] // shards_of).reshape((-1,) + (1,) * (len(shape) - 1 - position))
    return loudness


def cumulative_ranks(number_of, skew):
    loads = [(1 << 20) // math.isqrt(rank ** skew) + 1 for rank in range(1, number_of + 1)]
    width = 1 + sum(loads) // (1 << 30)
    return np.cumsum(np.array([max(1, weight // width) for weight in loads]))


def ranked(stream_key, shape, number_of, lean):
    grid = cumulative_ranks(number_of, lean)
    ticket = jax.random.randint(jax.random.fold_in(stream_key, 1), shape, 0, int(grid[number_of - 1]))
    rank = jnp.searchsorted(jnp.asarray(grid, jnp.int32), ticket, side="right")
    return jax.random.permutation(jax.random.fold_in(stream_key, 2), number_of)[rank].astype(jnp.int32)


def scatter_about(rng, extent, scale, limit, shards=(), kind=jnp.bfloat16):
    array = scale * jax.random.normal(rng, extent, jnp.float32)
    if shards:
        array = array * steps_of(rng, extent, shards, -0.22, 0.18)
    return jnp.clip(array, -limit, limit).astype(kind)


def setup_inputs(seed: int = 0) -> dict:
    key_list = jax.random.split(jax.random.key(seed), 25)
    region_features = draw_region_features(jax.random.fold_in(key_list[24], 71), 0)
    text_ids = with_ends(ranked(key_list[1], (ROWS,), VOCAB, 2), jax.random.fold_in(key_list[1], 3), 0, VOCAB - 1).astype(jnp.int32)
    boxes = with_ends(jax.random.randint(key_list[2], (ROWS, 4), 0, BINS), jax.random.fold_in(key_list[2], 1), 0, BINS - 1).astype(jnp.int32)
    segment_ids = with_ends(jax.random.randint(key_list[3], (ROWS,), 0, SEGMENTS), jax.random.fold_in(key_list[3], 1), 0, SEGMENTS - 1).astype(jnp.int32)
    document_lengths = draw_document_lengths(jax.random.fold_in(key_list[24], 71), 0)
    cotangent = scatter_about(key_list[5], (ROWS, D), 1.0, 6.0, ((0, 32),))
    batch_gain = jnp.clip(jnp.exp(math.log(2.0) - 1.3862944 * jax.random.uniform(key_list[6], (D,), jnp.float32) ** steps_of(key_list[6], (D,), ((0, 16),), -0.2, 0.2)), 0.5, 2.0).astype(jnp.bfloat16)
    batch_bias = scatter_about(key_list[7], (D,), 0.5, 3.0, ((0, 16),))
    text_table = scatter_about(key_list[8], (VOCAB, D), 1.0, 6.0, ((0, 16),))
    side_table = scatter_about(key_list[9], (SIDE, D), 0.5, 3.0, ((0, 16),))
    embed_gain = jnp.clip(jnp.exp(math.log(2.0) - 1.3862944 * jax.random.uniform(key_list[10], (D,), jnp.float32) ** steps_of(key_list[10], (D,), ((0, 16),), -0.2, 0.2)), 0.5, 2.0).astype(jnp.bfloat16)
    embed_bias = scatter_about(key_list[11], (D,), 0.5, 3.0, ((0, 16),))
    in_weight = scatter_about(key_list[12], (D, 3 * D), D ** -0.5, 0.21875, ((0, 16),))
    in_bias = scatter_about(key_list[13], (2 * D,), 0.5, 3.0, ((0, 16),))
    out_weight = scatter_about(key_list[14], (D, D), (D // 16) ** -0.5, 0.875, ((0, 16),))
    out_bias = scatter_about(key_list[15], (D,), 0.5, 3.0, ((0, 16),))
    first_gain = jnp.clip(jnp.exp(math.log(2.0) - 1.3862944 * jax.random.uniform(key_list[16], (D,), jnp.float32) ** steps_of(key_list[16], (D,), ((0, 16),), -0.2, 0.2)), 0.5, 2.0).astype(jnp.bfloat16)
    first_bias = scatter_about(key_list[17], (D,), 0.5, 3.0, ((0, 16),))
    up_weight = scatter_about(key_list[18], (D, FF), D ** -0.5, 0.21875, ((0, 16),))
    up_bias = scatter_about(key_list[19], (FF,), 0.5, 3.0, ((0, 16),))
    down_weight = scatter_about(key_list[20], (FF, D), FF ** -0.5, 0.109375, ((0, 16),))
    down_bias = scatter_about(key_list[21], (D,), 0.5, 3.0, ((0, 16),))
    second_gain = jnp.clip(jnp.exp(math.log(2.0) - 1.3862944 * jax.random.uniform(key_list[22], (D,), jnp.float32) ** steps_of(key_list[22], (D,), ((0, 16),), -0.2, 0.2)), 0.5, 2.0).astype(jnp.bfloat16)
    second_bias = scatter_about(key_list[23], (D,), 0.5, 3.0, ((0, 16),))
    return {"region_features": region_features, "text_ids": text_ids, "boxes": boxes, "segment_ids": segment_ids, "document_lengths": document_lengths, "cotangent": cotangent, "batch_gain": batch_gain, "batch_bias": batch_bias, "text_table": text_table, "side_table": side_table, "embed_gain": embed_gain, "embed_bias": embed_bias, "in_weight": in_weight, "in_bias": in_bias, "out_weight": out_weight, "out_bias": out_bias, "first_gain": first_gain, "first_bias": first_bias, "up_weight": up_weight, "up_bias": up_bias, "down_weight": down_weight, "down_bias": down_bias, "second_gain": second_gain, "second_bias": second_bias}


@jax.custom_vjp
def low(v):
    return lax.optimization_barrier(v.astype(jnp.bfloat16)).astype(jnp.float32)

@jax.custom_vjp
def low_back(v):
    return v

def low_keep(v):
    return (low(v), None)

def low_pass(kept, grad):
    return (grad,)

def back_keep(v):
    return (v, None)

def back_low(kept, grad):
    return (low(grad),)
low.defvjp(low_keep, low_pass)
low_back.defvjp(back_keep, back_low)
HIGH = lax.Precision.HIGHEST
epsilon = 1e-05

def norm_rows(value, gain, shift):
    center = value - lax.optimization_barrier(jnp.mean(value, axis=-1, keepdims=True))
    spread = lax.rsqrt(lax.optimization_barrier(jnp.mean(center * center, axis=-1, keepdims=True)) + epsilon)
    return center * spread * gain + shift

def attend_block(operands):
    query, keys, values, member = operands
    query = query.reshape(BLOCK, HEADS, HEAD)
    keys = keys.reshape(BLOCK, HEADS, HEAD)
    values = values.reshape(BLOCK, HEADS, HEAD)
    scores = low_back(jnp.einsum('qhd,khd->hqk', query, keys, precision=HIGH) * 0.125)
    same = member[:, None] == member[None, :]
    scores = jnp.where(same[None], scores, -1e+30)
    top = lax.optimization_barrier(jnp.max(scores, axis=-1, keepdims=True))
    expo = jnp.exp(scores - top)
    probs = expo / lax.optimization_barrier(jnp.sum(expo, axis=-1, keepdims=True))
    context = jnp.einsum('hqk,khd->qhd', low(probs), values, precision=HIGH)
    return context.reshape(BLOCK, D)

def reference(region_features, text_ids, boxes, segment_ids, document_lengths, cotangent, batch_gain, batch_bias, text_table, side_table, embed_gain, embed_bias, in_weight, in_bias, out_weight, out_bias, first_gain, first_bias, up_weight, up_bias, down_weight, down_bias, second_gain, second_bias):
    ends = jnp.cumsum(document_lengths, axis=1).astype(jnp.int32)
    place = jnp.arange(BLOCK, dtype=jnp.int32)
    member = lax.optimization_barrier(jnp.sum((place[None, :, None] >= ends[:, None, :]).astype(jnp.int32), axis=2))
    valid_rows = (member < SLOTS).astype(jnp.float32).reshape(ROWS, 1)
    member_groups = member.reshape(BLOCKS // 8, 8, BLOCK)
    side_index = (boxes[:, 0], boxes[:, 2], boxes[:, 1] + BINS, boxes[:, 3] + BINS, segment_ids + 2 * BINS)
    params = tuple((value.astype(jnp.float32) for value in (batch_gain, batch_bias, text_table, side_table, embed_gain, embed_bias, in_weight, in_bias, out_weight, out_bias, first_gain, first_bias, up_weight, up_bias, down_weight, down_bias, second_gain, second_bias)))
    features = region_features.astype(jnp.float32)

    def forward(features, batch_gain, batch_bias, text_table, side_table, embed_gain, embed_bias, in_weight, in_bias, out_weight, out_bias, first_gain, first_bias, up_weight, up_bias, down_weight, down_bias, second_gain, second_bias):
        count = jnp.sum(valid_rows)
        mean = lax.optimization_barrier(jnp.sum(features * valid_rows, axis=0)) / count
        center = features - mean
        variance = lax.optimization_barrier(jnp.sum(center * center * valid_rows, axis=0)) / count
        batch_out = center * lax.rsqrt(variance + epsilon) * batch_gain + batch_bias
        looked = jnp.take(text_table, text_ids, axis=0)
        for column in side_index:
            looked = looked + jnp.take(side_table, column, axis=0)
        start = batch_out + low_back(looked)
        embedded = norm_rows(start, embed_gain, embed_bias)

        def group_layer(operands):
            rows, members = operands
            mixed = jnp.dot(low(rows), in_weight, precision=HIGH)
            query = low_back(low(mixed[:, :D] + in_bias[:D]))
            keys = low_back(low(mixed[:, D:2 * D]))
            values = low_back(low(mixed[:, 2 * D:] + in_bias[D:]))
            context = lax.map(jax.checkpoint(attend_block), (query.reshape(8, BLOCK, D), keys.reshape(8, BLOCK, D), values.reshape(8, BLOCK, D), members))
            context = low_back(low(context.reshape(8 * BLOCK, D)))
            branch = low_back(jnp.dot(context, out_weight, precision=HIGH) + out_bias)
            first = norm_rows(rows + branch, first_gain, first_bias)
            hidden = low_back(jnp.dot(low(first), up_weight, precision=HIGH) + up_bias)
            active = low(jax.nn.gelu(hidden, approximate=False))
            second = low_back(jnp.dot(active, down_weight, precision=HIGH) + down_bias)
            return norm_rows(first + second, second_gain, second_bias)
        final = lax.map(jax.checkpoint(group_layer), (embedded.reshape(BLOCKS // 8, 8 * BLOCK, D), member_groups))
        return final.reshape(ROWS, D)
    final, pullback = jax.vjp(forward, features, *params)
    grads = pullback(cotangent.astype(jnp.float32) * valid_rows)
    feature_grad, batch_gain_grad, batch_bias_grad, text_table_grad, side_table_grad, embed_gain_grad, embed_bias_grad, in_weight_grad, in_bias_grad, out_weight_grad, out_bias_grad, first_gain_grad, first_bias_grad, up_weight_grad, up_bias_grad, down_weight_grad, down_bias_grad, second_gain_grad, second_bias_grad = grads
    return (final.astype(jnp.bfloat16), feature_grad.astype(jnp.bfloat16), batch_gain_grad, batch_bias_grad, text_table_grad, side_table_grad, embed_gain_grad, embed_bias_grad, in_weight_grad, in_bias_grad, out_weight_grad, out_bias_grad, first_gain_grad, first_bias_grad, up_weight_grad, up_bias_grad, down_weight_grad, down_bias_grad, second_gain_grad, second_bias_grad)
```

```python
import functools
import math

import jax
import jax.numpy as jnp
from jax import lax
from jax.experimental import pallas as pl
from jax.experimental.pallas import tpu as pltpu
from jax.sharding import PartitionSpec as P

HEAD = 64
BINS = 1024
SIDE = 2560
BLOCK = 512
SLOTS = 4
CAP = 48
LANES = 128
MESH = pl.DeviceIdType.MESH
f32 = jnp.float32
bf16 = jnp.bfloat16

epsilon = 1e-05


def widen(value):
    return value.astype(jnp.float32)


def mm(a, b):
    return jnp.dot(a, b, preferred_element_type=f32)


def mm_nt(a, b):
    return lax.dot_general(a, b, (((1,), (1,)), ((), ())), preferred_element_type=f32)


def iota(shape, dim):
    return lax.broadcasted_iota(jnp.int32, shape, dim)


def spot():
    shard = lax.axis_index("shard")
    return lax.axis_index("rep"), shard // 4, (shard // 2) % 2, shard % 2


def at(z, y, x):
    return z * 4 + y * 2 + x


def rows_of(start, size, step):
    return pl.ds(pl.multiple_of(start * size, step), size)


class Gather:
    def __init__(self, index, shard_ref, full_ref, own_sem, send_sem, recv_sem, twin_sem):
        self.index, self.shard, self.full = index, shard_ref, full_ref
        self.own_sem, self.send_sem, self.recv_sem, self.twin_sem = own_sem, send_sem, recv_sem, twin_sem
        self.rep, self.z, self.y, self.x = spot()
        self.me = at(self.z, self.y, self.x)
        self.rows = shard_ref.shape[0]
        self.half = shard_ref.shape[1] // 2

    def block(self, source, half):
        return self.full.at[
            rows_of(source, self.rows, 16), rows_of(half, self.half, LANES)
        ]

    def copy(self, source, slot, target, src=None, twin=False):
        return pltpu.make_async_remote_copy(
            src_ref=self.block(source, self.rep) if src is None else src,
            dst_ref=self.block(source, self.rep),
            send_sem=self.send_sem.at[self.index, slot],
            recv_sem=(self.twin_sem if twin else self.recv_sem).at[self.index, source],
            device_id=target,
            device_id_type=MESH,
        )

    def own(self):
        return pltpu.make_async_copy(
            self.shard, self.full.at[rows_of(self.me, self.rows, 16)], self.own_sem.at[self.index]
        )

    def start(self):
        src = self.shard.at[:, rows_of(self.rep, self.half, LANES)]

        def step(k, carry):
            there = lax.rem(self.z + k, 4)
            self.copy(self.me, there, (self.rep, at(there, self.y, self.x)), src=src).start()
            return carry

        lax.fori_loop(1, 4, step, 0)
        self.own().start()

    def to_twin(self, source):
        self.copy(source, 16 + source, (1 - self.rep, self.me), twin=True).start()

    def beside(self, plane, swap):
        even = lax.rem(plane + self.y + self.x + swap, 2) == 0
        return (
            self.rep,
            at(self.z, jnp.where(even, self.y, 1 - self.y), jnp.where(even, 1 - self.x, self.x)),
        )

    def hop_one(self):
        self.own().wait()

        def step(k, carry):
            plane = lax.rem(self.z + k, 4)
            source = at(plane, self.y, self.x)

            @pl.when(k > 0)
            def _():
                self.copy(source, 0, (self.rep, self.me)).wait_recv()

            self.copy(source, 4 + plane, self.beside(plane, 0)).start()

            @pl.when(k > 0)
            def _():
                self.to_twin(source)

            return carry

        lax.fori_loop(0, 4, step, 0)

        def again(k, carry):
            plane = lax.rem(self.z + k, 4)
            source = at(plane, self.y, self.x)
            self.copy(source, 8 + plane, self.beside(plane, 1)).start()
            return carry

        lax.fori_loop(0, 4, again, 0)

    def hop_two(self):
        def step(k, carry):
            plane = lax.rem(self.z + k, 4)
            even = lax.rem(plane + self.y + self.x, 2) == 0
            source = at(
                plane, jnp.where(even, 1 - self.y, self.y), jnp.where(even, self.x, 1 - self.x)
            )
            self.copy(source, 0, (self.rep, self.me)).wait_recv()
            self.copy(source, 12 + plane, self.beside(plane, 0)).start()
            self.to_twin(source)
            return carry

        lax.fori_loop(0, 4, step, 0)

    def last(self):
        def step(k, carry):
            plane = lax.rem(self.z + k, 4)
            even = lax.rem(plane + self.y + self.x, 2) == 0
            near = at(
                plane, jnp.where(even, self.y, 1 - self.y), jnp.where(even, 1 - self.x, self.x)
            )
            far = at(plane, 1 - self.y, 1 - self.x)
            for source in (near, far):
                self.copy(source, 0, (self.rep, self.me)).wait_recv()
                self.to_twin(source)
            return carry

        lax.fori_loop(0, 4, step, 0)

    def ready(self):
        def step(k, carry):
            source = lax.rem(self.me + k, 16)
            pltpu.make_async_remote_copy(
                src_ref=self.block(source, 1 - self.rep),
                dst_ref=self.block(source, 1 - self.rep),
                send_sem=self.send_sem.at[self.index, 0],
                recv_sem=self.twin_sem.at[self.index, source],
                device_id=(self.rep, self.me),
                device_id_type=MESH,
            ).wait_recv()
            return carry

        lax.fori_loop(1, 16, step, 0)

    def drain(self):
        def step(k, carry):
            @pl.when((k != self.z) & (k != 16 + self.me))
            def _():
                self.copy(self.me, k, (self.rep, self.me)).wait_send()

            return carry

        lax.fori_loop(0, 32, step, 0)


def exchange_all(outbox, inbox, send_sem, recv_sem, start):
    rep, shard = lax.axis_index("rep"), lax.axis_index("shard")
    mine = rep * 16 + shard

    def copy(k):
        there = lax.rem(mine + k, 32)
        return there, pltpu.make_async_remote_copy(
            src_ref=outbox.at[lax.rem(there, 16)],
            dst_ref=inbox.at[mine],
            send_sem=send_sem.at[k],
            recv_sem=recv_sem.at[mine],
            device_id=(there // 16, lax.rem(there, 16)),
            device_id_type=MESH,
        )

    if start:

        def step(k, carry):
            copy(k)[1].start()
            return carry

        lax.fori_loop(1, 32, step, 0)
        return

    def done(k, carry):
        there, sent = copy(k)
        sent.wait_send()
        pltpu.make_async_remote_copy(
            src_ref=outbox.at[0],
            dst_ref=inbox.at[there],
            send_sem=send_sem.at[k],
            recv_sem=recv_sem.at[there],
            device_id=(rep, shard),
            device_id_type=MESH,
        ).wait_recv()
        return carry

    lax.fori_loop(1, 32, done, 0)


def greet_all():
    barrier = pltpu.get_barrier_semaphore()
    mine = lax.axis_index("rep") * 16 + lax.axis_index("shard")

    def step(k, carry):
        there = lax.rem(mine + k, 32)
        pl.semaphore_signal(
            barrier, inc=1, device_id=(there // 16, lax.rem(there, 16)), device_id_type=MESH
        )
        return carry

    lax.fori_loop(1, 32, step, 0)
    return barrier


def members(lens_ref, shape, dim):
    place = iota(shape, dim)
    end = jnp.int32(0)
    member = jnp.zeros(shape, jnp.int32)
    for slot in range(SLOTS):
        end = end + lens_ref[0, slot]
        member = member + (place >= end).astype(jnp.int32)
    return member


def spread_rows(value):
    return lax.rsqrt(jnp.mean(value * value, axis=-1, keepdims=True) + epsilon)


def onehot(condition):
    return jnp.where(condition, 1.0, 0.0).astype(bf16)


def remainder(shape, dim, offset, size):
    place = iota(shape, dim).astype(f32) - offset
    group = jnp.floor((place + 0.5) * (1.0 / size))
    return group, place - group * size


def expand_vectors(packed):
    def select(low, width, offset, size):
        _, want = remainder((1, size * 16), 1, 0, size)
        depth = iota((width, 1), 0).astype(f32) + (low - offset)
        return onehot(depth == want)

    kinds, _ = remainder((1, 768), 1, 0, 48)
    stacked = jnp.concatenate(
        [jnp.where(kinds == k, packed, 0.0) for k in range(10)], axis=0
    ).astype(bf16)
    _, depth = remainder((768, 1), 0, 0, 48)
    _, want = remainder((1, 768), 1, 0, 48)
    spread = mm(stacked, onehot(depth == want))
    owner, _ = remainder((1, 768), 1, 0, 48)
    shard_of = iota((16, 1), 0).astype(f32)
    narrow = jnp.concatenate(
        [
            jnp.sum(jnp.where(owner == shard_of, spread[k * 16 : k * 16 + 16], 0.0), axis=0, keepdims=True)
            for k in range(10)
        ],
        axis=0,
    )
    low = packed.astype(bf16)
    owner, _ = remainder((1, 1536), 1, 0, 96)
    middle = mm(low[:, 384:640], select(384, 256, 480, 96))
    middle = jnp.sum(jnp.where(owner == shard_of, middle, 0.0), axis=0, keepdims=True)
    owner, _ = remainder((1, 3072), 1, 0, 192)
    wide = mm(low[:, 512:768], select(512, 256, 576, 192))
    wide = jnp.sum(jnp.where(owner == shard_of, wide, 0.0), axis=0, keepdims=True)
    return narrow, middle, wide


def transpose_to(target, source):
    for j in range(source.shape[1] // LANES):
        target[j * LANES : (j + 1) * LANES, :] = jnp.transpose(
            source[:, j * LANES : (j + 1) * LANES]
        )


def forward_kernel(
    lens_ref, feat_ref, col_ref, row_ref, vec_ref, cot_ref, text_ref,
    side_sh, in_sh, out_sh, up_sh, down_sh,
    w_in, w_out, w_up, w_down, emb_t, ctx_t, first_t, act_t,
    dgelu_o, xh0_o, xh1_o, gp2_o, qkv_o, rows_o,
    col_o, lse_o, vec_o, bias1_o, bias2_o, last_o, slot_o, req_o, stat_o,
    side_f, in_f, out_f, up_f, down_f,
    outbox, inbox, text_send, text_recv, mask,
    low, wide_s, qkv, ctx_s, ctx, act, act_s, dgelu, emb_s, first_s, xh0, xh1, first, gp2, rows_s,
    own_sem, send_sem, recv_sem, twin_sem, small_send, small_recv, text_ssem, text_rsem,
    keep_sem, pair_send, pair_recv,
):
    rep, z, y, x = spot()
    me = at(z, y, x)
    mine = rep * 16 + me
    vocab = text_ref.shape[0]
    barrier = greet_all()

    side_a, in_a, out_a, up_a, down_a = arrays = [
        Gather(i, sh, full, own_sem, send_sem, recv_sem, twin_sem)
        for i, (sh, full) in enumerate(
            ((side_sh, side_f), (in_sh, in_f), (out_sh, out_f), (up_sh, up_f), (down_sh, down_f))
        )
    ]

    kept = []

    def keep(source, target):
        copy = pltpu.make_async_copy(source, target, keep_sem.at[len(kept)])
        kept.append(copy)
        copy.start()

    paired = []

    def pair(source, target):
        columns = target.at[:, rows_of(rep, BLOCK, LANES)]
        keep(source, columns)
        copy = pltpu.make_async_remote_copy(
            src_ref=source,
            dst_ref=columns,
            send_sem=pair_send.at[len(paired)],
            recv_sem=pair_recv.at[len(paired)],
            device_id=(1 - rep, me),
            device_id_type=MESH,
        )
        paired.append(copy)
        copy.start()

    valid = (members(lens_ref, (BLOCK, 1), 0) < SLOTS).astype(f32)
    count = jnp.sum(valid, axis=0, keepdims=True)
    col_o[:, 3:4] = valid

    def add_total(c, total):
        rows = rows_of(c, 64, 64)
        return total + jnp.sum(widen(feat_ref[rows, :]) * col_o[rows, 3:4], axis=0, keepdims=True)

    local = lax.fori_loop(0, 8, add_total, jnp.zeros((1, 768), f32)) / jnp.maximum(count, 1.0)

    def add_square(c, square):
        rows = rows_of(c, 64, 64)
        center = widen(feat_ref[rows, :]) - local
        return square + jnp.sum(center * center * col_o[rows, 3:4], axis=0, keepdims=True)

    square = lax.fori_loop(0, 8, add_square, jnp.zeros((1, 768), f32))

    ids_c, base_c, owner_c = col_ref[:, 0:1], col_ref[:, 6:7], col_ref[:, 7:8]
    ids_r, base_r, owner_r = row_ref[0:1, :], row_ref[6:7, :], row_ref[7:8, :]
    equal = jnp.where(ids_c == ids_r, 1.0, 0.0)
    earlier = iota((BLOCK, 1), 0) < iota((1, BLOCK), 1)
    later = iota((BLOCK, 1), 0) > iota((1, BLOCK), 1)
    first_r = 1.0 - jnp.max(jnp.where(earlier, equal, 0.0), axis=0, keepdims=True)
    first_c = 1.0 - jnp.max(jnp.where(later, equal, 0.0), axis=1, keepdims=True)
    rank_c = jnp.sum(
        jnp.where((ids_r < ids_c) & (ids_r >= base_c), first_r, 0.0), axis=1, keepdims=True
    )
    rank_r = jnp.sum(
        jnp.where((ids_c < ids_r) & (ids_c >= base_r), first_c, 0.0), axis=0, keepdims=True
    )
    most = jnp.max(rank_r, axis=1, keepdims=True) + 1.0
    col_o[:, 2:3] = jnp.where(rank_c < CAP, widen(owner_c) * CAP + rank_c, -1.0)
    slot_o[...] = jnp.broadcast_to(
        jnp.where(rank_r < CAP, widen(owner_r) * CAP + rank_r, -1.0), (8, BLOCK)
    )
    within = widen(ids_c - base_c)
    lane = iota((1, LANES), 1).astype(f32)
    for t in range(16):
        hit = (jnp.where(owner_c == t, rank_c, -1.0)) == lane
        outbox[t, 13:14, :] = jnp.max(jnp.where(hit, within, -1.0), axis=0, keepdims=True)
        for j in range(6):
            outbox[t, j : j + 1, :] = local[:, j * LANES : (j + 1) * LANES]
            outbox[t, 6 + j : 7 + j, :] = square[:, j * LANES : (j + 1) * LANES]
        outbox[t, 12:13, :] = jnp.where(lane == 1.0, most, count)
        outbox[t, 14:20, :] = vec_ref[...]
        outbox[t, 20:24, :] = jnp.zeros((4, LANES), f32)
    pl.semaphore_wait(barrier, 31)
    exchange_all(outbox, inbox, small_send, small_recv, True)
    for a in arrays:
        a.start()
    inbox[mine] = outbox[me]
    same = members(lens_ref, (BLOCK, 1), 0) == members(lens_ref, (1, BLOCK), 1)
    mask[...] = jnp.where(same, 0.0, -1e30)

    side_a.hop_one()
    exchange_all(outbox, inbox, small_send, small_recv, False)

    asked = jnp.concatenate([inbox[rep * 16 + t, 13:14, :] for t in range(16)], axis=0)
    asked = jnp.concatenate([asked, jnp.full((LANES - 16, LANES), -1.0, f32)], axis=0)
    asked = jnp.transpose(asked)
    column = iota((1, vocab), 1).astype(f32)
    for t in range(16):
        text_send[t * CAP : (t + 1) * CAP, :] = mm(
            onehot(asked[:CAP, t : t + 1] == column), text_ref[...]
        ).astype(bf16)

    def text_copy(t, source):
        return pltpu.make_async_remote_copy(
            src_ref=text_send.at[rows_of(t, CAP, 16)],
            dst_ref=text_recv.at[rows_of(source, CAP, 16)],
            send_sem=text_ssem.at[t],
            recv_sem=text_rsem.at[source],
            device_id=(rep, t),
            device_id_type=MESH,
        )

    def text_start(k, carry):
        text_copy(lax.rem(me + k, 16), me).start()
        return carry

    lax.fori_loop(1, 16, text_start, 0)
    text_recv[rows_of(me, CAP, 16), :] = text_send[rows_of(me, CAP, 16), :]
    req_o[...] = jnp.concatenate([inbox[t, 13:14, :] for t in range(32)], axis=0)

    def gathered(j):
        return jnp.concatenate([inbox[t, j : j + 1, :] for t in range(32)], axis=0)

    tail = gathered(12)
    counts = tail[:, 0:1]
    all_rows = jnp.sum(counts, axis=0, keepdims=True)
    means, spreads = [], []
    for j in range(6):
        part = gathered(j)
        mean = jnp.sum(part * counts, axis=0, keepdims=True) / all_rows
        shift = part - mean
        variance = (
            jnp.sum(gathered(6 + j) + counts * shift * shift, axis=0, keepdims=True) / all_rows
        )
        means.append(mean)
        spreads.append(lax.rsqrt(variance + epsilon))
    mean = jnp.concatenate(means, axis=1)
    spread = jnp.concatenate(spreads, axis=1)
    most = jnp.max(tail[:, 1:2], axis=0, keepdims=True)
    stat_o[...] = jnp.concatenate(
        [
            mean,
            spread,
            jnp.broadcast_to(all_rows, (1, 768)),
            jnp.broadcast_to(most, (1, 768)),
            jnp.zeros((4, 768), f32),
        ],
        axis=0,
    )
    packed = jnp.concatenate(
        [
            jnp.concatenate([inbox[t, 14 + j : 15 + j, :] for t in range(16)], axis=0)
            for j in range(6)
        ],
        axis=1,
    )
    narrow, middle, wide = expand_vectors(packed)
    vec_o[...] = jnp.concatenate([narrow, jnp.zeros((6, 768), f32)], axis=0)
    bias1_o[...] = jnp.broadcast_to(middle, (8, 1536))
    bias2_o[...] = jnp.broadcast_to(wide, (8, 3072))

    in_a.hop_one()
    side_a.hop_two()
    out_a.hop_one()
    side_a.last()

    def text_wait(k, carry):
        there = lax.rem(me + k, 16)
        text_copy(there, there).wait_recv()
        return carry

    lax.fori_loop(1, 16, text_wait, 0)
    side_a.ready()

    def embed(c, carry):
        rows = rows_of(c, 128, 128)
        hat = (widen(feat_ref[rows, :]) - stat_o[0:1, :]) * stat_o[1:2, :]
        begin = hat * vec_o[0:1, :] + vec_o[1:2, :]
        slots = iota((1, 16 * CAP), 1).astype(f32)
        begin = begin + mm(onehot(col_o[rows, 2:3] == slots), text_recv[...])
        where = col_ref[rows, :]
        bins = iota((1, BINS), 1)
        hits = (where[:, 1:2] == bins).astype(f32) + (where[:, 2:3] == bins).astype(f32)
        begin = begin + mm(hits.astype(bf16), side_f[0:BINS, :])
        hits = (where[:, 3:4] == bins).astype(f32) + (where[:, 4:5] == bins).astype(f32)
        begin = begin + mm(hits.astype(bf16), side_f[BINS : 2 * BINS, :])
        segments = iota((1, SIDE - 2 * BINS), 1)
        begin = begin + mm(onehot(where[:, 5:6] == segments), side_f[2 * BINS :, :])
        center = begin - jnp.mean(begin, axis=-1, keepdims=True)
        scale = spread_rows(center)
        hat = center * scale
        xh0[rows, :] = hat
        col_o[rows, 0:1] = scale
        value = hat * vec_o[2:3, :] + vec_o[3:4, :]
        wide_s[rows, :] = value
        low[rows, :] = value.astype(bf16)
        return carry

    lax.fori_loop(0, 4, embed, 0)
    keep(xh0, xh0_o)
    in_a.hop_two()
    up_a.hop_one()
    transpose_to(emb_s, low)
    pair(emb_s, emb_t)
    in_a.last()
    in_a.ready()
    keep(in_f, w_in)

    def project(i, carry):
        columns = rows_of(i, 256, 256)
        qkv[:, columns] = mm(low[...], in_f[:, columns]).astype(bf16)
        return carry

    def project_biased(i, carry):
        columns = rows_of(i, 256, 256)
        source = rows_of(lax.rem(i, 6), 256, 256)
        qkv[:, columns] = (mm(low[...], in_f[:, columns]) + bias1_o[0:1, source]).astype(bf16)
        return carry

    lax.fori_loop(0, 3, project_biased, 0)
    lax.fori_loop(3, 6, project, 0)

    def project_values(i, carry):
        columns = rows_of(i + 6, 256, 256)
        source = rows_of(i + 3, 256, 256)
        qkv[:, columns] = (mm(low[...], in_f[:, columns]) + bias1_o[0:1, source]).astype(bf16)
        return carry

    lax.fori_loop(0, 3, project_values, 0)
    keep(qkv, qkv_o)
    out_a.hop_two()
    out_a.last()

    def attend(p, carry):
        query = qkv[:, rows_of(p, LANES, LANES)]
        keys = qkv[:, rows_of(p + 6, LANES, LANES)]
        values = jnp.transpose(qkv[:, rows_of(p + 12, LANES, LANES)])
        for head in range(2):
            low_lanes = iota((1, LANES), 1) // HEAD == head
            masked = query * jnp.where(low_lanes, 0.125, 0.0).astype(bf16)
            for part in range(2):
                scores = mm_nt(keys, masked[part * 256 : part * 256 + 256, :])
                scores = scores + mask[:, part * 256 : part * 256 + 256]
                top = jnp.max(scores, axis=0, keepdims=True)
                expo = jnp.exp(scores - top)
                total = jnp.sum(expo, axis=0, keepdims=True)
                got = mm(values[head * HEAD : (head + 1) * HEAD, :], expo.astype(bf16))
                ctx_s[
                    pl.ds(pl.multiple_of(p * LANES + head * HEAD, HEAD), HEAD),
                    part * 256 : part * 256 + 256,
                ] = (got * (1.0 / total)).astype(bf16)
                lse_o[pl.ds(2 * p + head, 1), part * 256 : part * 256 + 256] = top + jnp.log(total)
        ctx[:, rows_of(p, LANES, LANES)] = jnp.transpose(ctx_s[rows_of(p, LANES, LANES), :])
        return carry

    lax.fori_loop(0, 3, attend, 0)
    down_a.hop_one()
    lax.fori_loop(3, 6, attend, 0)
    lse_o[12:16, :] = jnp.zeros((4, BLOCK), f32)
    pair(ctx_s, ctx_t)
    up_a.hop_two()
    out_a.ready()
    keep(out_f, w_out)

    def attention_norm(c, carry):
        rows = rows_of(c, 128, 128)
        value = wide_s[rows, :] + mm(ctx[rows, :], out_f[...]) + vec_o[4:5, :]
        center = value - jnp.mean(value, axis=-1, keepdims=True)
        scale = spread_rows(center)
        hat = center * scale
        xh1[rows, :] = hat
        col_o[rows, 1:2] = scale
        value = hat * vec_o[5:6, :] + vec_o[6:7, :]
        first[rows, :] = value
        low[rows, :] = value.astype(bf16)
        return carry

    lax.fori_loop(0, 4, attention_norm, 0)
    keep(xh1, xh1_o)
    transpose_to(first_s, low)
    pair(first_s, first_t)
    up_a.last()
    up_a.ready()
    keep(up_f, w_up)

    def feed(i, carry):
        columns = rows_of(i, 256, 256)
        hidden = mm(low[...], up_f[:, columns]) + bias2_o[0:1, columns]
        part = 0.5 + 0.5 * lax.erf(hidden * (1.0 / math.sqrt(2.0)))
        value = (hidden * part).astype(bf16)
        act[:, columns] = value
        act_s[columns, :] = jnp.transpose(value)
        bell = jnp.exp(hidden * hidden * -0.5) * (1.0 / math.sqrt(2.0 * math.pi))
        dgelu[:, columns] = (part + hidden * bell).astype(bf16)
        return carry

    lax.fori_loop(0, 12, feed, 0)
    keep(dgelu, dgelu_o)
    pair(act_s, act_t)
    down_a.hop_two()
    down_a.last()
    down_a.ready()
    keep(down_f, w_down)

    def second_part(i, carry):
        columns = rows_of(i, 256, 256)
        wide_s[:, columns] = mm(act[...], down_f[:, columns]) + vec_o[7:8, columns]
        return carry

    lax.fori_loop(0, 3, second_part, 0)

    def last_norm(c, carry):
        rows = rows_of(c, 128, 128)
        value = first[rows, :] + wide_s[rows, :]
        center = value - jnp.mean(value, axis=-1, keepdims=True)
        scale = spread_rows(center)
        hat = center * scale
        rows_s[rows, :] = (hat * vec_o[8:9, :] + vec_o[9:10, :]).astype(bf16)
        grad = widen(cot_ref[rows, :]) * col_o[rows, 3:4]
        gained = grad * vec_o[8:9, :]
        gp2[rows, :] = scale * (
            gained
            - jnp.mean(gained, axis=-1, keepdims=True)
            - hat * jnp.mean(gained * hat, axis=-1, keepdims=True)
        )
        gain, bias = carry
        return (
            gain + jnp.sum(grad * hat, axis=0, keepdims=True),
            bias + jnp.sum(grad, axis=0, keepdims=True),
        )

    zero = jnp.zeros((1, 768), f32)
    gain, bias = lax.fori_loop(0, 4, last_norm, (zero, zero))
    last_o[...] = jnp.concatenate([gain, bias, jnp.zeros((6, 768), f32)], axis=0)
    keep(gp2, gp2_o)
    keep(rows_s, rows_o)

    for a in arrays:
        a.drain()

    def text_drain(k, carry):
        text_copy(lax.rem(me + k, 16), me).wait_send()
        return carry

    lax.fori_loop(1, 16, text_drain, 0)
    for copy in paired:
        copy.wait_send()
        copy.wait_recv()
    for copy in kept:
        copy.wait()


def shape(*dims, dtype=f32):
    return jax.ShapeDtypeStruct(dims, dtype)


def forward_call(lens, feat, col, row, vec, cot, text, side, w_in, w_out, w_up, w_down):
    vm, hbm = pl.BlockSpec(memory_space=pltpu.VMEM), pl.BlockSpec(memory_space=pl.ANY)
    sm = pl.BlockSpec(memory_space=pltpu.SMEM)
    full = [(16 * w.shape[0], w.shape[1]) for w in (side, w_in, w_out, w_up, w_down)]
    out_shape = (
        *(shape(*dims, dtype=bf16) for dims in full[1:]),
        shape(768, 1024, dtype=bf16), shape(768, 1024, dtype=bf16), shape(768, 1024, dtype=bf16),
        shape(3072, 1024, dtype=bf16),
        shape(BLOCK, 3072, dtype=bf16),
        shape(BLOCK, 768), shape(BLOCK, 768), shape(BLOCK, 768),
        shape(BLOCK, 2304, dtype=bf16), shape(BLOCK, 768, dtype=bf16),
        shape(BLOCK, LANES), shape(16, BLOCK), shape(16, 768), shape(8, 1536), shape(8, 3072),
        shape(8, 768), shape(8, BLOCK), shape(32, LANES), shape(8, 768),
    )
    v = lambda *dims, dtype=bf16: pltpu.VMEM(dims, dtype)
    dma = pltpu.SemaphoreType.DMA
    return pl.pallas_call(
        forward_kernel,
        name="forward",
        out_shape=out_shape,
        in_specs=[sm] + [vm] * 6 + [hbm] * 5,
        out_specs=tuple([hbm] * 14 + [vm] * 9),
        scratch_shapes=[
            *(v(*dims) for dims in full),
            v(16, 24, LANES, dtype=f32), v(32, 24, LANES, dtype=f32),
            v(16 * CAP, 768), v(16 * CAP, 768), v(BLOCK, BLOCK, dtype=f32),
            v(BLOCK, 768), v(BLOCK, 768, dtype=f32), v(BLOCK, 2304), v(768, BLOCK), v(BLOCK, 768),
            v(BLOCK, 3072), v(3072, BLOCK), v(BLOCK, 3072), v(768, BLOCK), v(768, BLOCK),
            v(BLOCK, 768, dtype=f32), v(BLOCK, 768, dtype=f32), v(BLOCK, 768, dtype=f32),
            v(BLOCK, 768, dtype=f32), v(BLOCK, 768),
            dma((5,)), dma((5, 32)), dma((5, 16)), dma((5, 16)), dma((32,)), dma((32,)),
            dma((16,)), dma((16,)), dma((14,)), dma((4,)), dma((4,)),
        ],
        compiler_params=pltpu.CompilerParams(
            collective_id=0, has_side_effects=True, vmem_limit_bytes=60 * 2**20
        ),
    )(lens, feat, col, row, vec, cot, text, side, w_in, w_out, w_up, w_down)


def pack_indices(text_ids, boxes, segment_ids, vocab):
    owner = text_ids // vocab
    return jnp.stack(
        [
            text_ids, boxes[:, 0], boxes[:, 2], boxes[:, 1], boxes[:, 3], segment_ids,
            owner * vocab, owner,
        ],
        axis=1,
    )


def norm_rows(value, gain, shift):
    center = value - jnp.mean(value, axis=-1, keepdims=True)
    spread = lax.rsqrt(jnp.mean(center * center, axis=-1, keepdims=True) + epsilon)
    return center * spread * gain + shift


def gelu_exact(value):
    return jax.nn.gelu(value, approximate=False)


def block_scores(query, keys, member):
    query_heads = query.reshape(BLOCK, -1, HEAD)
    key_heads = keys.reshape(BLOCK, -1, HEAD)
    scores = (
        jnp.einsum("qhd,khd->hqk", query_heads, key_heads, preferred_element_type=jnp.float32)
        * 0.125
    )
    same = member[:, None] == member[None, :]
    return jnp.where(same[None], scores, -1e30)


def attend_forward(operands):
    query, keys, values, member = operands
    scores = block_scores(query, keys, member)
    top = jnp.max(scores, axis=-1, keepdims=True)
    expo = jnp.exp(scores - top)
    total = jnp.sum(expo, axis=-1, keepdims=True)
    probs_low = (expo / total).astype(jnp.bfloat16)
    context = jnp.einsum(
        "hqk,khd->qhd",
        probs_low,
        values.reshape(BLOCK, -1, HEAD),
        preferred_element_type=jnp.float32,
    )
    return (context.reshape(BLOCK, -1).astype(jnp.bfloat16), top + jnp.log(total))


def attend_backward(operands):
    query, keys, values, member, logsum, grad_context = operands
    scores = block_scores(query, keys, member)
    probs = jnp.exp(scores - logsum)
    probs_low = probs.astype(jnp.bfloat16)
    value_heads = values.reshape(BLOCK, -1, HEAD)
    grad_heads = grad_context.reshape(BLOCK, -1, HEAD)
    grad_values = jnp.einsum(
        "hqk,qhd->khd", probs_low, grad_heads, preferred_element_type=jnp.float32
    )
    grad_probs = jnp.einsum(
        "qhd,khd->hqk", grad_heads, value_heads, preferred_element_type=jnp.float32
    )
    delta = jnp.sum(grad_probs * probs, axis=-1, keepdims=True)
    grad_scores = (probs * (grad_probs - delta)).astype(jnp.bfloat16)
    grad_query = (
        jnp.einsum(
            "hqk,khd->qhd",
            grad_scores,
            keys.reshape(BLOCK, -1, HEAD),
            preferred_element_type=jnp.float32,
        )
        * 0.125
    )
    grad_keys = (
        jnp.einsum(
            "hqk,qhd->khd",
            grad_scores,
            query.reshape(BLOCK, -1, HEAD),
            preferred_element_type=jnp.float32,
        )
        * 0.125
    )
    joined = jnp.concatenate(
        [
            grad_query.reshape(BLOCK, -1),
            grad_keys.reshape(BLOCK, -1),
            grad_values.reshape(BLOCK, -1),
        ],
        axis=1,
    )
    return joined.astype(jnp.bfloat16)


def general(
    region_features,
    text_ids,
    boxes,
    segment_ids,
    document_lengths,
    cotangent,
    batch_gain,
    batch_bias,
    text_table,
    side_table,
    embed_gain,
    embed_bias,
    in_weight,
    in_bias,
    out_weight,
    out_bias,
    first_gain,
    first_bias,
    up_weight,
    up_bias,
    down_weight,
    down_bias,
    second_gain,
    second_bias,
):
    rows_here, width = region_features.shape
    blocks_here = document_lengths.shape[0]
    vocab_here = text_table.shape[0]
    ends = jnp.cumsum(document_lengths, axis=1)
    place = jnp.arange(BLOCK, dtype=jnp.int32)
    member = jnp.sum((place[None, :, None] >= ends[:, None, :]).astype(jnp.int32), axis=2)
    valid = (member < SLOTS).astype(jnp.float32).reshape(rows_here, 1)
    gathered = (
        lax.all_gather(batch_gain, "shard", axis=0, tiled=True),
        lax.all_gather(batch_bias, "shard", axis=0, tiled=True),
        lax.all_gather(side_table, "shard", axis=0, tiled=True),
        lax.all_gather(embed_gain, "shard", axis=0, tiled=True),
        lax.all_gather(embed_bias, "shard", axis=0, tiled=True),
        lax.all_gather(in_weight, "shard", axis=0, tiled=True),
        lax.all_gather(in_bias, "shard", axis=0, tiled=True),
        lax.all_gather(out_weight, "shard", axis=0, tiled=True),
        lax.all_gather(out_bias, "shard", axis=0, tiled=True),
        lax.all_gather(first_gain, "shard", axis=0, tiled=True),
        lax.all_gather(first_bias, "shard", axis=0, tiled=True),
        lax.all_gather(up_weight, "shard", axis=0, tiled=True),
        lax.all_gather(up_bias, "shard", axis=0, tiled=True),
        lax.all_gather(down_weight, "shard", axis=0, tiled=True),
        lax.all_gather(down_bias, "shard", axis=0, tiled=True),
        lax.all_gather(second_gain, "shard", axis=0, tiled=True),
        lax.all_gather(second_bias, "shard", axis=0, tiled=True),
    )
    (
        full_batch_gain,
        full_batch_bias,
        full_side,
        full_embed_gain,
        full_embed_bias,
        full_in_weight,
        full_in_bias,
        full_out_weight,
        full_out_bias,
        full_first_gain,
        full_first_bias,
        full_up_weight,
        full_up_bias,
        full_down_weight,
        full_down_bias,
        full_second_gain,
        full_second_bias,
    ) = gathered
    features = widen(region_features)
    masked = features * valid
    total, count = lax.psum((jnp.sum(masked, axis=0), jnp.sum(valid)), ("rep", "shard"))
    mean = total / count
    center = features - mean
    variance = lax.psum(jnp.sum(center * center * valid, axis=0), ("rep", "shard")) / count
    spread = lax.rsqrt(variance + epsilon)
    batch_hat = center * spread
    gain_wide = widen(full_batch_gain)
    batch_out = batch_hat * gain_wide + widen(full_batch_bias)
    piece = lax.all_gather(text_table, "shard", axis=0, tiled=True)
    add_column = jnp.arange(piece.shape[0], dtype=jnp.int32)
    onehot = (text_ids[:, None] == add_column[None, :]).astype(jnp.bfloat16)
    text_rows = jnp.dot(onehot, piece, preferred_element_type=jnp.float32)
    side_column = jnp.arange(SIDE, dtype=jnp.int32)
    hits = jnp.zeros((rows_here, SIDE), jnp.float32)
    for column in (
        boxes[:, 0],
        boxes[:, 2],
        boxes[:, 1] + BINS,
        boxes[:, 3] + BINS,
        segment_ids + 2 * BINS,
    ):
        hits = hits + (column[:, None] == side_column[None, :]).astype(jnp.float32)
    hits_low = hits.astype(jnp.bfloat16)
    looked = text_rows + jnp.dot(hits_low, full_side, preferred_element_type=jnp.float32)
    start_rows = batch_out + looked
    embedded, back_embed = jax.vjp(
        norm_rows, start_rows, widen(full_embed_gain), widen(full_embed_bias)
    )
    embedded_low = embedded.astype(jnp.bfloat16)
    mixed = jnp.dot(embedded_low, full_in_weight, preferred_element_type=jnp.float32)
    bias_wide = widen(full_in_bias)
    query = (mixed[:, :width] + bias_wide[:width]).astype(jnp.bfloat16)
    keys = mixed[:, width : 2 * width].astype(jnp.bfloat16)
    values = (mixed[:, 2 * width :] + bias_wide[width:]).astype(jnp.bfloat16)
    shaped = (
        query.reshape(blocks_here, BLOCK, width),
        keys.reshape(blocks_here, BLOCK, width),
        values.reshape(blocks_here, BLOCK, width),
    )
    context, logsum = lax.map(attend_forward, shaped + (member,))
    context = context.reshape(rows_here, width)
    branch = jnp.dot(context, full_out_weight, preferred_element_type=jnp.float32) + widen(
        full_out_bias
    )
    first, back_first = jax.vjp(
        norm_rows, embedded + branch, widen(full_first_gain), widen(full_first_bias)
    )
    first_low = first.astype(jnp.bfloat16)
    hidden = jnp.dot(first_low, full_up_weight, preferred_element_type=jnp.float32) + widen(
        full_up_bias
    )
    gelu_value, gelu_back = jax.vjp(gelu_exact, hidden)
    active = gelu_value.astype(jnp.bfloat16)
    second = jnp.dot(active, full_down_weight, preferred_element_type=jnp.float32) + widen(
        full_down_bias
    )
    final, back_second = jax.vjp(
        norm_rows, first + second, widen(full_second_gain), widen(full_second_bias)
    )
    out_rows = final.astype(jnp.bfloat16)
    grad_final = widen(cotangent) * valid
    grad_pre2, grad_second_gain, grad_second_bias = back_second(grad_final)
    grad_second = grad_pre2.astype(jnp.bfloat16)
    grad_down_weight = jnp.einsum(
        "rf,rd->fd", active, grad_second, preferred_element_type=jnp.float32
    )
    grad_down_bias = jnp.sum(widen(grad_second), axis=0)
    grad_active = jnp.einsum(
        "rd,fd->rf", grad_second, full_down_weight, preferred_element_type=jnp.float32
    )
    grad_hidden = gelu_back(grad_active)[0].astype(jnp.bfloat16)
    grad_up_weight = jnp.einsum(
        "rd,rf->df", first_low, grad_hidden, preferred_element_type=jnp.float32
    )
    grad_up_bias = jnp.sum(widen(grad_hidden), axis=0)
    grad_first = grad_pre2 + jnp.einsum(
        "rf,df->rd", grad_hidden, full_up_weight, preferred_element_type=jnp.float32
    )
    grad_pre1, grad_first_gain, grad_first_bias = back_first(grad_first)
    grad_branch = grad_pre1.astype(jnp.bfloat16)
    grad_out_weight = jnp.einsum(
        "rd,re->de", context, grad_branch, preferred_element_type=jnp.float32
    )
    grad_out_bias = jnp.sum(widen(grad_branch), axis=0)
    grad_context = jnp.einsum(
        "re,de->rd", grad_branch, full_out_weight, preferred_element_type=jnp.float32
    ).astype(jnp.bfloat16)
    grad_mixed = lax.map(
        attend_backward, shaped + (member, logsum, grad_context.reshape(blocks_here, BLOCK, width))
    )
    grad_mixed = grad_mixed.reshape(rows_here, 3 * width)
    grad_in_weight = jnp.einsum(
        "rd,re->de", embedded_low, grad_mixed, preferred_element_type=jnp.float32
    )
    column_sums = jnp.sum(widen(grad_mixed), axis=0)
    grad_in_bias = jnp.concatenate([column_sums[:width], column_sums[2 * width :]])
    grad_embedded = grad_pre1 + jnp.einsum(
        "re,de->rd", grad_mixed, full_in_weight, preferred_element_type=jnp.float32
    )
    grad_start, grad_embed_gain, grad_embed_bias = back_embed(grad_embedded)
    grad_looked = grad_start.astype(jnp.bfloat16)
    column = jnp.arange(lax.axis_size("shard") * vocab_here, dtype=jnp.int32)
    onehot = (column[:, None] == text_ids[None, :]).astype(jnp.bfloat16)
    text_grad = lax.psum_scatter(
        jnp.dot(onehot, grad_looked, preferred_element_type=jnp.float32),
        "shard",
        scatter_dimension=0,
        tiled=True,
    )
    grad_side = jnp.einsum("rs,rd->sd", hits_low, grad_looked, preferred_element_type=jnp.float32)
    shift_sum, scale_sum = lax.psum(
        (jnp.sum(grad_start * valid, axis=0), jnp.sum(grad_start * batch_hat * valid, axis=0)),
        ("rep", "shard"),
    )
    feature_grad = (
        valid
        * gain_wide
        * spread
        * (grad_start - shift_sum / count - batch_hat * scale_sum / count)
    ).astype(jnp.bfloat16)
    owned = (
        lax.psum_scatter(grad_side, "shard", scatter_dimension=0, tiled=True),
        lax.psum_scatter(grad_embed_gain, "shard", scatter_dimension=0, tiled=True),
        lax.psum_scatter(grad_embed_bias, "shard", scatter_dimension=0, tiled=True),
        lax.psum_scatter(grad_in_weight, "shard", scatter_dimension=0, tiled=True),
        lax.psum_scatter(grad_in_bias, "shard", scatter_dimension=0, tiled=True),
        lax.psum_scatter(grad_out_weight, "shard", scatter_dimension=0, tiled=True),
        lax.psum_scatter(grad_out_bias, "shard", scatter_dimension=0, tiled=True),
        lax.psum_scatter(grad_first_gain, "shard", scatter_dimension=0, tiled=True),
        lax.psum_scatter(grad_first_bias, "shard", scatter_dimension=0, tiled=True),
        lax.psum_scatter(grad_up_weight, "shard", scatter_dimension=0, tiled=True),
        lax.psum_scatter(grad_up_bias, "shard", scatter_dimension=0, tiled=True),
        lax.psum_scatter(grad_down_weight, "shard", scatter_dimension=0, tiled=True),
        lax.psum_scatter(grad_down_bias, "shard", scatter_dimension=0, tiled=True),
        lax.psum_scatter(grad_second_gain, "shard", scatter_dimension=0, tiled=True),
        lax.psum_scatter(grad_second_bias, "shard", scatter_dimension=0, tiled=True),
    )
    (
        own_side,
        own_embed_gain,
        own_embed_bias,
        own_in_weight,
        own_in_bias,
        own_out_weight,
        own_out_bias,
        own_first_gain,
        own_first_bias,
        own_up_weight,
        own_up_bias,
        own_down_weight,
        own_down_bias,
        own_second_gain,
        own_second_bias,
    ) = owned
    summed = (
        lax.psum(own_side.astype(jnp.bfloat16), "rep").astype(jnp.float32),
        lax.psum(own_embed_gain.astype(jnp.bfloat16), "rep").astype(jnp.float32),
        lax.psum(own_embed_bias.astype(jnp.bfloat16), "rep").astype(jnp.float32),
        lax.psum(own_in_weight.astype(jnp.bfloat16), "rep").astype(jnp.float32),
        lax.psum(own_in_bias.astype(jnp.bfloat16), "rep").astype(jnp.float32),
        lax.psum(own_out_weight.astype(jnp.bfloat16), "rep").astype(jnp.float32),
        lax.psum(own_out_bias.astype(jnp.bfloat16), "rep").astype(jnp.float32),
        lax.psum(own_first_gain.astype(jnp.bfloat16), "rep").astype(jnp.float32),
        lax.psum(own_first_bias.astype(jnp.bfloat16), "rep").astype(jnp.float32),
        lax.psum(own_up_weight.astype(jnp.bfloat16), "rep").astype(jnp.float32),
        lax.psum(own_up_bias.astype(jnp.bfloat16), "rep").astype(jnp.float32),
        lax.psum(own_down_weight.astype(jnp.bfloat16), "rep").astype(jnp.float32),
        lax.psum(own_down_bias.astype(jnp.bfloat16), "rep").astype(jnp.float32),
        lax.psum(own_second_gain.astype(jnp.bfloat16), "rep").astype(jnp.float32),
        lax.psum(own_second_bias.astype(jnp.bfloat16), "rep").astype(jnp.float32),
        lax.psum(text_grad.astype(jnp.bfloat16), "rep").astype(jnp.float32),
    )
    (
        side_grad,
        embed_gain_grad,
        embed_bias_grad,
        in_weight_grad,
        in_bias_grad,
        out_weight_grad,
        out_bias_grad,
        first_gain_grad,
        first_bias_grad,
        up_weight_grad,
        up_bias_grad,
        down_weight_grad,
        down_bias_grad,
        second_gain_grad,
        second_bias_grad,
        text_table_grad,
    ) = summed
    portion = width // lax.axis_size("shard")
    offset = lax.axis_index("shard") * portion
    batch_gain_grad = lax.dynamic_slice_in_dim(scale_sum, offset, portion)
    batch_bias_grad = lax.dynamic_slice_in_dim(shift_sum, offset, portion)
    return (
        out_rows,
        feature_grad,
        batch_gain_grad,
        batch_bias_grad,
        text_table_grad,
        side_grad,
        embed_gain_grad,
        embed_bias_grad,
        in_weight_grad,
        in_bias_grad,
        out_weight_grad,
        out_bias_grad,
        first_gain_grad,
        first_bias_grad,
        up_weight_grad,
        up_bias_grad,
        down_weight_grad,
        down_bias_grad,
        second_gain_grad,
        second_bias_grad,
    )


def fast(*args):
    (
        region_features, text_ids, boxes, segment_ids, document_lengths, cotangent,
        batch_gain, batch_bias, text_table, side_table, embed_gain, embed_bias,
        in_weight, in_bias, out_weight, out_bias, first_gain, first_bias,
        up_weight, up_bias, down_weight, down_bias, second_gain, second_bias,
    ) = args
    vocab = text_table.shape[0]
    col = pack_indices(text_ids, boxes, segment_ids, vocab)
    vec = widen(
        jnp.concatenate(
            [
                batch_gain, batch_bias, embed_gain, embed_bias, out_bias, first_gain, first_bias,
                down_bias, second_gain, second_bias, in_bias, up_bias,
            ]
        )
    ).reshape(6, LANES)
    made = forward_call(
        document_lengths, region_features, col, col.T, vec, cotangent, text_table,
        side_table, in_weight, out_weight, up_weight, down_weight,
    )
    return lax.cond(made[-1][3, 0] > CAP, lambda: general(*args), lambda: backward(args, col, made))


def backward(args, col, made):
    (
        w_in, w_out, w_up, w_down, emb_t, ctx_t, first_t, act_t, dgelu, xh0, xh1, gp2, qkv, out_rows,
        cols, lse, vec, bias1, bias2, last, slot, req, stat,
    ) = made
    region_features, text_ids = args[0], args[1]
    document_lengths = args[4]
    rep = lax.axis_index("rep")
    mine = lambda a: lax.dynamic_slice_in_dim(a, rep * BLOCK, BLOCK, axis=1)
    ends = jnp.cumsum(document_lengths, axis=1)
    place = jnp.arange(BLOCK, dtype=jnp.int32)
    member = jnp.sum((place[None, :, None] >= ends[:, None, :]).astype(jnp.int32), axis=2)
    valid = cols[:, 3:4]
    mean, spread, count = stat[0], stat[1], stat[2, 0]
    batch_hat = (widen(region_features) - mean) * spread

    def norm_back(grad, hat, scale, gain):
        gained = grad * gain
        dx = scale * (
            gained
            - jnp.mean(gained, -1, keepdims=True)
            - hat * jnp.mean(gained * hat, -1, keepdims=True)
        )
        return dx, jnp.sum(grad * hat, 0), jnp.sum(grad, 0)

    gs = gp2.astype(bf16)
    g_down = mm(mine(act_t), gs).astype(bf16)
    gh = (widen(dgelu) * mm_nt(gs, w_down)).astype(bf16)
    g_up = mm(mine(first_t), gh).astype(bf16)
    gp1, dg1, db1 = norm_back(gp2 + mm_nt(gh, w_up), xh1, cols[:, 1:2], vec[5])
    gb = gp1.astype(bf16)
    g_out = mm(mine(ctx_t), gb).astype(bf16)
    gctx = mm_nt(gb, w_out).astype(bf16)
    gm = attend_backward(
        (qkv[:, :768], qkv[:, 768:1536], qkv[:, 1536:], member[0], lse[:12, :, None], gctx)
    )
    g_in = mm(mine(emb_t), gm).astype(bf16)
    gstart, dg0, db0 = norm_back(gp1 + mm_nt(gm, w_in), xh0, cols[:, 0:1], vec[2])
    gl = gstart.astype(bf16)
    side_column = jnp.arange(SIDE, dtype=jnp.int32)
    hits = jnp.zeros((BLOCK, SIDE), jnp.float32)
    for column in (col[:, 1], col[:, 2], col[:, 3] + BINS, col[:, 4] + BINS, col[:, 5] + 2 * BINS):
        hits = hits + (column[:, None] == side_column[None, :]).astype(jnp.float32)
    g_side = lax.dot_general(
        hits.astype(bf16), gl, (((0,), (0,)), ((), ())), preferred_element_type=f32
    ).astype(bf16)
    ids = jnp.arange(16 * args[8].shape[0], dtype=jnp.int32)
    g_text = mm((ids[:, None] == text_ids[None, :]).astype(bf16), gl).astype(bf16)
    shift_sum, scale_sum = lax.psum(
        (jnp.sum(gstart * valid, axis=0), jnp.sum(gstart * batch_hat * valid, axis=0)),
        ("rep", "shard"),
    )
    feature_grad = (
        valid * vec[0] * spread * (gstart - shift_sum / count - batch_hat * scale_sum / count)
    ).astype(bf16)
    sums = jnp.sum(widen(gm), axis=0)
    vectors = [
        dg0, db0, jnp.concatenate([sums[:768], sums[1536:]]), jnp.sum(widen(gb), 0), dg1, db1,
        jnp.sum(widen(gh), 0), jnp.sum(widen(gs), 0), last[0], last[1],
    ]
    spread_out = lambda a: lax.psum(
        lax.psum_scatter(a, "shard", scatter_dimension=0, tiled=True), "rep"
    ).astype(f32)
    joined = jnp.concatenate([v.reshape(16, -1) for v in vectors], axis=1).reshape(-1)
    pieces = spread_out(joined)
    out, low = [], 0
    for v in vectors:
        size = v.shape[0] // 16
        out.append(pieces[low : low + size])
        low += size
    portion = 768 // 16
    offset = lax.axis_index("shard") * portion
    own = lambda a: lax.dynamic_slice_in_dim(a, offset, portion)
    return (
        out_rows, feature_grad, own(scale_sum), own(shift_sum), spread_out(g_text),
        spread_out(g_side), out[0], out[1], spread_out(g_in), out[2], spread_out(g_out), out[3],
        out[4], out[5], spread_out(g_up), out[6], spread_out(g_down), out[7], out[8], out[9],
    )


def fits(mesh):
    return dict(mesh.shape) == {"rep": 2, "shard": 16}


def solution(mesh):
    in_specs = (
        P(("rep", "shard"), None),
        P(("rep", "shard")),
        P(("rep", "shard"), None),
        P(("rep", "shard")),
        P(("rep", "shard"), None),
        P(("rep", "shard"), None),
        P("shard"),
        P("shard"),
        P("shard", None),
        P("shard", None),
        P("shard"),
        P("shard"),
        P("shard", None),
        P("shard"),
        P("shard", None),
        P("shard"),
        P("shard"),
        P("shard"),
        P("shard", None),
        P("shard"),
        P("shard", None),
        P("shard"),
        P("shard"),
        P("shard"),
    )
    out_specs = (
        P(("rep", "shard"), None),
        P(("rep", "shard"), None),
        P("shard"),
        P("shard"),
        P("shard", None),
        P("shard", None),
        P("shard"),
        P("shard"),
        P("shard", None),
        P("shard"),
        P("shard", None),
        P("shard"),
        P("shard"),
        P("shard"),
        P("shard", None),
        P("shard"),
        P("shard", None),
        P("shard"),
        P("shard"),
        P("shard"),
    )
    return jax.shard_map(
        fast if fits(mesh) else general, mesh=mesh, in_specs=in_specs, out_specs=out_specs, check_vma=False
    )
```

```python
import functools
import math

import jax
import jax.numpy as jnp
from jax import lax
from jax.experimental import pallas as pl
from jax.experimental.pallas import tpu as pltpu
from jax.sharding import PartitionSpec as P

HEAD = 64
BINS = 1024
SIDE = 2560
BLOCK = 512
SLOTS = 4
CAP = 48
LANES = 128
MESH = pl.DeviceIdType.MESH
f32 = jnp.float32
bf16 = jnp.bfloat16

epsilon = 1e-05


def widen(value):
    return value.astype(jnp.float32)


def mm(a, b):
    return jnp.dot(a, b, preferred_element_type=f32)


def mm_nt(a, b):
    return lax.dot_general(a, b, (((1,), (1,)), ((), ())), preferred_element_type=f32)


def iota(shape, dim):
    return lax.broadcasted_iota(jnp.int32, shape, dim)


def spot():
    shard = lax.axis_index("shard")
    return lax.axis_index("rep"), shard // 4, (shard // 2) % 2, shard % 2


def at(z, y, x):
    return z * 4 + y * 2 + x


def rows_of(start, size, step):
    return pl.ds(pl.multiple_of(start * size, step), size)


class Gather:
    def __init__(self, index, shard_ref, full_ref, own_sem, send_sem, recv_sem, twin_sem):
        self.index, self.shard, self.full = index, shard_ref, full_ref
        self.own_sem, self.send_sem, self.recv_sem, self.twin_sem = own_sem, send_sem, recv_sem, twin_sem
        self.rep, self.z, self.y, self.x = spot()
        self.me = at(self.z, self.y, self.x)
        self.rows = shard_ref.shape[0]
        self.half = shard_ref.shape[1] // 2

    def block(self, source, half):
        return self.full.at[
            rows_of(source, self.rows, 16), rows_of(half, self.half, LANES)
        ]

    def copy(self, source, slot, target, src=None, twin=False):
        return pltpu.make_async_remote_copy(
            src_ref=self.block(source, self.rep) if src is None else src,
            dst_ref=self.block(source, self.rep),
            send_sem=self.send_sem.at[self.index, slot],
            recv_sem=(self.twin_sem if twin else self.recv_sem).at[self.index, source],
            device_id=target,
            device_id_type=MESH,
        )

    def own(self):
        return pltpu.make_async_copy(
            self.shard, self.full.at[rows_of(self.me, self.rows, 16)], self.own_sem.at[self.index]
        )

    def start(self):
        src = self.shard.at[:, rows_of(self.rep, self.half, LANES)]

        def step(k, carry):
            there = lax.rem(self.z + k, 4)
            self.copy(self.me, there, (self.rep, at(there, self.y, self.x)), src=src).start()
            return carry

        lax.fori_loop(1, 4, step, 0)
        self.copy(self.me, 4 + self.z, self.beside(self.z, 0), src=src).start()
        self.copy(self.me, 8 + self.z, self.beside(self.z, 1), src=src).start()
        self.own().start()

    def to_twin(self, source):
        self.copy(source, 16 + source, (1 - self.rep, self.me), twin=True).start()

    def beside(self, plane, swap):
        even = lax.rem(plane + self.y + self.x + swap, 2) == 0
        return (
            self.rep,
            at(self.z, jnp.where(even, self.y, 1 - self.y), jnp.where(even, 1 - self.x, self.x)),
        )

    def hop_one(self):
        def step(k, carry):
            plane = lax.rem(self.z + k, 4)
            source = at(plane, self.y, self.x)
            self.copy(source, 0, (self.rep, self.me)).wait_recv()
            self.copy(source, 4 + plane, self.beside(plane, 0)).start()
            self.copy(source, 8 + plane, self.beside(plane, 1)).start()
            self.to_twin(source)
            return carry

        lax.fori_loop(1, 4, step, 0)

    def hop_two(self):
        def step(k, carry):
            plane = lax.rem(self.z + k, 4)
            even = lax.rem(plane + self.y + self.x, 2) == 0
            source = at(
                plane, jnp.where(even, 1 - self.y, self.y), jnp.where(even, self.x, 1 - self.x)
            )
            self.copy(source, 0, (self.rep, self.me)).wait_recv()
            self.copy(source, 12 + plane, self.beside(plane, 0)).start()
            self.to_twin(source)
            return carry

        lax.fori_loop(0, 4, step, 0)

    def last(self):
        def step(k, carry):
            plane = lax.rem(self.z + k, 4)
            even = lax.rem(plane + self.y + self.x, 2) == 0
            near = at(
                plane, jnp.where(even, self.y, 1 - self.y), jnp.where(even, 1 - self.x, self.x)
            )
            far = at(plane, 1 - self.y, 1 - self.x)
            for source in (near, far):
                self.copy(source, 0, (self.rep, self.me)).wait_recv()
                self.to_twin(source)
            return carry

        lax.fori_loop(0, 4, step, 0)

    def ready(self):
        self.own().wait()

        def step(k, carry):
            source = lax.rem(self.me + k, 16)
            pltpu.make_async_remote_copy(
                src_ref=self.block(source, 1 - self.rep),
                dst_ref=self.block(source, 1 - self.rep),
                send_sem=self.send_sem.at[self.index, 0],
                recv_sem=self.twin_sem.at[self.index, source],
                device_id=(self.rep, self.me),
                device_id_type=MESH,
            ).wait_recv()
            return carry

        lax.fori_loop(1, 16, step, 0)

    def drain(self):
        def step(k, carry):
            @pl.when((k != self.z) & (k != 16 + self.me))
            def _():
                self.copy(self.me, k, (self.rep, self.me)).wait_send()

            return carry

        lax.fori_loop(0, 32, step, 0)


def exchange_all(outbox, inbox, send_sem, recv_sem, start):
    rep, shard = lax.axis_index("rep"), lax.axis_index("shard")
    mine = rep * 16 + shard

    def copy(k):
        there = lax.rem(mine + k, 32)
        return there, pltpu.make_async_remote_copy(
            src_ref=outbox.at[lax.rem(there, 16)],
            dst_ref=inbox.at[mine],
            send_sem=send_sem.at[k],
            recv_sem=recv_sem.at[mine],
            device_id=(there // 16, lax.rem(there, 16)),
            device_id_type=MESH,
        )

    if start:

        def step(k, carry):
            copy(k)[1].start()
            return carry

        lax.fori_loop(1, 32, step, 0)
        return

    def done(k, carry):
        there, sent = copy(k)
        sent.wait_send()
        pltpu.make_async_remote_copy(
            src_ref=outbox.at[0],
            dst_ref=inbox.at[there],
            send_sem=send_sem.at[k],
            recv_sem=recv_sem.at[there],
            device_id=(rep, shard),
            device_id_type=MESH,
        ).wait_recv()
        return carry

    lax.fori_loop(1, 32, done, 0)


def greet_all():
    barrier = pltpu.get_barrier_semaphore()
    mine = lax.axis_index("rep") * 16 + lax.axis_index("shard")

    def step(k, carry):
        there = lax.rem(mine + k, 32)
        pl.semaphore_signal(
            barrier, inc=1, device_id=(there // 16, lax.rem(there, 16)), device_id_type=MESH
        )
        return carry

    lax.fori_loop(1, 32, step, 0)
    return barrier


def members(lens_ref, shape, dim):
    place = iota(shape, dim)
    end = jnp.int32(0)
    member = jnp.zeros(shape, jnp.int32)
    for slot in range(SLOTS):
        end = end + lens_ref[0, slot]
        member = member + (place >= end).astype(jnp.int32)
    return member


def spread_rows(value):
    return lax.rsqrt(jnp.mean(value * value, axis=-1, keepdims=True) + epsilon)


def onehot(condition):
    return jnp.where(condition, 1.0, 0.0).astype(bf16)


def remainder(shape, dim, offset, size):
    place = iota(shape, dim).astype(f32) - offset
    group = jnp.floor((place + 0.5) * (1.0 / size))
    return group, place - group * size


def expand_vectors(packed):
    def select(low, width, offset, size):
        _, want = remainder((1, size * 16), 1, 0, size)
        depth = iota((width, 1), 0).astype(f32) + (low - offset)
        return onehot(depth == want)

    kinds, _ = remainder((1, 768), 1, 0, 48)
    stacked = jnp.concatenate(
        [jnp.where(kinds == k, packed, 0.0) for k in range(10)], axis=0
    ).astype(bf16)
    _, depth = remainder((768, 1), 0, 0, 48)
    _, want = remainder((1, 768), 1, 0, 48)
    spread = mm(stacked, onehot(depth == want))
    owner, _ = remainder((1, 768), 1, 0, 48)
    shard_of = iota((16, 1), 0).astype(f32)
    narrow = jnp.concatenate(
        [
            jnp.sum(jnp.where(owner == shard_of, spread[k * 16 : k * 16 + 16], 0.0), axis=0, keepdims=True)
            for k in range(10)
        ],
        axis=0,
    )
    low = packed.astype(bf16)
    owner, _ = remainder((1, 1536), 1, 0, 96)
    middle = mm(low[:, 384:640], select(384, 256, 480, 96))
    middle = jnp.sum(jnp.where(owner == shard_of, middle, 0.0), axis=0, keepdims=True)
    owner, _ = remainder((1, 3072), 1, 0, 192)
    wide = mm(low[:, 512:768], select(512, 256, 576, 192))
    wide = jnp.sum(jnp.where(owner == shard_of, wide, 0.0), axis=0, keepdims=True)
    return narrow, middle, wide


def transpose_to(target, source):
    for j in range(source.shape[1] // LANES):
        target[j * LANES : (j + 1) * LANES, :] = jnp.transpose(
            source[:, j * LANES : (j + 1) * LANES]
        )


def forward_kernel(
    lens_ref, feat_ref, col_ref, row_ref, vec_ref, cot_ref, text_ref,
    side_sh, in_sh, out_sh, up_sh, down_sh,
    w_in, w_out, w_up, w_down, emb_t, ctx_t, first_t, act_t,
    dgelu_o, xh0_o, xh1_o, gp2_o, qkv_o, rows_o,
    col_o, lse_o, vec_o, bias1_o, bias2_o, last_o, slot_o, req_o, stat_o,
    side_f, in_f, out_f, up_f, down_f,
    outbox, inbox, text_send, text_recv, mask,
    low, wide_s, qkv, ctx_s, ctx, act, act_s, dgelu, emb_s, first_s, xh0, xh1, first, gp2, rows_s,
    own_sem, send_sem, recv_sem, twin_sem, small_send, small_recv, text_ssem, text_rsem,
    keep_sem, pair_send, pair_recv,
):
    rep, z, y, x = spot()
    me = at(z, y, x)
    mine = rep * 16 + me
    vocab = text_ref.shape[0]
    barrier = greet_all()

    side_a, in_a, out_a, up_a, down_a = arrays = [
        Gather(i, sh, full, own_sem, send_sem, recv_sem, twin_sem)
        for i, (sh, full) in enumerate(
            ((side_sh, side_f), (in_sh, in_f), (out_sh, out_f), (up_sh, up_f), (down_sh, down_f))
        )
    ]

    kept = []

    def keep(source, target):
        copy = pltpu.make_async_copy(source, target, keep_sem.at[len(kept)])
        kept.append(copy)
        copy.start()

    paired = []

    def pair(source, target):
        columns = target.at[:, rows_of(rep, BLOCK, LANES)]
        keep(source, columns)
        copy = pltpu.make_async_remote_copy(
            src_ref=source,
            dst_ref=columns,
            send_sem=pair_send.at[len(paired)],
            recv_sem=pair_recv.at[len(paired)],
            device_id=(1 - rep, me),
            device_id_type=MESH,
        )
        paired.append(copy)
        copy.start()

    valid = (members(lens_ref, (BLOCK, 1), 0) < SLOTS).astype(f32)
    count = jnp.sum(valid, axis=0, keepdims=True)
    col_o[:, 3:4] = valid

    def add_total(c, total):
        rows = rows_of(c, 64, 64)
        return total + jnp.sum(widen(feat_ref[rows, :]) * col_o[rows, 3:4], axis=0, keepdims=True)

    local = lax.fori_loop(0, 8, add_total, jnp.zeros((1, 768), f32)) / jnp.maximum(count, 1.0)

    def add_square(c, square):
        rows = rows_of(c, 64, 64)
        center = widen(feat_ref[rows, :]) - local
        return square + jnp.sum(center * center * col_o[rows, 3:4], axis=0, keepdims=True)

    square = lax.fori_loop(0, 8, add_square, jnp.zeros((1, 768), f32))

    ids_c, base_c, owner_c = col_ref[:, 0:1], col_ref[:, 6:7], col_ref[:, 7:8]
    ids_r, base_r, owner_r = row_ref[0:1, :], row_ref[6:7, :], row_ref[7:8, :]
    equal = jnp.where(ids_c == ids_r, 1.0, 0.0)
    earlier = iota((BLOCK, 1), 0) < iota((1, BLOCK), 1)
    later = iota((BLOCK, 1), 0) > iota((1, BLOCK), 1)
    first_r = 1.0 - jnp.max(jnp.where(earlier, equal, 0.0), axis=0, keepdims=True)
    first_c = 1.0 - jnp.max(jnp.where(later, equal, 0.0), axis=1, keepdims=True)
    rank_c = jnp.sum(
        jnp.where((ids_r < ids_c) & (ids_r >= base_c), first_r, 0.0), axis=1, keepdims=True
    )
    rank_r = jnp.sum(
        jnp.where((ids_c < ids_r) & (ids_c >= base_r), first_c, 0.0), axis=0, keepdims=True
    )
    most = jnp.max(rank_r, axis=1, keepdims=True) + 1.0
    col_o[:, 2:3] = jnp.where(rank_c < CAP, widen(owner_c) * CAP + rank_c, -1.0)
    slot_o[...] = jnp.broadcast_to(
        jnp.where(rank_r < CAP, widen(owner_r) * CAP + rank_r, -1.0), (8, BLOCK)
    )
    pieces = jnp.concatenate(
        [vec_ref[k : k + 1, 0:48] for k in range(10)]
        + [vec_ref[10:11, 0:96], vec_ref[11:12, 0:192]],
        axis=1,
    )
    within = widen(ids_c - base_c)
    lane = iota((1, LANES), 1).astype(f32)
    for t in range(16):
        hit = (jnp.where(owner_c == t, rank_c, -1.0)) == lane
        outbox[t, 13:14, :] = jnp.max(jnp.where(hit, within, -1.0), axis=0, keepdims=True)
        for j in range(6):
            outbox[t, j : j + 1, :] = local[:, j * LANES : (j + 1) * LANES]
            outbox[t, 6 + j : 7 + j, :] = square[:, j * LANES : (j + 1) * LANES]
        outbox[t, 12:13, :] = jnp.where(lane == 1.0, most, count)
        for j in range(6):
            outbox[t, 14 + j : 15 + j, :] = pieces[:, j * LANES : (j + 1) * LANES]
        outbox[t, 20:24, :] = jnp.zeros((4, LANES), f32)
    pl.semaphore_wait(barrier, 31)
    side_a.start()
    exchange_all(outbox, inbox, small_send, small_recv, True)
    in_a.start()
    out_a.start()
    inbox[mine] = outbox[me]
    same = members(lens_ref, (BLOCK, 1), 0) == members(lens_ref, (1, BLOCK), 1)
    mask[...] = jnp.where(same, 0.0, -1e30)

    side_a.hop_one()
    exchange_all(outbox, inbox, small_send, small_recv, False)

    asked = jnp.concatenate([inbox[rep * 16 + t, 13:14, :] for t in range(16)], axis=0)
    asked = jnp.concatenate([asked, jnp.full((LANES - 16, LANES), -1.0, f32)], axis=0)
    asked = jnp.transpose(asked)
    column = iota((1, vocab), 1).astype(f32)
    for t in range(16):
        text_send[t * CAP : (t + 1) * CAP, :] = mm(
            onehot(asked[:CAP, t : t + 1] == column), text_ref[...]
        ).astype(bf16)

    def text_copy(t, source):
        return pltpu.make_async_remote_copy(
            src_ref=text_send.at[rows_of(t, CAP, 16)],
            dst_ref=text_recv.at[rows_of(source, CAP, 16)],
            send_sem=text_ssem.at[t],
            recv_sem=text_rsem.at[source],
            device_id=(rep, t),
            device_id_type=MESH,
        )

    def text_start(k, carry):
        text_copy(lax.rem(me + k, 16), me).start()
        return carry

    lax.fori_loop(1, 16, text_start, 0)
    up_a.start()
    down_a.start()
    text_recv[rows_of(me, CAP, 16), :] = text_send[rows_of(me, CAP, 16), :]
    req_o[...] = jnp.concatenate([inbox[t, 13:14, :] for t in range(32)], axis=0)

    def gathered(j):
        return jnp.concatenate([inbox[t, j : j + 1, :] for t in range(32)], axis=0)

    tail = gathered(12)
    counts = tail[:, 0:1]
    all_rows = jnp.sum(counts, axis=0, keepdims=True)
    means, spreads = [], []
    for j in range(6):
        part = gathered(j)
        mean = jnp.sum(part * counts, axis=0, keepdims=True) / all_rows
        shift = part - mean
        variance = (
            jnp.sum(gathered(6 + j) + counts * shift * shift, axis=0, keepdims=True) / all_rows
        )
        means.append(mean)
        spreads.append(lax.rsqrt(variance + epsilon))
    mean = jnp.concatenate(means, axis=1)
    spread = jnp.concatenate(spreads, axis=1)
    most = jnp.max(tail[:, 1:2], axis=0, keepdims=True)
    stat_o[...] = jnp.concatenate(
        [
            mean,
            spread,
            jnp.broadcast_to(all_rows, (1, 768)),
            jnp.broadcast_to(most, (1, 768)),
            jnp.zeros((4, 768), f32),
        ],
        axis=0,
    )
    packed = jnp.concatenate(
        [
            jnp.concatenate([inbox[t, 14 + j : 15 + j, :] for t in range(16)], axis=0)
            for j in range(6)
        ],
        axis=1,
    )
    narrow, middle, wide = expand_vectors(packed)
    vec_o[...] = jnp.concatenate([narrow, jnp.zeros((6, 768), f32)], axis=0)
    bias1_o[...] = jnp.broadcast_to(middle, (8, 1536))
    bias2_o[...] = jnp.broadcast_to(wide, (8, 3072))


    in_a.hop_one()
    side_a.hop_two()
    out_a.hop_one()
    side_a.last()
    in_a.hop_two()
    in_a.last()
    out_a.hop_two()
    out_a.last()
    def text_wait(k, carry):
        there = lax.rem(me + k, 16)
        text_copy(there, there).wait_recv()
        return carry

    lax.fori_loop(1, 16, text_wait, 0)

    side_a.ready()
    def embed(c, carry):
        rows = rows_of(c, 128, 128)
        hat = (widen(feat_ref[rows, :]) - stat_o[0:1, :]) * stat_o[1:2, :]
        begin = hat * vec_o[0:1, :] + vec_o[1:2, :]
        slots = iota((1, 16 * CAP), 1).astype(f32)
        begin = begin + mm(onehot(col_o[rows, 2:3] == slots), text_recv[...])
        where = col_ref[rows, :]
        bins = iota((1, BINS), 1)
        hits = (where[:, 1:2] == bins).astype(f32) + (where[:, 2:3] == bins).astype(f32)
        begin = begin + mm(hits.astype(bf16), side_f[0:BINS, :])
        hits = (where[:, 3:4] == bins).astype(f32) + (where[:, 4:5] == bins).astype(f32)
        begin = begin + mm(hits.astype(bf16), side_f[BINS : 2 * BINS, :])
        segments = iota((1, SIDE - 2 * BINS), 1)
        begin = begin + mm(onehot(where[:, 5:6] == segments), side_f[2 * BINS :, :])
        center = begin - jnp.mean(begin, axis=-1, keepdims=True)
        scale = spread_rows(center)
        hat = center * scale
        xh0[rows, :] = hat
        col_o[rows, 0:1] = scale
        value = hat * vec_o[2:3, :] + vec_o[3:4, :]
        wide_s[rows, :] = value
        low[rows, :] = value.astype(bf16)
        return carry

    lax.fori_loop(0, 4, embed, 0)
    keep(xh0, xh0_o)
    transpose_to(emb_s, low)
    pair(emb_s, emb_t)
    up_a.hop_one()
    in_a.ready()
    keep(in_f, w_in)

    def project(i, carry):
        columns = rows_of(i, 256, 256)
        qkv[:, columns] = mm(low[...], in_f[:, columns]).astype(bf16)
        return carry

    def project_biased(i, carry):
        columns = rows_of(i, 256, 256)
        source = rows_of(lax.rem(i, 6), 256, 256)
        qkv[:, columns] = (mm(low[...], in_f[:, columns]) + bias1_o[0:1, source]).astype(bf16)
        return carry

    lax.fori_loop(0, 3, project_biased, 0)
    lax.fori_loop(3, 6, project, 0)

    def project_values(i, carry):
        columns = rows_of(i + 6, 256, 256)
        source = rows_of(i + 3, 256, 256)
        qkv[:, columns] = (mm(low[...], in_f[:, columns]) + bias1_o[0:1, source]).astype(bf16)
        return carry

    lax.fori_loop(0, 3, project_values, 0)
    keep(qkv, qkv_o)

    def attend(p, carry):
        query = qkv[:, rows_of(p, LANES, LANES)]
        keys = qkv[:, rows_of(p + 6, LANES, LANES)]
        values = jnp.transpose(qkv[:, rows_of(p + 12, LANES, LANES)])
        for head in range(2):
            low_lanes = iota((1, LANES), 1) // HEAD == head
            masked = query * jnp.where(low_lanes, 0.125, 0.0).astype(bf16)
            for part in range(2):
                scores = mm_nt(keys, masked[part * 256 : part * 256 + 256, :])
                scores = scores + mask[:, part * 256 : part * 256 + 256]
                top = jnp.max(scores, axis=0, keepdims=True)
                expo = jnp.exp(scores - top)
                total = jnp.sum(expo, axis=0, keepdims=True)
                got = mm(values[head * HEAD : (head + 1) * HEAD, :], expo.astype(bf16))
                ctx_s[
                    pl.ds(pl.multiple_of(p * LANES + head * HEAD, HEAD), HEAD),
                    part * 256 : part * 256 + 256,
                ] = (got * (1.0 / total)).astype(bf16)
                lse_o[pl.ds(2 * p + head, 1), part * 256 : part * 256 + 256] = top + jnp.log(total)
        ctx[:, rows_of(p, LANES, LANES)] = jnp.transpose(ctx_s[rows_of(p, LANES, LANES), :])
        return carry

    lax.fori_loop(0, 3, attend, 0)
    up_a.hop_two()
    down_a.hop_one()
    lax.fori_loop(3, 6, attend, 0)
    lse_o[12:16, :] = jnp.zeros((4, BLOCK), f32)
    pair(ctx_s, ctx_t)
    up_a.last()
    out_a.ready()
    keep(out_f, w_out)

    def attention_norm(c, carry):
        rows = rows_of(c, 128, 128)
        value = wide_s[rows, :] + mm(ctx[rows, :], out_f[...]) + vec_o[4:5, :]
        center = value - jnp.mean(value, axis=-1, keepdims=True)
        scale = spread_rows(center)
        hat = center * scale
        xh1[rows, :] = hat
        col_o[rows, 1:2] = scale
        value = hat * vec_o[5:6, :] + vec_o[6:7, :]
        first[rows, :] = value
        low[rows, :] = value.astype(bf16)
        return carry

    lax.fori_loop(0, 4, attention_norm, 0)
    keep(xh1, xh1_o)
    transpose_to(first_s, low)
    pair(first_s, first_t)
    down_a.hop_two()
    up_a.ready()
    keep(up_f, w_up)

    def feed(i, carry):
        columns = rows_of(i, 256, 256)
        hidden = mm(low[...], up_f[:, columns]) + bias2_o[0:1, columns]
        part = 0.5 + 0.5 * lax.erf(hidden * (1.0 / math.sqrt(2.0)))
        value = (hidden * part).astype(bf16)
        act[:, columns] = value
        act_s[columns, :] = jnp.transpose(value)
        bell = jnp.exp(hidden * hidden * -0.5) * (1.0 / math.sqrt(2.0 * math.pi))
        dgelu[:, columns] = (part + hidden * bell).astype(bf16)
        return carry

    lax.fori_loop(0, 12, feed, 0)
    keep(dgelu, dgelu_o)
    pair(act_s, act_t)
    down_a.last()
    down_a.ready()
    keep(down_f, w_down)

    def second_part(i, carry):
        columns = rows_of(i, 256, 256)
        wide_s[:, columns] = mm(act[...], down_f[:, columns]) + vec_o[7:8, columns]
        return carry

    lax.fori_loop(0, 3, second_part, 0)

    def last_norm(c, carry):
        rows = rows_of(c, 128, 128)
        value = first[rows, :] + wide_s[rows, :]
        center = value - jnp.mean(value, axis=-1, keepdims=True)
        scale = spread_rows(center)
        hat = center * scale
        rows_s[rows, :] = (hat * vec_o[8:9, :] + vec_o[9:10, :]).astype(bf16)
        grad = widen(cot_ref[rows, :]) * col_o[rows, 3:4]
        gained = grad * vec_o[8:9, :]
        gp2[rows, :] = scale * (
            gained
            - jnp.mean(gained, axis=-1, keepdims=True)
            - hat * jnp.mean(gained * hat, axis=-1, keepdims=True)
        )
        gain, bias = carry
        return (
            gain + jnp.sum(grad * hat, axis=0, keepdims=True),
            bias + jnp.sum(grad, axis=0, keepdims=True),
        )

    zero = jnp.zeros((1, 768), f32)
    gain, bias = lax.fori_loop(0, 4, last_norm, (zero, zero))
    last_o[...] = jnp.concatenate([gain, bias, jnp.zeros((6, 768), f32)], axis=0)
    keep(gp2, gp2_o)
    keep(rows_s, rows_o)

    for a in arrays:
        a.drain()

    def text_drain(k, carry):
        text_copy(lax.rem(me + k, 16), me).wait_send()
        return carry

    lax.fori_loop(1, 16, text_drain, 0)
    for copy in paired:
        copy.wait_send()
        copy.wait_recv()
    for copy in kept:
        copy.wait()


def shape(*dims, dtype=f32):
    return jax.ShapeDtypeStruct(dims, dtype)


def forward_call(lens, feat, col, row, vec, cot, text, side, w_in, w_out, w_up, w_down):
    vm, hbm = pl.BlockSpec(memory_space=pltpu.VMEM), pl.BlockSpec(memory_space=pl.ANY)
    sm = pl.BlockSpec(memory_space=pltpu.SMEM)
    full = [(16 * w.shape[0], w.shape[1]) for w in (side, w_in, w_out, w_up, w_down)]
    out_shape = (
        *(shape(*dims, dtype=bf16) for dims in full[1:]),
        shape(768, 1024, dtype=bf16), shape(768, 1024, dtype=bf16), shape(768, 1024, dtype=bf16),
        shape(3072, 1024, dtype=bf16),
        shape(BLOCK, 3072, dtype=bf16),
        shape(BLOCK, 768), shape(BLOCK, 768), shape(BLOCK, 768),
        shape(BLOCK, 2304, dtype=bf16), shape(BLOCK, 768, dtype=bf16),
        shape(BLOCK, LANES), shape(16, BLOCK), shape(16, 768), shape(8, 1536), shape(8, 3072),
        shape(8, 768), shape(8, BLOCK), shape(32, LANES), shape(8, 768),
    )
    v = lambda *dims, dtype=bf16: pltpu.VMEM(dims, dtype)
    dma = pltpu.SemaphoreType.DMA
    return pl.pallas_call(
        forward_kernel,
        name="forward",
        out_shape=out_shape,
        in_specs=[sm] + [vm] * 6 + [hbm] * 5,
        out_specs=tuple([hbm] * 14 + [vm] * 9),
        scratch_shapes=[
            *(v(*dims) for dims in full),
            v(16, 24, LANES, dtype=f32), v(32, 24, LANES, dtype=f32),
            v(16 * CAP, 768), v(16 * CAP, 768), v(BLOCK, BLOCK, dtype=f32),
            v(BLOCK, 768), v(BLOCK, 768, dtype=f32), v(BLOCK, 2304), v(768, BLOCK), v(BLOCK, 768),
            v(BLOCK, 3072), v(3072, BLOCK), v(BLOCK, 3072), v(768, BLOCK), v(768, BLOCK),
            v(BLOCK, 768, dtype=f32), v(BLOCK, 768, dtype=f32), v(BLOCK, 768, dtype=f32),
            v(BLOCK, 768, dtype=f32), v(BLOCK, 768),
            dma((5,)), dma((5, 32)), dma((5, 16)), dma((5, 16)), dma((32,)), dma((32,)),
            dma((16,)), dma((16,)), dma((14,)), dma((4,)), dma((4,)),
        ],
        compiler_params=pltpu.CompilerParams(
            collective_id=0, has_side_effects=True, vmem_limit_bytes=60 * 2**20
        ),
    )(lens, feat, col, row, vec, cot, text, side, w_in, w_out, w_up, w_down)


def pack_indices(text_ids, boxes, segment_ids, vocab):
    owner = text_ids // vocab
    return jnp.stack(
        [
            text_ids, boxes[:, 0], boxes[:, 2], boxes[:, 1], boxes[:, 3], segment_ids,
            owner * vocab, owner,
        ],
        axis=1,
    )


def norm_rows(value, gain, shift):
    center = value - jnp.mean(value, axis=-1, keepdims=True)
    spread = lax.rsqrt(jnp.mean(center * center, axis=-1, keepdims=True) + epsilon)
    return center * spread * gain + shift


def gelu_exact(value):
    return jax.nn.gelu(value, approximate=False)


def block_scores(query, keys, member):
    query_heads = query.reshape(BLOCK, -1, HEAD)
    key_heads = keys.reshape(BLOCK, -1, HEAD)
    scores = (
        jnp.einsum("qhd,khd->hqk", query_heads, key_heads, preferred_element_type=jnp.float32)
        * 0.125
    )
    same = member[:, None] == member[None, :]
    return jnp.where(same[None], scores, -1e30)


def attend_forward(operands):
    query, keys, values, member = operands
    scores = block_scores(query, keys, member)
    top = jnp.max(scores, axis=-1, keepdims=True)
    expo = jnp.exp(scores - top)
    total = jnp.sum(expo, axis=-1, keepdims=True)
    probs_low = (expo / total).astype(jnp.bfloat16)
    context = jnp.einsum(
        "hqk,khd->qhd",
        probs_low,
        values.reshape(BLOCK, -1, HEAD),
        preferred_element_type=jnp.float32,
    )
    return (context.reshape(BLOCK, -1).astype(jnp.bfloat16), top + jnp.log(total))


def attend_backward(operands):
    query, keys, values, member, logsum, grad_context = operands
    scores = block_scores(query, keys, member)
    probs = jnp.exp(scores - logsum)
    probs_low = probs.astype(jnp.bfloat16)
    value_heads = values.reshape(BLOCK, -1, HEAD)
    grad_heads = grad_context.reshape(BLOCK, -1, HEAD)
    grad_values = jnp.einsum(
        "hqk,qhd->khd", probs_low, grad_heads, preferred_element_type=jnp.float32
    )
    grad_probs = jnp.einsum(
        "qhd,khd->hqk", grad_heads, value_heads, preferred_element_type=jnp.float32
    )
    delta = jnp.sum(grad_probs * probs, axis=-1, keepdims=True)
    grad_scores = (probs * (grad_probs - delta)).astype(jnp.bfloat16)
    grad_query = (
        jnp.einsum(
            "hqk,khd->qhd",
            grad_scores,
            keys.reshape(BLOCK, -1, HEAD),
            preferred_element_type=jnp.float32,
        )
        * 0.125
    )
    grad_keys = (
        jnp.einsum(
            "hqk,qhd->khd",
            grad_scores,
            query.reshape(BLOCK, -1, HEAD),
            preferred_element_type=jnp.float32,
        )
        * 0.125
    )
    joined = jnp.concatenate(
        [
            grad_query.reshape(BLOCK, -1),
            grad_keys.reshape(BLOCK, -1),
            grad_values.reshape(BLOCK, -1),
        ],
        axis=1,
    )
    return joined.astype(jnp.bfloat16)


def general(
    region_features,
    text_ids,
    boxes,
    segment_ids,
    document_lengths,
    cotangent,
    batch_gain,
    batch_bias,
    text_table,
    side_table,
    embed_gain,
    embed_bias,
    in_weight,
    in_bias,
    out_weight,
    out_bias,
    first_gain,
    first_bias,
    up_weight,
    up_bias,
    down_weight,
    down_bias,
    second_gain,
    second_bias,
):
    rows_here, width = region_features.shape
    blocks_here = document_lengths.shape[0]
    vocab_here = text_table.shape[0]
    ends = jnp.cumsum(document_lengths, axis=1)
    place = jnp.arange(BLOCK, dtype=jnp.int32)
    member = jnp.sum((place[None, :, None] >= ends[:, None, :]).astype(jnp.int32), axis=2)
    valid = (member < SLOTS).astype(jnp.float32).reshape(rows_here, 1)
    shards = lax.axis_size("shard")
    vectors = (
        batch_gain, batch_bias, embed_gain, embed_bias, in_bias, out_bias, first_gain, first_bias,
        up_bias, down_bias, second_gain, second_bias,
    )
    sizes = [v.shape[0] for v in vectors]
    marks = [sum(sizes[:k]) for k in range(len(sizes) + 1)]
    joined = lax.all_gather(jnp.concatenate(vectors), "shard", axis=0)
    (
        full_batch_gain,
        full_batch_bias,
        full_embed_gain,
        full_embed_bias,
        full_in_bias,
        full_out_bias,
        full_first_gain,
        full_first_bias,
        full_up_bias,
        full_down_bias,
        full_second_gain,
        full_second_bias,
    ) = [joined[:, low:high].reshape(-1) for low, high in zip(marks, marks[1:])]
    full_side, full_in_weight, full_out_weight, full_up_weight, full_down_weight = [
        lax.all_gather(w, "shard", axis=0, tiled=True)
        for w in (side_table, in_weight, out_weight, up_weight, down_weight)
    ]
    features = widen(region_features)
    masked = features * valid
    total, count = lax.psum((jnp.sum(masked, axis=0), jnp.sum(valid)), ("rep", "shard"))
    mean = total / count
    center = features - mean
    variance = lax.psum(jnp.sum(center * center * valid, axis=0), ("rep", "shard")) / count
    spread = lax.rsqrt(variance + epsilon)
    batch_hat = center * spread
    gain_wide = widen(full_batch_gain)
    batch_out = batch_hat * gain_wide + widen(full_batch_bias)
    piece = lax.all_gather(text_table, "shard", axis=0, tiled=True)
    add_column = jnp.arange(piece.shape[0], dtype=jnp.int32)
    onehot = (text_ids[:, None] == add_column[None, :]).astype(jnp.bfloat16)
    text_rows = jnp.dot(onehot, piece, preferred_element_type=jnp.float32)
    side_column = jnp.arange(SIDE, dtype=jnp.int32)
    hits = jnp.zeros((rows_here, SIDE), jnp.float32)
    for column in (
        boxes[:, 0],
        boxes[:, 2],
        boxes[:, 1] + BINS,
        boxes[:, 3] + BINS,
        segment_ids + 2 * BINS,
    ):
        hits = hits + (column[:, None] == side_column[None, :]).astype(jnp.float32)
    hits_low = hits.astype(jnp.bfloat16)
    looked = text_rows + jnp.dot(hits_low, full_side, preferred_element_type=jnp.float32)
    start_rows = batch_out + looked
    embedded, back_embed = jax.vjp(
        norm_rows, start_rows, widen(full_embed_gain), widen(full_embed_bias)
    )
    embedded_low = embedded.astype(jnp.bfloat16)
    mixed = jnp.dot(embedded_low, full_in_weight, preferred_element_type=jnp.float32)
    bias_wide = widen(full_in_bias)
    query = (mixed[:, :width] + bias_wide[:width]).astype(jnp.bfloat16)
    keys = mixed[:, width : 2 * width].astype(jnp.bfloat16)
    values = (mixed[:, 2 * width :] + bias_wide[width:]).astype(jnp.bfloat16)
    shaped = (
        query.reshape(blocks_here, BLOCK, width),
        keys.reshape(blocks_here, BLOCK, width),
        values.reshape(blocks_here, BLOCK, width),
    )
    context, logsum = lax.map(attend_forward, shaped + (member,))
    context = context.reshape(rows_here, width)
    branch = jnp.dot(context, full_out_weight, preferred_element_type=jnp.float32) + widen(
        full_out_bias
    )
    first, back_first = jax.vjp(
        norm_rows, embedded + branch, widen(full_first_gain), widen(full_first_bias)
    )
    first_low = first.astype(jnp.bfloat16)
    hidden = jnp.dot(first_low, full_up_weight, preferred_element_type=jnp.float32) + widen(
        full_up_bias
    )
    gelu_value, gelu_back = jax.vjp(gelu_exact, hidden)
    active = gelu_value.astype(jnp.bfloat16)
    second = jnp.dot(active, full_down_weight, preferred_element_type=jnp.float32) + widen(
        full_down_bias
    )
    final, back_second = jax.vjp(
        norm_rows, first + second, widen(full_second_gain), widen(full_second_bias)
    )
    out_rows = final.astype(jnp.bfloat16)
    grad_final = widen(cotangent) * valid
    grad_pre2, grad_second_gain, grad_second_bias = back_second(grad_final)
    grad_second = grad_pre2.astype(jnp.bfloat16)
    grad_down_weight = jnp.einsum(
        "rf,rd->fd", active, grad_second, preferred_element_type=jnp.float32
    )
    grad_down_bias = jnp.sum(widen(grad_second), axis=0)
    grad_active = jnp.einsum(
        "rd,fd->rf", grad_second, full_down_weight, preferred_element_type=jnp.float32
    )
    grad_hidden = gelu_back(grad_active)[0].astype(jnp.bfloat16)
    grad_up_weight = jnp.einsum(
        "rd,rf->df", first_low, grad_hidden, preferred_element_type=jnp.float32
    )
    grad_up_bias = jnp.sum(widen(grad_hidden), axis=0)
    grad_first = grad_pre2 + jnp.einsum(
        "rf,df->rd", grad_hidden, full_up_weight, preferred_element_type=jnp.float32
    )
    grad_pre1, grad_first_gain, grad_first_bias = back_first(grad_first)
    grad_branch = grad_pre1.astype(jnp.bfloat16)
    grad_out_weight = jnp.einsum(
        "rd,re->de", context, grad_branch, preferred_element_type=jnp.float32
    )
    grad_out_bias = jnp.sum(widen(grad_branch), axis=0)
    grad_context = jnp.einsum(
        "re,de->rd", grad_branch, full_out_weight, preferred_element_type=jnp.float32
    ).astype(jnp.bfloat16)
    grad_mixed = lax.map(
        attend_backward, shaped + (member, logsum, grad_context.reshape(blocks_here, BLOCK, width))
    )
    grad_mixed = grad_mixed.reshape(rows_here, 3 * width)
    grad_in_weight = jnp.einsum(
        "rd,re->de", embedded_low, grad_mixed, preferred_element_type=jnp.float32
    )
    column_sums = jnp.sum(widen(grad_mixed), axis=0)
    grad_in_bias = jnp.concatenate([column_sums[:width], column_sums[2 * width :]])
    grad_embedded = grad_pre1 + jnp.einsum(
        "re,de->rd", grad_mixed, full_in_weight, preferred_element_type=jnp.float32
    )
    grad_start, grad_embed_gain, grad_embed_bias = back_embed(grad_embedded)
    grad_looked = grad_start.astype(jnp.bfloat16)
    column = jnp.arange(lax.axis_size("shard") * vocab_here, dtype=jnp.int32)
    onehot = (column[:, None] == text_ids[None, :]).astype(jnp.bfloat16)
    text_grad = lax.psum_scatter(
        jnp.dot(onehot, grad_looked, preferred_element_type=jnp.float32),
        "shard",
        scatter_dimension=0,
        tiled=True,
    )
    grad_side = jnp.einsum("rs,rd->sd", hits_low, grad_looked, preferred_element_type=jnp.float32)
    shift_sum, scale_sum = lax.psum(
        (jnp.sum(grad_start * valid, axis=0), jnp.sum(grad_start * batch_hat * valid, axis=0)),
        ("rep", "shard"),
    )
    feature_grad = (
        valid
        * gain_wide
        * spread
        * (grad_start - shift_sum / count - batch_hat * scale_sum / count)
    ).astype(jnp.bfloat16)
    small = (
        scale_sum / lax.axis_size(("rep", "shard")),
        shift_sum / lax.axis_size(("rep", "shard")),
        grad_embed_gain, grad_embed_bias, grad_in_bias, grad_out_bias, grad_first_gain,
        grad_first_bias, grad_up_bias, grad_down_bias, grad_second_gain, grad_second_bias,
    )
    joined = jnp.concatenate([v.reshape(shards, -1) for v in small], axis=1).reshape(-1)
    owned = [
        lax.psum_scatter(value, "shard", scatter_dimension=0, tiled=True)
        for value in (
            grad_side, grad_in_weight, grad_out_weight, grad_up_weight, grad_down_weight, joined
        )
    ]
    side_grad, in_weight_grad, out_weight_grad, up_weight_grad, down_weight_grad = [
        widen(v) for v in lax.psum(tuple(v.astype(jnp.bfloat16) for v in owned[:5]), "rep")
    ]
    text_table_grad = widen(lax.psum(text_grad.astype(jnp.bfloat16), "rep"))
    pieces = lax.psum(owned[5], "rep")
    (
        batch_gain_grad,
        batch_bias_grad,
        embed_gain_grad,
        embed_bias_grad,
        in_bias_grad,
        out_bias_grad,
        first_gain_grad,
        first_bias_grad,
        up_bias_grad,
        down_bias_grad,
        second_gain_grad,
        second_bias_grad,
    ) = [pieces[low:high] for low, high in zip(marks, marks[1:])]
    return (
        out_rows,
        feature_grad,
        batch_gain_grad,
        batch_bias_grad,
        text_table_grad,
        side_grad,
        embed_gain_grad,
        embed_bias_grad,
        in_weight_grad,
        in_bias_grad,
        out_weight_grad,
        out_bias_grad,
        first_gain_grad,
        first_bias_grad,
        up_weight_grad,
        up_bias_grad,
        down_weight_grad,
        down_bias_grad,
        second_gain_grad,
        second_bias_grad,
    )


class Scatter:
    def __init__(self, index, total, near, relay, line, done, out, sems):
        self.index, self.total, self.near, self.relay, self.line = index, total, near, relay, line
        self.done, self.out = done, out
        self.send_sem, self.near_sem, self.relay_sem, self.line_sem, self.twin_sem, self.keep_sem = sems
        self.rep, self.z, self.y, self.x = spot()
        self.me = at(self.z, self.y, self.x)
        self.rows, self.half = near.shape[1], near.shape[2]

    def rows_at(self, source):
        return rows_of(source, self.rows, 16)

    def beside(self, plane, swap):
        even = lax.rem(plane + self.y + self.x + swap, 2) == 0
        return jnp.where(even, self.y, 1 - self.y), jnp.where(even, 1 - self.x, self.x)

    def copy(self, source, slot, target, dst, recv_sem):
        return pltpu.make_async_remote_copy(
            src_ref=self.total.at[self.rows_at(source)],
            dst_ref=dst,
            send_sem=self.send_sem.at[self.index, slot],
            recv_sem=recv_sem,
            device_id=(self.rep, target),
            device_id_type=MESH,
        )

    def near_copy(self, plane, kind):
        y, x = self.beside(plane, kind)
        target = at(self.z, y, x)
        source = at(plane, y, x) if kind == 0 else at(plane, 1 - self.y, 1 - self.x)
        slot = 2 * plane + kind
        return self.copy(
            source, slot, target, self.near.at[slot], self.near_sem.at[self.index, slot]
        )

    def relay_copy(self, plane):
        y, x = self.beside(plane, 1)
        return self.copy(
            at(plane, y, x), 8 + plane, at(self.z, y, x), self.relay.at[plane],
            self.relay_sem.at[self.index, plane],
        )

    def line_copy(self, plane):
        there = at(plane, self.y, self.x)
        return self.copy(
            there, 12 + plane, there, self.line.at[self.z], self.line_sem.at[self.index, self.z]
        )

    def line_wait(self, plane):
        self.copy(
            self.me, 12 + plane, self.me, self.line.at[plane], self.line_sem.at[self.index, plane]
        ).wait_recv()

    def hop_one(self):
        def step(k, carry):
            plane = lax.rem(self.z + k + 1, 4)
            self.near_copy(plane, 1).start()
            return carry

        lax.fori_loop(0, 4, step, 0)

        def again(k, carry):
            plane = lax.rem(self.z + k + 1, 4)
            self.near_copy(plane, 0).start()
            return carry

        lax.fori_loop(0, 4, again, 0)

    def hop_two(self):
        def step(k, carry):
            plane = lax.rem(self.z + k + 1, 4)
            self.near_copy(plane, 1).wait_recv()
            y, x = self.beside(plane, 1)
            rows = self.rows_at(at(plane, y, x))
            self.total[rows, :] = (
                widen(self.total[rows, :]) + widen(self.near[2 * plane + 1])
            ).astype(bf16)
            self.relay_copy(plane).start()
            return carry

        lax.fori_loop(0, 4, step, 0)

    def hop_three(self):
        def step(k, carry):
            plane = lax.rem(self.z + k + 1, 4)
            self.near_copy(plane, 0).wait_recv()
            self.relay_copy(plane).wait_recv()
            rows = self.rows_at(at(plane, self.y, self.x))
            self.total[rows, :] = (
                widen(self.total[rows, :]) + widen(self.near[2 * plane]) + widen(self.relay[plane])
            ).astype(bf16)

            @pl.when(k < 3)
            def _():
                self.line_copy(plane).start()

            return carry

        lax.fori_loop(0, 4, step, 0)

    def finals(self):
        columns = rows_of(self.rep, self.half, LANES)
        return (
            pltpu.make_async_copy(
                self.done, self.out.at[:, columns], self.keep_sem.at[self.index]
            ),
            pltpu.make_async_remote_copy(
                src_ref=self.done,
                dst_ref=self.out.at[:, columns],
                send_sem=self.send_sem.at[self.index, 16],
                recv_sem=self.twin_sem.at[self.index],
                device_id=(1 - self.rep, self.me),
                device_id_type=MESH,
            ),
        )

    def finish(self):
        rows = self.rows_at(self.me)
        self.done[...] = widen(self.total[rows, :])

        def add(k, carry):
            plane = lax.rem(self.z + k, 4)
            self.line_wait(plane)
            self.done[...] = self.done[...] + widen(self.line[plane])
            return carry

        lax.fori_loop(1, 4, add, 0)
        for copy in self.finals():
            copy.start()

    def drain(self):
        def step(k, carry):
            self.near_copy(k, 0).wait_send()
            self.near_copy(k, 1).wait_send()
            self.relay_copy(k).wait_send()

            @pl.when(k != self.z)
            def _():
                self.line_copy(k).wait_send()

            return carry

        lax.fori_loop(0, 4, step, 0)
        kept, twin = self.finals()
        kept.wait()
        twin.wait_send()
        twin.wait_recv()


def compress_vectors(narrow, middle, wide):
    shard_of = iota((16, 1), 0).astype(f32)
    owner, _ = remainder((1, 768), 1, 0, 48)
    stacked = jnp.concatenate(
        [jnp.where(owner == shard_of, narrow[k : k + 1, :], 0.0) for k in range(10)], axis=0
    ).astype(bf16)
    _, depth = remainder((768, 1), 0, 0, 48)
    _, want = remainder((1, 768), 1, 0, 48)
    spread = mm(stacked, onehot(depth == want))
    packed = sum(
        jnp.where(owner == k, spread[k * 16 : k * 16 + 16], 0.0) for k in range(10)
    )

    def piece(row, low, offset, size):
        total = size * 16
        holder, _ = remainder((1, total), 1, 0, size)
        _, place = remainder((total, 1), 0, 0, size)
        lane = iota((1, 256), 1).astype(f32) + (low - offset)
        return mm(jnp.where(holder == shard_of, row, 0.0).astype(bf16), onehot(place == lane))

    packed = packed + jnp.concatenate(
        [jnp.zeros((16, 384), f32), piece(middle, 384, 480, 96), jnp.zeros((16, 128), f32)], axis=1
    )
    return packed + jnp.concatenate(
        [jnp.zeros((16, 512), f32), piece(wide, 512, 576, 192)], axis=1
    )


def norm_back(grad, hat, scale, gain):
    gained = grad * gain
    return scale * (
        gained
        - jnp.mean(gained, axis=-1, keepdims=True)
        - hat * jnp.mean(gained * hat, axis=-1, keepdims=True)
    )


def backward_kernel(
    lens_ref, feat_ref, row_ref, cols_ref, lse_ref, vec_ref, last_ref, slot_ref, req_ref, stat_ref,
    w_in, w_out, w_up, w_down, emb_t, ctx_t, first_t, act_t, dgelu_h, xh0_h, xh1_h, gp2_h, qkv_h,
    feat_o, text_o, side_o, in_o, out_o, up_o, down_o, vec_o,
    w_in_s, w_out_s, act_b, down_b, up_b, dgelu_b, ctx_s, first_s, xh1, grad, qkv,
    low, low_twin, hidden, hidden_twin, branch, branch_twin, gctx, mixed, mixed_twin,
    looked, looked_twin, row_twin,
    down_g, up_g, out_g, in_g, side_g,
    down_n, up_n, out_n, in_n, side_n,
    down_r, up_r, out_r, in_r, side_r,
    down_l, up_l, out_l, in_l, side_l,
    down_d, up_d, out_d, in_d, side_d,
    text_u, text_in, text_d, ask_s, mask, feat_s, vectors, in_row, up_row, outbox, inbox,
    load_sem, act_sem, tile_sem, pair_send, pair_recv,
    send_sem, near_sem, relay_sem, line_sem, twin_sem, keep_sem,
    small_send, small_recv, text_ssem, text_rsem, text_keep,
):
    rep, z, y, x = spot()
    me = at(z, y, x)
    mine = rep * 16 + me
    vocab = text_d.shape[0]
    barrier = greet_all()

    loads = {}

    def load(name, source, target):
        loads[name] = pltpu.make_async_copy(source, target, load_sem.at[len(loads)])
        loads[name].start()

    load("grad", gp2_h, grad)

    def act_copy(i):
        slot = lax.rem(i, 4)
        return pltpu.make_async_copy(
            act_t.at[rows_of(i, 256, 256)], act_b.at[slot], act_sem.at[slot]
        )

    def tile_of(i):
        return lax.rem(i + 6 * (1 - rep), 12)

    def tile_copies(i):
        slot = lax.rem(i, 4)
        tile = rows_of(tile_of(i), 256, 256)
        return (
            pltpu.make_async_copy(w_down.at[tile], down_b.at[slot], tile_sem.at[0, slot]),
            pltpu.make_async_copy(w_up.at[:, tile], up_b.at[slot], tile_sem.at[1, slot]),
            pltpu.make_async_copy(dgelu_h.at[:, tile], dgelu_b.at[slot], tile_sem.at[2, slot]),
        )

    for k in range(3):
        for copy in tile_copies(k):
            copy.start()
    for k in range(3):
        act_copy(k).start()

    sems = (send_sem, near_sem, relay_sem, line_sem, twin_sem, keep_sem)
    down_a = Scatter(0, down_g, down_n, down_r, down_l, down_d, down_o, sems)
    up_a = Scatter(1, up_g, up_n, up_r, up_l, up_d, up_o, sems)
    out_a = Scatter(2, out_g, out_n, out_r, out_l, out_d, out_o, sems)
    in_a = Scatter(3, in_g, in_n, in_r, in_l, in_d, in_o, sems)
    side_a = Scatter(4, side_g, side_n, side_r, side_l, side_d, side_o, sems)

    paired = []

    def pair(source, target):
        copy = pltpu.make_async_remote_copy(
            src_ref=source,
            dst_ref=target,
            send_sem=pair_send.at[len(paired)],
            recv_sem=pair_recv.at[len(paired)],
            device_id=(1 - rep, me),
            device_id_type=MESH,
        )
        paired.append(copy)
        copy.start()
        return copy

    def half_of(width, core):
        return rows_of(core, width // 2, LANES)

    own_columns = rows_of(rep, BLOCK, LANES)
    twin_columns = rows_of(1 - rep, BLOCK, LANES)

    same = members(lens_ref, (BLOCK, 1), 0) == members(lens_ref, (1, BLOCK), 1)
    mask[...] = jnp.where(same, 0.0, -1e30)
    vectors[...] = jnp.concatenate(
        [jnp.zeros((8, 768), f32), last_ref[0:2, :], jnp.zeros((6, 768), f32)], axis=0
    )

    loads["grad"].wait()

    def second(c, total):
        rows = rows_of(c, 128, 128)
        value = grad[rows, :].astype(bf16)
        low[rows, :] = value
        return total + jnp.sum(widen(value), axis=0, keepdims=True)

    zero = jnp.zeros((1, 768), f32)
    vectors[7:8, :] = lax.fori_loop(0, 4, second, zero)
    pl.semaphore_wait(barrier, 31)
    row_pair = pair(row_ref, row_twin)
    low_pair = pair(low.at[:, half_of(768, 1 - rep)], low_twin)

    def feed(i, carry):
        slot = lax.rem(i, 4)
        for copy in tile_copies(i):
            copy.wait()

        @pl.when(i < 9)
        def _():
            for copy in tile_copies(i + 3):
                copy.start()

        tile = rows_of(tile_of(i), 256, 256)
        value = (widen(dgelu_b[slot]) * mm_nt(low[...], down_b[slot])).astype(bf16)
        hidden[:, tile] = value
        up_row[0:1, tile] = jnp.sum(widen(value), axis=0, keepdims=True)
        grad[...] = grad[...] + mm_nt(value, up_b[slot])
        return carry

    lax.fori_loop(0, 3, feed, 0)
    low_pair.wait_recv()

    def down_step(i, carry):
        slot = lax.rem(i, 4)
        act_copy(i).wait()

        @pl.when(i < 9)
        def _():
            act_copy(i + 3).start()

        down_g[rows_of(i, 256, 256), :] = (
            mm(act_b[slot, :, own_columns], low[:, half_of(768, rep)])
            + mm(act_b[slot, :, twin_columns], low_twin[...])
        ).astype(bf16)
        return carry

    lax.fori_loop(0, 12, down_step, 0)
    down_a.hop_one()

    load("first", first_t, first_s)
    load("xh1", xh1_h, xh1)
    load("out", w_out, w_out_s)
    load("qkv", qkv_h, qkv)
    load("ctx", ctx_t, ctx_s)
    load("in", w_in, w_in_s)

    lax.fori_loop(3, 6, feed, 0)
    hidden_pair = pair(hidden.at[:, half_of(3072, 1 - rep)], hidden_twin)
    lax.fori_loop(6, 12, feed, 0)
    down_a.hop_two()
    loads["first"].wait()
    hidden_pair.wait_recv()

    def up_step(i, carry):
        tile = rows_of(i, 256, 256)
        own = pl.ds(pl.multiple_of(rep * 1536 + i * 256, 256), 256)
        up_g[:, tile] = (
            mm(first_s[:, own_columns], hidden[:, own])
            + mm(first_s[:, twin_columns], hidden_twin[:, tile])
        ).astype(bf16)
        return carry

    lax.fori_loop(0, 6, up_step, 0)
    load("emb", emb_t, first_s)
    up_a.hop_one()

    loads["xh1"].wait()

    def norm_one(c, carry):
        rows = rows_of(c, 128, 128)
        value, hat = grad[rows, :], xh1[rows, :]
        back = norm_back(value, hat, cols_ref[rows, 1:2], vec_ref[5:6, :])
        grad[rows, :] = back
        rounded = back.astype(bf16)
        branch[rows, :] = rounded
        gain, bias, out = carry
        return (
            gain + jnp.sum(value * hat, axis=0, keepdims=True),
            bias + jnp.sum(value, axis=0, keepdims=True),
            out + jnp.sum(widen(rounded), axis=0, keepdims=True),
        )

    gain, bias, out = lax.fori_loop(0, 4, norm_one, (zero, zero, zero))
    load("xh0", xh0_h, xh1)
    vectors[4:5, :] = out
    vectors[5:6, :] = gain
    vectors[6:7, :] = bias
    branch_pair = pair(branch.at[:, half_of(768, 1 - rep)], branch_twin)
    loads["out"].wait()

    def context_step(i, carry):
        tile = rows_of(i, 256, 256)
        gctx[:, tile] = mm_nt(branch[...], w_out_s[tile, :]).astype(bf16)
        return carry

    lax.fori_loop(0, 3, context_step, 0)
    down_a.hop_three()
    loads["ctx"].wait()
    branch_pair.wait_recv()

    def out_step(i, carry):
        rows = rows_of(i, 256, 256)
        out_g[rows, :] = (
            mm(ctx_s[rows, own_columns], branch[:, half_of(768, rep)])
            + mm(ctx_s[rows, twin_columns], branch_twin[...])
        ).astype(bf16)
        return carry

    lax.fori_loop(0, 3, out_step, 0)
    out_a.hop_one()
    up_a.hop_two()

    loads["qkv"].wait()

    def attend(p, carry):
        pair_lanes = rows_of(p, LANES, LANES)
        query = qkv[:, pair_lanes]
        keys = qkv[:, rows_of(p + 6, LANES, LANES)]
        values = qkv[:, rows_of(p + 12, LANES, LANES)]
        outer = gctx[:, pair_lanes]
        keys_t = jnp.transpose(keys)
        query_t, key_parts, value_parts = [], [], []
        for head in range(2):
            in_head = iota((1, LANES), 1) // HEAD == head
            masked = query * jnp.where(in_head, 0.125, 0.0).astype(bf16)
            outer_masked = outer * jnp.where(in_head, 1.0, 0.0).astype(bf16)
            key_part = jnp.zeros((BLOCK, LANES), f32)
            value_part = jnp.zeros((BLOCK, LANES), f32)
            columns = []
            for part in range(2):
                s = slice(part * 256, part * 256 + 256)
                scores = mm_nt(keys, masked[s, :]) + mask[:, s]
                probs = jnp.exp(scores - lse_ref[pl.ds(2 * p + head, 1), s])
                grads = mm_nt(values, outer_masked[s, :])
                delta = jnp.sum(probs * grads, axis=0, keepdims=True)
                inner = (probs * (grads - delta)).astype(bf16)
                value_part = value_part + mm(probs.astype(bf16), outer[s, :])
                key_part = key_part + mm(inner, query[s, :])
                columns.append(mm(keys_t[head * HEAD : (head + 1) * HEAD, :], inner))
            query_t.append(jnp.concatenate(columns, axis=1))
            key_parts.append(key_part)
            value_parts.append(value_part)
        first_head = iota((1, LANES), 1) < HEAD
        gathered = (jnp.concatenate(query_t, axis=0) * 0.125).astype(bf16)
        mixed[:, pair_lanes] = jnp.transpose(gathered)
        mixed[:, rows_of(p + 6, LANES, LANES)] = (
            jnp.where(first_head, key_parts[0], key_parts[1]) * 0.125
        ).astype(bf16)
        mixed[:, rows_of(p + 12, LANES, LANES)] = jnp.where(
            first_head, value_parts[0], value_parts[1]
        ).astype(bf16)
        return carry

    lax.fori_loop(0, 2, attend, 0)
    out_a.hop_two()
    down_a.finish()
    lax.fori_loop(2, 4, attend, 0)
    up_a.hop_three()
    lax.fori_loop(4, 6, attend, 0)
    out_a.hop_three()
    mixed_pair = pair(mixed.at[:, half_of(2304, 1 - rep)], mixed_twin)

    loads["in"].wait()

    def embed_step(i, carry):
        tile = rows_of(i, 256, 256)
        grad[:, tile] = grad[:, tile] + mm_nt(mixed[...], w_in_s[tile, :])
        return carry

    lax.fori_loop(0, 3, embed_step, 0)

    def bias_step(i, carry):
        tile = rows_of(i, 256, 256)
        in_row[0:1, tile] = jnp.sum(widen(mixed[:, tile]), axis=0, keepdims=True)
        return carry

    lax.fori_loop(0, 9, bias_step, 0)
    loads["emb"].wait()
    mixed_pair.wait_recv()

    def in_step(i, carry):
        tile = rows_of(i, 384, 128)
        own = pl.ds(pl.multiple_of(rep * 1152 + i * 384, 128), 384)
        in_g[:, tile] = (
            mm(first_s[:, own_columns], mixed[:, own])
            + mm(first_s[:, twin_columns], mixed_twin[:, tile])
        ).astype(bf16)
        return carry

    lax.fori_loop(0, 3, in_step, 0)
    in_a.hop_one()

    loads["xh0"].wait()

    def norm_zero(c, carry):
        rows = rows_of(c, 128, 128)
        value, hat = grad[rows, :], xh1[rows, :]
        back = norm_back(value, hat, cols_ref[rows, 0:1], vec_ref[2:3, :])
        grad[rows, :] = back
        looked[rows, :] = back.astype(bf16)
        gain, bias, scales, shifts = carry
        kept = back * cols_ref[rows, 3:4]
        batch_hat = (widen(feat_ref[rows, :]) - stat_ref[0:1, :]) * stat_ref[1:2, :]
        return (
            gain + jnp.sum(value * hat, axis=0, keepdims=True),
            bias + jnp.sum(value, axis=0, keepdims=True),
            scales + jnp.sum(kept * batch_hat, axis=0, keepdims=True),
            shifts + jnp.sum(kept, axis=0, keepdims=True),
        )

    gain, bias, scales, shifts = lax.fori_loop(0, 4, norm_zero, (zero, zero, zero, zero))
    looked_pair = pair(looked.at[:, half_of(768, 1 - rep)], looked_twin)
    vectors[0:1, :] = scales
    vectors[1:2, :] = shifts
    vectors[2:3, :] = gain
    vectors[3:4, :] = bias
    packed = compress_vectors(
        vectors[...],
        jnp.concatenate([in_row[0:1, 0:768], in_row[0:1, 1536:2304]], axis=1),
        up_row[0:1, :],
    )
    for t in range(16):
        for j in range(6):
            lanes = slice(j * LANES, (j + 1) * LANES)
            outbox[t, j : j + 1, :] = packed[t : t + 1, lanes]
            outbox[t, 6 + j : 7 + j, :] = scales[:, lanes]
            outbox[t, 12 + j : 13 + j, :] = shifts[:, lanes]
        outbox[t, 18:24, :] = jnp.zeros((6, LANES), f32)
    exchange_all(outbox, inbox, small_send, small_recv, True)
    inbox[mine] = outbox[me]

    def text_sum(i, carry):
        rows = rows_of(i, 256, 256)
        place = (iota((256, 1), 0) + i * 256).astype(f32)
        text_u[rows, :] = mm(onehot(slot_ref[0:1, :] == place), looked[...]).astype(bf16)
        return carry

    lax.fori_loop(0, 16 * CAP // 256, text_sum, 0)

    def text_copy(k):
        there = lax.rem(mine + k, 32)
        return pltpu.make_async_remote_copy(
            src_ref=text_u.at[
                rows_of(lax.rem(there, 16), CAP, 16), rows_of(there // 16, 384, LANES)
            ],
            dst_ref=text_in.at[rows_of(mine, CAP, 16)],
            send_sem=text_ssem.at[k],
            recv_sem=text_rsem.at[mine],
            device_id=(there // 16, lax.rem(there, 16)),
            device_id_type=MESH,
        )

    def text_start(k, carry):
        text_copy(k).start()
        return carry

    lax.fori_loop(1, 32, text_start, 0)
    text_in[rows_of(mine, CAP, 16), :] = text_u[rows_of(me, CAP, 16), half_of(768, rep)]

    row_pair.wait_recv()
    looked_pair.wait_recv()
    for tile in range(5):
        base = tile * 512
        kinds = (1, 2) if base < BINS else (3, 4) if base < 2 * BINS else (5,)
        place = iota((512, 1), 0) + base % BINS

        def counted(ref):
            return sum((ref[k : k + 1, :] == place).astype(f32) for k in kinds).astype(bf16)

        side_g[base : base + 512, :] = (
            mm(counted(row_ref), looked[:, half_of(768, rep)])
            + mm(counted(row_twin), looked_twin[...])
        ).astype(bf16)
    side_a.hop_one()
    in_a.hop_two()
    up_a.finish()
    out_a.finish()

    _, want = remainder((1, 32 * CAP), 1, 0, CAP)
    sender, _ = remainder((1, 32 * CAP), 1, 0, CAP)
    pick = onehot(iota((LANES, 1), 0).astype(f32) == want)
    asked = req_ref[...] + 1.0
    coarse = jnp.floor(asked * (1.0 / 32.0))
    fine = asked - 32.0 * coarse
    place = 32.0 * mm(coarse.astype(bf16), pick) + mm(fine.astype(bf16), pick)
    ours = sender == iota((32, 1), 0).astype(f32)
    ask_s[0:1, :] = jnp.sum(jnp.where(ours, place, 0.0), axis=0, keepdims=True)

    side_a.hop_two()
    in_a.hop_three()

    def text_wait(k, carry):
        there = lax.rem(mine + k, 32)
        pltpu.make_async_remote_copy(
            src_ref=text_in.at[rows_of(there, CAP, 16)],
            dst_ref=text_in.at[rows_of(there, CAP, 16)],
            send_sem=text_ssem.at[k],
            recv_sem=text_rsem.at[there],
            device_id=(rep, me),
            device_id_type=MESH,
        ).wait_recv()
        return carry

    lax.fori_loop(1, 32, text_wait, 0)

    def text_step(i, carry):
        rows = rows_of(i, 192, 64)
        place = (iota((192, 1), 0) + (i * 192 + 1)).astype(f32)
        text_d[rows, :] = mm(onehot(ask_s[0:1, :] == place), text_in[...])
        return carry

    lax.fori_loop(0, vocab // 192, text_step, 0)
    text_local = pltpu.make_async_copy(text_d, text_o.at[:, half_of(768, rep)], text_keep.at[0])
    text_local.start()
    text_pair = pair(text_d, text_o.at[:, half_of(768, rep)])

    exchange_all(outbox, inbox, small_send, small_recv, False)
    sums = sum(inbox[t] for t in range(32))
    vec_o[...] = sums[0:8, :]
    scale_row = jnp.concatenate([sums[6 + j : 7 + j, :] for j in range(6)], axis=1)
    shift_row = jnp.concatenate([sums[12 + j : 13 + j, :] for j in range(6)], axis=1)
    scale_row = scale_row / stat_ref[2:3, :]
    shift_row = shift_row / stat_ref[2:3, :]

    def feature(c, carry):
        rows = rows_of(c, 128, 128)
        batch_hat = (widen(feat_ref[rows, :]) - stat_ref[0:1, :]) * stat_ref[1:2, :]
        value = grad[rows, :] - shift_row - batch_hat * scale_row
        feat_s[rows, :] = (
            cols_ref[rows, 3:4] * (vec_ref[0:1, :] * stat_ref[1:2, :]) * value
        ).astype(bf16)
        return carry

    lax.fori_loop(0, 4, feature, 0)
    feat_local = pltpu.make_async_copy(feat_s, feat_o, text_keep.at[1])
    feat_local.start()
    side_a.hop_three()
    in_a.finish()
    side_a.finish()

    for a in (down_a, up_a, out_a, in_a, side_a):
        a.drain()

    def text_drain(k, carry):
        text_copy(k).wait_send()
        return carry

    lax.fori_loop(1, 32, text_drain, 0)
    for copy in paired:
        copy.wait_send()
    text_pair.wait_recv()
    text_local.wait()
    feat_local.wait()


def backward_call(lens, feat, row, made, vocab):
    (
        w_in, w_out, w_up, w_down, emb_t, ctx_t, first_t, act_t, dgelu, xh0, xh1, gp2, qkv, _,
        cols, lse, vec, _, _, last, slot, req, stat,
    ) = made
    vm, hbm = pl.BlockSpec(memory_space=pltpu.VMEM), pl.BlockSpec(memory_space=pl.ANY)
    sm = pl.BlockSpec(memory_space=pltpu.SMEM)
    v = lambda *dims, dtype=bf16: pltpu.VMEM(dims, dtype)
    dma = pltpu.SemaphoreType.DMA
    parts = [(192, 384), (48, 1536), (48, 384), (48, 1152), (160, 384)]
    return pl.pallas_call(
        backward_kernel,
        name="backward",
        out_shape=(
            shape(BLOCK, 768, dtype=bf16), shape(vocab, 768), shape(160, 768), shape(48, 2304),
            shape(48, 768), shape(48, 3072), shape(192, 768), shape(8, LANES),
        ),
        in_specs=[sm] + [vm] * 9 + [hbm] * 13,
        out_specs=tuple([hbm] * 7 + [vm]),
        scratch_shapes=[
            v(768, 2304), v(768, 768), v(4, 256, 1024), v(4, 256, 768), v(4, 768, 256),
            v(4, BLOCK, 256), v(768, 1024), v(768, 1024),
            v(BLOCK, 768, dtype=f32), v(BLOCK, 768, dtype=f32),
            v(BLOCK, 2304),
            v(BLOCK, 768), v(BLOCK, 384), v(BLOCK, 3072), v(BLOCK, 1536), v(BLOCK, 768),
            v(BLOCK, 384), v(BLOCK, 768), v(BLOCK, 2304), v(BLOCK, 1152),
            v(BLOCK, 768), v(BLOCK, 384), v(8, BLOCK, dtype=jnp.int32),
            *(v(16 * r, c) for r, c in parts),
            *(v(8, r, c) for r, c in parts),
            *(v(4, r, c) for r, c in parts),
            *(v(4, r, c) for r, c in parts),
            *(v(r, c, dtype=f32) for r, c in parts),
            v(16 * CAP, 768), v(32 * CAP, 384), v(vocab, 384, dtype=f32),
            v(8, 32 * CAP, dtype=f32), v(BLOCK, BLOCK, dtype=f32), v(BLOCK, 768),
            v(16, 768, dtype=f32), v(8, 2304, dtype=f32), v(8, 3072, dtype=f32),
            v(16, 24, LANES, dtype=f32), v(32, 24, LANES, dtype=f32),
            dma((9,)), dma((4,)), dma((3, 4)), dma((8,)), dma((8,)),
            dma((5, 17)), dma((5, 8)), dma((5, 4)), dma((5, 4)), dma((5,)), dma((5,)),
            dma((32,)), dma((32,)), dma((32,)), dma((32,)), dma((2,)),
        ],
        compiler_params=pltpu.CompilerParams(
            collective_id=1, has_side_effects=True, vmem_limit_bytes=62 * 2**20
        ),
    )(
        lens, feat, row, cols, lse, vec, last, slot, req, stat,
        w_in, w_out, w_up, w_down, emb_t, ctx_t, first_t, act_t, dgelu, xh0, xh1, gp2, qkv,
    )


def backward(args, row, made):
    got = backward_call(args[4], args[0], row, made, args[8].shape[0])
    feature_grad, g_text, g_side, g_in, g_out, g_up, g_down, pieces = got
    pieces = pieces.reshape(-1)
    cut = lambda k: pieces[k * 48 : (k + 1) * 48]
    return (
        made[13], feature_grad, cut(0), cut(1), g_text, g_side, cut(2), cut(3), g_in,
        pieces[480:576], g_out, cut(4), cut(5), cut(6), g_up, pieces[576:768], g_down, cut(7),
        cut(8), cut(9),
    )

def fast(*args):
    (
        region_features, text_ids, boxes, segment_ids, document_lengths, cotangent,
        batch_gain, batch_bias, text_table, side_table, embed_gain, embed_bias,
        in_weight, in_bias, out_weight, out_bias, first_gain, first_bias,
        up_weight, up_bias, down_weight, down_bias, second_gain, second_bias,
    ) = args
    vocab = text_table.shape[0]
    col = pack_indices(text_ids, boxes, segment_ids, vocab)
    row = col.T
    vec = jnp.stack(
        [
            jnp.pad(widen(v), (0, 256 - v.shape[0]))
            for v in (
                batch_gain, batch_bias, embed_gain, embed_bias, out_bias, first_gain, first_bias,
                down_bias, second_gain, second_bias, in_bias, up_bias,
            )
        ]
    )
    made = forward_call(
        document_lengths, region_features, col, row, vec, cotangent, text_table,
        side_table, in_weight, out_weight, up_weight, down_weight,
    )
    return lax.cond(made[-1][3, 0] > CAP, lambda: general(*args), lambda: backward(args, row, made))


def fits(mesh):
    return dict(mesh.shape) == {"rep": 2, "shard": 16}


def solution(mesh):
    in_specs = (
        P(("rep", "shard"), None),
        P(("rep", "shard")),
        P(("rep", "shard"), None),
        P(("rep", "shard")),
        P(("rep", "shard"), None),
        P(("rep", "shard"), None),
        P("shard"),
        P("shard"),
        P("shard", None),
        P("shard", None),
        P("shard"),
        P("shard"),
        P("shard", None),
        P("shard"),
        P("shard", None),
        P("shard"),
        P("shard"),
        P("shard"),
        P("shard", None),
        P("shard"),
        P("shard", None),
        P("shard"),
        P("shard"),
        P("shard"),
    )
    out_specs = (
        P(("rep", "shard"), None),
        P(("rep", "shard"), None),
        P("shard"),
        P("shard"),
        P("shard", None),
        P("shard", None),
        P("shard"),
        P("shard"),
        P("shard", None),
        P("shard"),
        P("shard", None),
        P("shard"),
        P("shard"),
        P("shard"),
        P("shard", None),
        P("shard"),
        P("shard", None),
        P("shard"),
        P("shard"),
        P("shard"),
    )
    return jax.shard_map(
        fast if fits(mesh) else general, mesh=mesh, in_specs=in_specs, out_specs=out_specs, check_vma=False
    )
```

```python
import functools
import math

import jax
import jax.numpy as jnp
from jax import lax
from jax.experimental import pallas as pl
from jax.experimental.pallas import tpu as pltpu
from jax.sharding import PartitionSpec as P

HEAD = 64
BINS = 1024
SIDE = 2560
BLOCK = 512
SLOTS = 4
CAP = 64
LANES = 128
MESH = pl.DeviceIdType.MESH
f32 = jnp.float32
bf16 = jnp.bfloat16

epsilon = 1e-05


def widen(value):
    return value.astype(jnp.float32)


def mm(a, b):
    return jnp.dot(a, b, preferred_element_type=f32)


def mm_nt(a, b):
    return lax.dot_general(a, b, (((1,), (1,)), ((), ())), preferred_element_type=f32)


def iota(shape, dim):
    return lax.broadcasted_iota(jnp.int32, shape, dim)


def spot():
    shard = lax.axis_index("shard")
    return lax.axis_index("rep"), shard // 4, (shard // 2) % 2, shard % 2


def at(z, y, x):
    return z * 4 + y * 2 + x


def rows_of(start, size, step):
    return pl.ds(pl.multiple_of(start * size, step), size)


class Gather:
    def __init__(self, index, shard_ref, full_ref, own_sem, send_sem, recv_sem, twin_sem):
        self.index, self.shard, self.full = index, shard_ref, full_ref
        self.own_sem, self.send_sem, self.recv_sem, self.twin_sem = own_sem, send_sem, recv_sem, twin_sem
        self.rep, self.z, self.y, self.x = spot()
        self.me = at(self.z, self.y, self.x)
        self.rows = shard_ref.shape[0]
        self.half = shard_ref.shape[1] // 2

    def block(self, source, half):
        return self.full.at[
            rows_of(source, self.rows, 16), rows_of(half, self.half, LANES)
        ]

    def copy(self, source, slot, target, src=None, twin=False):
        return pltpu.make_async_remote_copy(
            src_ref=self.block(source, self.rep) if src is None else src,
            dst_ref=self.block(source, self.rep),
            send_sem=self.send_sem.at[self.index, slot],
            recv_sem=(self.twin_sem if twin else self.recv_sem).at[self.index, source],
            device_id=target,
            device_id_type=MESH,
        )

    def own(self):
        return pltpu.make_async_copy(
            self.shard, self.full.at[rows_of(self.me, self.rows, 16)], self.own_sem.at[self.index]
        )

    def start_line(self):
        src = self.shard.at[:, rows_of(self.rep, self.half, LANES)]

        def step(k, carry):
            there = lax.rem(self.z + k, 4)
            self.copy(self.me, there, (self.rep, at(there, self.y, self.x)), src=src).start()
            return carry

        lax.fori_loop(1, 4, step, 0)

    def start_own(self):
        src = self.shard.at[:, rows_of(self.rep, self.half, LANES)]
        self.copy(self.me, 4 + self.z, self.beside(self.z, 0), src=src).start()
        self.copy(self.me, 8 + self.z, self.beside(self.z, 1), src=src).start()
        self.own().start()

    def to_twin(self, source):
        self.copy(source, 16 + source, (1 - self.rep, self.me), twin=True).start()

    def beside(self, plane, swap):
        even = lax.rem(plane + self.y + self.x + swap, 2) == 0
        return (
            self.rep,
            at(self.z, jnp.where(even, self.y, 1 - self.y), jnp.where(even, 1 - self.x, self.x)),
        )

    def hop_one(self):
        def step(k, carry):
            plane = lax.rem(self.z + k, 4)
            source = at(plane, self.y, self.x)
            self.copy(source, 0, (self.rep, self.me)).wait_recv()
            self.copy(source, 4 + plane, self.beside(plane, 0)).start()
            self.copy(source, 8 + plane, self.beside(plane, 1)).start()
            self.to_twin(source)
            return carry

        lax.fori_loop(1, 4, step, 0)

    def hop_two(self):
        def step(k, carry):
            plane = lax.rem(self.z + k, 4)
            even = lax.rem(plane + self.y + self.x, 2) == 0
            source = at(
                plane, jnp.where(even, 1 - self.y, self.y), jnp.where(even, self.x, 1 - self.x)
            )
            self.copy(source, 0, (self.rep, self.me)).wait_recv()
            self.copy(source, 12 + plane, self.beside(plane, 0)).start()
            self.to_twin(source)
            return carry

        lax.fori_loop(0, 4, step, 0)

    def last(self):
        def step(k, carry):
            plane = lax.rem(self.z + k, 4)
            even = lax.rem(plane + self.y + self.x, 2) == 0
            near = at(
                plane, jnp.where(even, self.y, 1 - self.y), jnp.where(even, 1 - self.x, self.x)
            )
            far = at(plane, 1 - self.y, 1 - self.x)
            for source in (near, far):
                self.copy(source, 0, (self.rep, self.me)).wait_recv()
                self.to_twin(source)
            return carry

        lax.fori_loop(0, 4, step, 0)

    def ready(self):
        self.own().wait()

        def step(k, carry):
            source = lax.rem(self.me + k, 16)
            pltpu.make_async_remote_copy(
                src_ref=self.block(source, 1 - self.rep),
                dst_ref=self.block(source, 1 - self.rep),
                send_sem=self.send_sem.at[self.index, 0],
                recv_sem=self.twin_sem.at[self.index, source],
                device_id=(self.rep, self.me),
                device_id_type=MESH,
            ).wait_recv()
            return carry

        lax.fori_loop(1, 16, step, 0)

    def drain(self):
        def step(k, carry):
            @pl.when((k != self.z) & (k != 16 + self.me))
            def _():
                self.copy(self.me, k, (self.rep, self.me)).wait_send()

            return carry

        lax.fori_loop(0, 32, step, 0)


def exchange(outbox, inbox, send_sem, recv_sem, start):
    rep, me = lax.axis_index("rep"), lax.axis_index("shard")
    each = len(outbox.shape) == 3

    def copy(k, source):
        there = lax.rem(me + k, 16)
        return pltpu.make_async_remote_copy(
            src_ref=outbox.at[there] if each else outbox,
            dst_ref=inbox.at[source],
            send_sem=send_sem.at[k],
            recv_sem=recv_sem.at[source],
            device_id=(rep, there),
            device_id_type=MESH,
        )

    def begin(k, carry):
        copy(k, me).start()
        return carry

    def done(k, carry):
        sent = copy(k, lax.rem(me + k, 16))
        sent.wait_send()
        sent.wait_recv()
        return carry

    lax.fori_loop(1, 16, begin if start else done, 0)


def greet():
    barrier = pltpu.get_barrier_semaphore()
    rep, me = lax.axis_index("rep"), lax.axis_index("shard")

    def step(k, carry):
        pl.semaphore_signal(
            barrier, inc=1, device_id=(rep, lax.rem(me + k, 16)), device_id_type=MESH
        )
        return carry

    lax.fori_loop(1, 16, step, 0)
    pl.semaphore_signal(barrier, inc=1, device_id=(1 - rep, me), device_id_type=MESH)
    return barrier


def members(lens_ref, shape, dim):
    place = iota(shape, dim)
    end = jnp.int32(0)
    member = jnp.zeros(shape, jnp.int32)
    for slot in range(SLOTS):
        end = end + lens_ref[0, slot]
        member = member + (place >= end).astype(jnp.int32)
    return member


def spread_rows(value):
    return lax.rsqrt(jnp.mean(value * value, axis=-1, keepdims=True) + epsilon)


def onehot(condition):
    return jnp.where(condition, 1.0, 0.0).astype(bf16)


def remainder(shape, dim, offset, size):
    place = iota(shape, dim).astype(f32) - offset
    group = jnp.floor((place + 0.5) * (1.0 / size))
    return group, place - group * size


def expand_vectors(packed):
    def select(low, width, offset, size):
        _, want = remainder((1, size * 16), 1, 0, size)
        depth = iota((width, 1), 0).astype(f32) + (low - offset)
        return onehot(depth == want)

    kinds, _ = remainder((1, 768), 1, 0, 48)
    stacked = jnp.concatenate(
        [jnp.where(kinds == k, packed, 0.0) for k in range(10)], axis=0
    ).astype(bf16)
    _, depth = remainder((768, 1), 0, 0, 48)
    _, want = remainder((1, 768), 1, 0, 48)
    spread = mm(stacked, onehot(depth == want))
    owner, _ = remainder((1, 768), 1, 0, 48)
    shard_of = iota((16, 1), 0).astype(f32)
    narrow = jnp.concatenate(
        [
            jnp.sum(jnp.where(owner == shard_of, spread[k * 16 : k * 16 + 16], 0.0), axis=0, keepdims=True)
            for k in range(10)
        ],
        axis=0,
    )
    low = packed.astype(bf16)
    owner, _ = remainder((1, 1536), 1, 0, 96)
    middle = mm(low[:, 384:640], select(384, 256, 480, 96))
    middle = jnp.sum(jnp.where(owner == shard_of, middle, 0.0), axis=0, keepdims=True)
    owner, _ = remainder((1, 3072), 1, 0, 192)
    wide = mm(low[:, 512:768], select(512, 256, 576, 192))
    wide = jnp.sum(jnp.where(owner == shard_of, wide, 0.0), axis=0, keepdims=True)
    return narrow, middle, wide


def transpose_to(target, source):
    for j in range(source.shape[1] // LANES):
        target[j * LANES : (j + 1) * LANES, :] = jnp.transpose(
            source[:, j * LANES : (j + 1) * LANES]
        )


def forward_kernel(
    dense, lens_ref, feat_ref, col_ref, row_ref, vec_ref, cot_ref, text_ref,
    side_sh, in_sh, out_sh, up_sh, down_sh, *rest,
):
    extra_ref = rest[0] if dense else None
    forward_body(
        dense, extra_ref, lens_ref, feat_ref, col_ref, row_ref, vec_ref, cot_ref, text_ref,
        side_sh, in_sh, out_sh, up_sh, down_sh, *rest[1 if dense else 0 :],
    )


def forward_body(
    dense, extra_ref, lens_ref, feat_ref, col_ref, row_ref, vec_ref, cot_ref, text_ref,
    side_sh, in_sh, out_sh, up_sh, down_sh,
    w_in, w_out, w_up, w_down, emb_t, ctx_t, first_t, act_t,
    dgelu_o, xh0_o, xh1_o, gp2_o, qkv_o, rows_o,
    col_o, lse_o, vec_o, bias1_o, bias2_o, last_o, slot_o, req_o, stat_o, row_o,
    side_f, in_f, out_f, up_f, down_f,
    row_twin, stat_out, stat_twin, ask_out, ask_in, vec_s, outbox, inbox,
    text_send, text_recv, mask,
    low, wide_s, qkv, ctx_s, ctx, act, act_s, dgelu, emb_s, first_s, xh0, xh1, first, gp2, rows_s,
    own_sem, send_sem, recv_sem, twin_sem, ask_send, ask_recv, small_send, small_recv,
    text_ssem, text_rsem, text_tsend, text_trecv, two_send, two_recv,
    keep_sem, pair_send, pair_recv,
):
    rep, z, y, x = spot()
    me = at(z, y, x)
    vocab = text_ref.shape[0]
    barrier = greet()

    side_a, in_a, out_a, up_a, down_a = arrays = [
        Gather(i, sh, full, own_sem, send_sem, recv_sem, twin_sem)
        for i, (sh, full) in enumerate(
            ((side_sh, side_f), (in_sh, in_f), (out_sh, out_f), (up_sh, up_f), (down_sh, down_f))
        )
    ]

    kept = []

    def keep(source, target):
        copy = pltpu.make_async_copy(source, target, keep_sem.at[len(kept)])
        kept.append(copy)
        copy.start()

    paired = []

    def pair(source, target):
        columns = target.at[:, rows_of(rep, BLOCK, LANES)]
        keep(source, columns)
        copy = pltpu.make_async_remote_copy(
            src_ref=source,
            dst_ref=columns,
            send_sem=pair_send.at[len(paired)],
            recv_sem=pair_recv.at[len(paired)],
            device_id=(1 - rep, me),
            device_id_type=MESH,
        )
        paired.append(copy)
        copy.start()

    twins = []

    def to_twin(source, target):
        copy = pltpu.make_async_remote_copy(
            src_ref=source,
            dst_ref=target,
            send_sem=two_send.at[len(twins)],
            recv_sem=two_recv.at[len(twins)],
            device_id=(1 - rep, me),
            device_id_type=MESH,
        )
        twins.append(copy)
        copy.start()
        return copy

    valid = (members(lens_ref, (BLOCK, 1), 0) < SLOTS).astype(f32)
    count = jnp.sum(valid, axis=0, keepdims=True)
    col_o[:, 3:4] = valid

    def add_total(c, total):
        rows = rows_of(c, 64, 64)
        return total + jnp.sum(widen(feat_ref[rows, :]) * col_o[rows, 3:4], axis=0, keepdims=True)

    local = lax.fori_loop(0, 8, add_total, jnp.zeros((1, 768), f32)) / jnp.maximum(count, 1.0)

    def add_square(c, square):
        rows = rows_of(c, 64, 64)
        center = widen(feat_ref[rows, :]) - local
        return square + jnp.sum(center * center * col_o[rows, 3:4], axis=0, keepdims=True)

    square = lax.fori_loop(0, 8, add_square, jnp.zeros((1, 768), f32))

    for j in range(6):
        stat_out[j : j + 1, :] = local[:, j * LANES : (j + 1) * LANES]
        stat_out[6 + j : 7 + j, :] = square[:, j * LANES : (j + 1) * LANES]
    stat_out[12:16, :] = jnp.broadcast_to(count, (4, LANES))
    pl.semaphore_wait(barrier, 16)
    row_pair = to_twin(row_ref, row_twin)
    stat_pair = to_twin(stat_out, stat_twin)

    side_a.start_own()
    side_a.start_line()
    in_a.start_own()
    in_a.start_line()
    limit = 0 if dense else CAP
    row_pair.wait_recv()
    row_o[...] = row_twin[...]
    twin_columns = jnp.transpose(
        jnp.concatenate([widen(row_twin[...]), jnp.zeros((LANES - 8, BLOCK), f32)], axis=0)
    )
    all_c = jnp.concatenate([widen(col_ref[...]), twin_columns[:, 0:8]], axis=0)
    ids_c, base_c, owner_c = all_c[:, 0:1], all_c[:, 6:7], all_c[:, 7:8]
    ids_r = widen(jnp.concatenate([row_ref[0:1, :], row_twin[0:1, :]], axis=1))
    earlier = iota((2 * BLOCK, 1), 0) < iota((1, 2 * BLOCK), 1)
    first_r = 1.0 - jnp.max(
        jnp.where(earlier & (ids_c == ids_r), 1.0, 0.0), axis=0, keepdims=True
    )
    rank_c = jnp.sum(
        jnp.where((ids_r < ids_c) & (ids_r >= base_c), first_r, 0.0), axis=1, keepdims=True
    )
    most = jnp.max(rank_c, axis=0, keepdims=True) + 1.0
    slot_c = jnp.where(rank_c < limit, owner_c * CAP + rank_c, -1.0)
    col_o[:, 2:3] = slot_c[0:BLOCK]
    slot_o[...] = jnp.transpose(jnp.broadcast_to(slot_c[0:BLOCK], (BLOCK, LANES)))[0:8, :]
    within = ids_c - base_c
    lane = iota((1, LANES), 1).astype(f32)
    for t in range(16):
        hit = jnp.where((owner_c == t) & (rank_c < limit), rank_c, -1.0) == lane
        ask = jnp.max(jnp.where(hit, within, -1.0), axis=0, keepdims=True)
        ask_out[t] = jnp.broadcast_to(ask, (8, LANES))
    exchange(ask_out, ask_in, ask_send, ask_recv, True)
    ask_in[me] = ask_out[me]

    pieces = jnp.concatenate(
        [vec_ref[k : k + 1, 0:48] for k in range(10)]
        + [vec_ref[10:11, 0:96], vec_ref[11:12, 0:192]],
        axis=1,
    )
    for j in range(6):
        vec_s[j : j + 1, :] = pieces[:, j * LANES : (j + 1) * LANES]
    stat_pair.wait_recv()
    count_one, count_two = stat_out[12:13, :], stat_twin[12:13, :]
    both = jnp.maximum(count_one + count_two, 1.0)
    part = pl.ds(rep * 3, 3)
    part_two = pl.ds(6 + rep * 3, 3)
    mean_one, mean_two = stat_out[part, :], stat_twin[part, :]
    mean = (mean_one * count_one + mean_two * count_two) / both
    outbox[0:3, :] = mean
    outbox[3:6, :] = (
        stat_out[part_two, :]
        + stat_twin[part_two, :]
        + count_one * (mean_one - mean) * (mean_one - mean)
        + count_two * (mean_two - mean) * (mean_two - mean)
    )
    outbox[6:7, :] = jnp.where(lane == 1.0, most, count_one + count_two)
    outbox[7:10, :] = vec_s[part, :]
    outbox[10:16, :] = jnp.zeros((6, LANES), f32)
    exchange(outbox, inbox.at[rep], small_send, small_recv, True)
    inbox[rep, me] = outbox[...]
    out_a.start_own()
    up_a.start_own()
    down_a.start_own()
    same = members(lens_ref, (BLOCK, 1), 0) == members(lens_ref, (1, BLOCK), 1)
    mask[...] = jnp.where(same, 0.0, -1e30)

    side_a.hop_one()
    exchange(ask_out, ask_in, ask_send, ask_recv, False)

    asked = jnp.concatenate([ask_in[t, 0:1, :] for t in range(16)], axis=0)
    req_o[...] = asked
    asked = jnp.concatenate([asked, jnp.full((LANES - 16, LANES), -1.0, f32)], axis=0)
    asked = jnp.transpose(asked)
    column = iota((1, vocab), 1).astype(f32)
    half = rows_of(rep, 384, LANES)
    for c in range(4):
        pick = jnp.concatenate(
            [onehot(asked[:CAP, t : t + 1] == column) for t in range(4 * c, 4 * c + 4)], axis=0
        )
        text_send[c * 256 : c * 256 + 256, :] = mm(pick, text_ref[:, half]).astype(bf16)

    def text_copy(t, source):
        return pltpu.make_async_remote_copy(
            src_ref=text_send.at[rows_of(t, CAP, 16)],
            dst_ref=text_recv.at[rows_of(source, CAP, 16), half],
            send_sem=text_ssem.at[t],
            recv_sem=text_rsem.at[source],
            device_id=(rep, t),
            device_id_type=MESH,
        )

    def text_twin(source, core):
        block = text_recv.at[rows_of(source, CAP, 16), rows_of(core, 384, LANES)]
        return pltpu.make_async_remote_copy(
            src_ref=block,
            dst_ref=block,
            send_sem=text_tsend.at[source],
            recv_sem=text_trecv.at[source],
            device_id=(1 - rep, me),
            device_id_type=MESH,
        )

    def text_start(k, carry):
        text_copy(lax.rem(me + k, 16), me).start()
        return carry

    lax.fori_loop(1, 16, text_start, 0)
    out_a.start_line()
    up_a.start_line()
    text_recv[rows_of(me, CAP, 16), half] = text_send[rows_of(me, CAP, 16), :]
    text_twin(me, rep).start()

    exchange(outbox, inbox.at[rep], small_send, small_recv, False)
    to_twin(inbox.at[rep], inbox.at[rep]).wait_recv()

    def gathered(j):
        return jnp.concatenate([inbox[0, t, j : j + 1, :] for t in range(16)], axis=0)

    def gathered_half(core, j):
        return jnp.concatenate([inbox[core, t, j : j + 1, :] for t in range(16)], axis=0)

    tail = gathered(6)
    counts = tail[:, 0:1]
    all_rows = jnp.sum(counts, axis=0, keepdims=True)
    means, spreads = [], []
    for j in range(6):
        part = gathered_half(j // 3, j % 3)
        mean = jnp.sum(part * counts, axis=0, keepdims=True) / all_rows
        shift = part - mean
        variance = (
            jnp.sum(gathered_half(j // 3, 3 + j % 3) + counts * shift * shift, axis=0, keepdims=True)
            / all_rows
        )
        means.append(mean)
        spreads.append(lax.rsqrt(variance + epsilon))
    mean = jnp.concatenate(means, axis=1)
    spread = jnp.concatenate(spreads, axis=1)
    most = jnp.max(tail[:, 1:2], axis=0, keepdims=True)
    stat_o[...] = jnp.concatenate(
        [
            mean,
            spread,
            jnp.broadcast_to(all_rows, (1, 768)),
            jnp.broadcast_to(most, (1, 768)),
            jnp.zeros((4, 768), f32),
        ],
        axis=0,
    )
    packed = jnp.concatenate([gathered_half(j // 3, 7 + j % 3) for j in range(6)], axis=1)
    narrow, middle, wide = expand_vectors(packed)
    vec_o[...] = jnp.concatenate([narrow, jnp.zeros((6, 768), f32)], axis=0)
    bias1_o[...] = jnp.broadcast_to(middle, (8, 1536))
    bias2_o[...] = jnp.broadcast_to(wide, (8, 3072))


    side_a.hop_two()
    in_a.hop_one()
    side_a.last()
    side_a.ready()
    def embed(c, carry):
        rows = rows_of(c, 128, 128)
        hat = (widen(feat_ref[rows, :]) - stat_o[0:1, :]) * stat_o[1:2, :]
        begin = hat * vec_o[0:1, :] + vec_o[1:2, :]
        where = col_ref[rows, :]
        bins = iota((1, BINS), 1)
        hits = (where[:, 1:2] == bins).astype(f32) + (where[:, 2:3] == bins).astype(f32)
        begin = begin + mm(hits.astype(bf16), side_f[0:BINS, :])
        hits = (where[:, 3:4] == bins).astype(f32) + (where[:, 4:5] == bins).astype(f32)
        begin = begin + mm(hits.astype(bf16), side_f[BINS : 2 * BINS, :])
        segments = iota((1, SIDE - 2 * BINS), 1)
        begin = begin + mm(onehot(where[:, 5:6] == segments), side_f[2 * BINS :, :])
        if dense:
            begin = begin + widen(extra_ref[rows, :])
        wide_s[rows, :] = begin
        return carry

    lax.fori_loop(0, 4, embed, 0)

    in_a.hop_two()
    out_a.hop_one()
    in_a.last()
    def text_wait(k, carry):
        there = lax.rem(me + k, 16)
        text_copy(there, there).wait_recv()
        text_twin(there, rep).start()
        return carry

    lax.fori_loop(1, 16, text_wait, 0)

    def text_ready(k, carry):
        text_twin(k, 1 - rep).wait_recv()
        return carry

    lax.fori_loop(0, 16, text_ready, 0)

    down_a.start_line()
    def embed_norm(c, carry):
        rows = rows_of(c, 128, 128)
        slots = iota((1, 16 * CAP), 1).astype(f32)
        begin = wide_s[rows, :] + mm(onehot(col_o[rows, 2:3] == slots), text_recv[...])
        center = begin - jnp.mean(begin, axis=-1, keepdims=True)
        scale = spread_rows(center)
        hat = center * scale
        xh0[rows, :] = hat
        col_o[rows, 0:1] = scale
        value = hat * vec_o[2:3, :] + vec_o[3:4, :]
        wide_s[rows, :] = value
        low[rows, :] = value.astype(bf16)
        return carry

    lax.fori_loop(0, 4, embed_norm, 0)
    keep(xh0, xh0_o)
    transpose_to(emb_s, low)
    pair(emb_s, emb_t)
    up_a.hop_one()
    out_a.hop_two()
    in_a.ready()
    keep(in_f, w_in)

    def project(i, carry):
        columns = rows_of(i, 256, 256)
        qkv[:, columns] = mm(low[...], in_f[:, columns]).astype(bf16)
        return carry

    def project_biased(i, carry):
        columns = rows_of(i, 256, 256)
        source = rows_of(lax.rem(i, 6), 256, 256)
        qkv[:, columns] = (mm(low[...], in_f[:, columns]) + bias1_o[0:1, source]).astype(bf16)
        return carry

    lax.fori_loop(0, 3, project_biased, 0)
    lax.fori_loop(3, 6, project, 0)

    def project_values(i, carry):
        columns = rows_of(i + 6, 256, 256)
        source = rows_of(i + 3, 256, 256)
        qkv[:, columns] = (mm(low[...], in_f[:, columns]) + bias1_o[0:1, source]).astype(bf16)
        return carry

    lax.fori_loop(0, 3, project_values, 0)
    keep(qkv, qkv_o)

    def attend(p, carry):
        query = qkv[:, rows_of(p, LANES, LANES)]
        keys = qkv[:, rows_of(p + 6, LANES, LANES)]
        values = jnp.transpose(qkv[:, rows_of(p + 12, LANES, LANES)])
        for head in range(2):
            low_lanes = iota((1, LANES), 1) // HEAD == head
            masked = query * jnp.where(low_lanes, 0.125, 0.0).astype(bf16)
            for part in range(2):
                scores = mm_nt(keys, masked[part * 256 : part * 256 + 256, :])
                scores = scores + mask[:, part * 256 : part * 256 + 256]
                top = jnp.max(scores, axis=0, keepdims=True)
                expo = jnp.exp(scores - top)
                total = jnp.sum(expo, axis=0, keepdims=True)
                got = mm(values[head * HEAD : (head + 1) * HEAD, :], expo.astype(bf16))
                ctx_s[
                    pl.ds(pl.multiple_of(p * LANES + head * HEAD, HEAD), HEAD),
                    part * 256 : part * 256 + 256,
                ] = (got * (1.0 / total)).astype(bf16)
                lse_o[pl.ds(2 * p + head, 1), part * 256 : part * 256 + 256] = top + jnp.log(total)
        ctx[:, rows_of(p, LANES, LANES)] = jnp.transpose(ctx_s[rows_of(p, LANES, LANES), :])
        return carry

    up_a.hop_two()
    lax.fori_loop(0, 3, attend, 0)
    out_a.last()
    down_a.hop_one()
    lax.fori_loop(3, 6, attend, 0)
    lse_o[12:16, :] = jnp.zeros((4, BLOCK), f32)
    pair(ctx_s, ctx_t)
    up_a.last()
    down_a.hop_two()
    out_a.ready()
    keep(out_f, w_out)

    def attention_norm(c, carry):
        rows = rows_of(c, 128, 128)
        value = wide_s[rows, :] + mm(ctx[rows, :], out_f[...]) + vec_o[4:5, :]
        center = value - jnp.mean(value, axis=-1, keepdims=True)
        scale = spread_rows(center)
        hat = center * scale
        xh1[rows, :] = hat
        col_o[rows, 1:2] = scale
        value = hat * vec_o[5:6, :] + vec_o[6:7, :]
        first[rows, :] = value
        low[rows, :] = value.astype(bf16)
        return carry

    lax.fori_loop(0, 4, attention_norm, 0)
    keep(xh1, xh1_o)
    transpose_to(first_s, low)
    pair(first_s, first_t)
    up_a.ready()
    keep(up_f, w_up)

    def feed(i, carry):
        columns = rows_of(i, 256, 256)
        hidden = mm(low[...], up_f[:, columns]) + bias2_o[0:1, columns]
        part = 0.5 + 0.5 * lax.erf(hidden * (1.0 / math.sqrt(2.0)))
        value = (hidden * part).astype(bf16)
        act[:, columns] = value
        act_s[columns, :] = jnp.transpose(value)
        bell = jnp.exp(hidden * hidden * -0.5) * (1.0 / math.sqrt(2.0 * math.pi))
        dgelu[:, columns] = (part + hidden * bell).astype(bf16)
        return carry

    lax.fori_loop(0, 12, feed, 0)
    keep(dgelu, dgelu_o)
    pair(act_s, act_t)
    down_a.last()
    down_a.ready()
    keep(down_f, w_down)

    def second_part(i, carry):
        columns = rows_of(i, 256, 256)
        wide_s[:, columns] = mm(act[...], down_f[:, columns]) + vec_o[7:8, columns]
        return carry

    lax.fori_loop(0, 3, second_part, 0)

    def last_norm(c, carry):
        rows = rows_of(c, 128, 128)
        value = first[rows, :] + wide_s[rows, :]
        center = value - jnp.mean(value, axis=-1, keepdims=True)
        scale = spread_rows(center)
        hat = center * scale
        rows_s[rows, :] = (hat * vec_o[8:9, :] + vec_o[9:10, :]).astype(bf16)
        grad = widen(cot_ref[rows, :]) * col_o[rows, 3:4]
        gained = grad * vec_o[8:9, :]
        gp2[rows, :] = scale * (
            gained
            - jnp.mean(gained, axis=-1, keepdims=True)
            - hat * jnp.mean(gained * hat, axis=-1, keepdims=True)
        )
        gain, bias = carry
        return (
            gain + jnp.sum(grad * hat, axis=0, keepdims=True),
            bias + jnp.sum(grad, axis=0, keepdims=True),
        )

    zero = jnp.zeros((1, 768), f32)
    gain, bias = lax.fori_loop(0, 4, last_norm, (zero, zero))
    last_o[...] = jnp.concatenate([gain, bias, jnp.zeros((6, 768), f32)], axis=0)
    keep(gp2, gp2_o)
    keep(rows_s, rows_o)

    for a in arrays:
        a.drain()

    def text_drain(k, carry):
        text_copy(lax.rem(me + k, 16), me).wait_send()
        return carry

    lax.fori_loop(1, 16, text_drain, 0)

    def twin_drain(k, carry):
        text_twin(k, rep).wait_send()
        return carry

    lax.fori_loop(0, 16, twin_drain, 0)
    for copy in twins:
        copy.wait_send()
    for copy in paired:
        copy.wait_send()
        copy.wait_recv()
    for copy in kept:
        copy.wait()


def shape(*dims, dtype=f32):
    return jax.ShapeDtypeStruct(dims, dtype)


def forward_call(lens, feat, col, row, vec, cot, text, side, w_in, w_out, w_up, w_down, extra=None):
    dense = extra is not None
    vm, hbm = pl.BlockSpec(memory_space=pltpu.VMEM), pl.BlockSpec(memory_space=pl.ANY)
    sm = pl.BlockSpec(memory_space=pltpu.SMEM)
    full = [(16 * w.shape[0], w.shape[1]) for w in (side, w_in, w_out, w_up, w_down)]
    out_shape = (
        *(shape(*dims, dtype=bf16) for dims in full[1:]),
        shape(768, 1024, dtype=bf16), shape(768, 1024, dtype=bf16), shape(768, 1024, dtype=bf16),
        shape(3072, 1024, dtype=bf16),
        shape(BLOCK, 3072, dtype=bf16),
        shape(BLOCK, 768), shape(BLOCK, 768), shape(BLOCK, 768),
        shape(BLOCK, 2304, dtype=bf16), shape(BLOCK, 768, dtype=bf16),
        shape(BLOCK, LANES), shape(16, BLOCK), shape(16, 768), shape(8, 1536), shape(8, 3072),
        shape(8, 768), shape(8, BLOCK), shape(16, LANES), shape(8, 768),
        shape(8, BLOCK, dtype=jnp.int32),
    )
    v = lambda *dims, dtype=bf16: pltpu.VMEM(dims, dtype)
    dma = pltpu.SemaphoreType.DMA
    return pl.pallas_call(
        functools.partial(forward_kernel, dense),
        name="forward_dense" if dense else "forward",
        out_shape=out_shape,
        in_specs=[sm] + [vm] * 6 + [hbm] * 5 + [vm] * dense,
        out_specs=tuple([hbm] * 14 + [vm] * 10),
        scratch_shapes=[
            *(v(*dims) for dims in full),
            pltpu.VMEM((8, BLOCK), jnp.int32), v(16, LANES, dtype=f32), v(16, LANES, dtype=f32),
            v(16, 8, LANES, dtype=f32), v(16, 8, LANES, dtype=f32), v(8, LANES, dtype=f32),
            v(16, LANES, dtype=f32), v(2, 16, 16, LANES, dtype=f32),
            v(16 * CAP, 384), v(16 * CAP, 768), v(BLOCK, BLOCK, dtype=f32),
            v(BLOCK, 768), v(BLOCK, 768, dtype=f32), v(BLOCK, 2304), v(768, BLOCK), v(BLOCK, 768),
            v(BLOCK, 3072), v(3072, BLOCK), v(BLOCK, 3072), v(768, BLOCK), v(768, BLOCK),
            v(BLOCK, 768, dtype=f32), v(BLOCK, 768, dtype=f32), v(BLOCK, 768, dtype=f32),
            v(BLOCK, 768, dtype=f32), v(BLOCK, 768),
            dma((5,)), dma((5, 32)), dma((5, 16)), dma((5, 16)), dma((16,)), dma((16,)), dma((16,)), dma((16,)),
            dma((16,)), dma((16,)), dma((16,)), dma((16,)), dma((3,)), dma((3,)), dma((14,)), dma((4,)), dma((4,)),
        ],
        compiler_params=pltpu.CompilerParams(
            collective_id=2 if dense else 0, has_side_effects=True, vmem_limit_bytes=62 * 2**20
        ),
    )(lens, feat, col, row, vec, cot, text, side, w_in, w_out, w_up, w_down, *([extra] if dense else []))


def pack_indices(text_ids, boxes, segment_ids, vocab):
    owner = text_ids // vocab
    return jnp.stack(
        [
            text_ids, boxes[:, 0], boxes[:, 2], boxes[:, 1], boxes[:, 3], segment_ids,
            owner * vocab, owner,
        ],
        axis=1,
    )


def norm_rows(value, gain, shift):
    center = value - jnp.mean(value, axis=-1, keepdims=True)
    spread = lax.rsqrt(jnp.mean(center * center, axis=-1, keepdims=True) + epsilon)
    return center * spread * gain + shift


def gelu_exact(value):
    return jax.nn.gelu(value, approximate=False)


def block_scores(query, keys, member):
    query_heads = query.reshape(BLOCK, -1, HEAD)
    key_heads = keys.reshape(BLOCK, -1, HEAD)
    scores = (
        jnp.einsum("qhd,khd->hqk", query_heads, key_heads, preferred_element_type=jnp.float32)
        * 0.125
    )
    same = member[:, None] == member[None, :]
    return jnp.where(same[None], scores, -1e30)


def attend_forward(operands):
    query, keys, values, member = operands
    scores = block_scores(query, keys, member)
    top = jnp.max(scores, axis=-1, keepdims=True)
    expo = jnp.exp(scores - top)
    total = jnp.sum(expo, axis=-1, keepdims=True)
    probs_low = (expo / total).astype(jnp.bfloat16)
    context = jnp.einsum(
        "hqk,khd->qhd",
        probs_low,
        values.reshape(BLOCK, -1, HEAD),
        preferred_element_type=jnp.float32,
    )
    return (context.reshape(BLOCK, -1).astype(jnp.bfloat16), top + jnp.log(total))


def attend_backward(operands):
    query, keys, values, member, logsum, grad_context = operands
    scores = block_scores(query, keys, member)
    probs = jnp.exp(scores - logsum)
    probs_low = probs.astype(jnp.bfloat16)
    value_heads = values.reshape(BLOCK, -1, HEAD)
    grad_heads = grad_context.reshape(BLOCK, -1, HEAD)
    grad_values = jnp.einsum(
        "hqk,qhd->khd", probs_low, grad_heads, preferred_element_type=jnp.float32
    )
    grad_probs = jnp.einsum(
        "qhd,khd->hqk", grad_heads, value_heads, preferred_element_type=jnp.float32
    )
    delta = jnp.sum(grad_probs * probs, axis=-1, keepdims=True)
    grad_scores = (probs * (grad_probs - delta)).astype(jnp.bfloat16)
    grad_query = (
        jnp.einsum(
            "hqk,khd->qhd",
            grad_scores,
            keys.reshape(BLOCK, -1, HEAD),
            preferred_element_type=jnp.float32,
        )
        * 0.125
    )
    grad_keys = (
        jnp.einsum(
            "hqk,qhd->khd",
            grad_scores,
            query.reshape(BLOCK, -1, HEAD),
            preferred_element_type=jnp.float32,
        )
        * 0.125
    )
    joined = jnp.concatenate(
        [
            grad_query.reshape(BLOCK, -1),
            grad_keys.reshape(BLOCK, -1),
            grad_values.reshape(BLOCK, -1),
        ],
        axis=1,
    )
    return joined.astype(jnp.bfloat16)


def general(
    region_features,
    text_ids,
    boxes,
    segment_ids,
    document_lengths,
    cotangent,
    batch_gain,
    batch_bias,
    text_table,
    side_table,
    embed_gain,
    embed_bias,
    in_weight,
    in_bias,
    out_weight,
    out_bias,
    first_gain,
    first_bias,
    up_weight,
    up_bias,
    down_weight,
    down_bias,
    second_gain,
    second_bias,
):
    rows_here, width = region_features.shape
    blocks_here = document_lengths.shape[0]
    vocab_here = text_table.shape[0]
    ends = jnp.cumsum(document_lengths, axis=1)
    place = jnp.arange(BLOCK, dtype=jnp.int32)
    member = jnp.sum((place[None, :, None] >= ends[:, None, :]).astype(jnp.int32), axis=2)
    valid = (member < SLOTS).astype(jnp.float32).reshape(rows_here, 1)
    shards = lax.axis_size("shard")
    vectors = (
        batch_gain, batch_bias, embed_gain, embed_bias, in_bias, out_bias, first_gain, first_bias,
        up_bias, down_bias, second_gain, second_bias,
    )
    sizes = [v.shape[0] for v in vectors]
    marks = [sum(sizes[:k]) for k in range(len(sizes) + 1)]
    joined = lax.all_gather(jnp.concatenate(vectors), "shard", axis=0)
    (
        full_batch_gain,
        full_batch_bias,
        full_embed_gain,
        full_embed_bias,
        full_in_bias,
        full_out_bias,
        full_first_gain,
        full_first_bias,
        full_up_bias,
        full_down_bias,
        full_second_gain,
        full_second_bias,
    ) = [joined[:, low:high].reshape(-1) for low, high in zip(marks, marks[1:])]
    full_side, full_in_weight, full_out_weight, full_up_weight, full_down_weight = [
        lax.all_gather(w, "shard", axis=0, tiled=True)
        for w in (side_table, in_weight, out_weight, up_weight, down_weight)
    ]
    features = widen(region_features)
    masked = features * valid
    total, count = lax.psum((jnp.sum(masked, axis=0), jnp.sum(valid)), ("rep", "shard"))
    mean = total / count
    center = features - mean
    variance = lax.psum(jnp.sum(center * center * valid, axis=0), ("rep", "shard")) / count
    spread = lax.rsqrt(variance + epsilon)
    batch_hat = center * spread
    gain_wide = widen(full_batch_gain)
    batch_out = batch_hat * gain_wide + widen(full_batch_bias)
    piece = lax.all_gather(text_table, "shard", axis=0, tiled=True)
    add_column = jnp.arange(piece.shape[0], dtype=jnp.int32)
    onehot = (text_ids[:, None] == add_column[None, :]).astype(jnp.bfloat16)
    text_rows = jnp.dot(onehot, piece, preferred_element_type=jnp.float32)
    side_column = jnp.arange(SIDE, dtype=jnp.int32)
    hits = jnp.zeros((rows_here, SIDE), jnp.float32)
    for column in (
        boxes[:, 0],
        boxes[:, 2],
        boxes[:, 1] + BINS,
        boxes[:, 3] + BINS,
        segment_ids + 2 * BINS,
    ):
        hits = hits + (column[:, None] == side_column[None, :]).astype(jnp.float32)
    hits_low = hits.astype(jnp.bfloat16)
    looked = text_rows + jnp.dot(hits_low, full_side, preferred_element_type=jnp.float32)
    start_rows = batch_out + looked
    embedded, back_embed = jax.vjp(
        norm_rows, start_rows, widen(full_embed_gain), widen(full_embed_bias)
    )
    embedded_low = embedded.astype(jnp.bfloat16)
    mixed = jnp.dot(embedded_low, full_in_weight, preferred_element_type=jnp.float32)
    bias_wide = widen(full_in_bias)
    query = (mixed[:, :width] + bias_wide[:width]).astype(jnp.bfloat16)
    keys = mixed[:, width : 2 * width].astype(jnp.bfloat16)
    values = (mixed[:, 2 * width :] + bias_wide[width:]).astype(jnp.bfloat16)
    shaped = (
        query.reshape(blocks_here, BLOCK, width),
        keys.reshape(blocks_here, BLOCK, width),
        values.reshape(blocks_here, BLOCK, width),
    )
    context, logsum = lax.map(attend_forward, shaped + (member,))
    context = context.reshape(rows_here, width)
    branch = jnp.dot(context, full_out_weight, preferred_element_type=jnp.float32) + widen(
        full_out_bias
    )
    first, back_first = jax.vjp(
        norm_rows, embedded + branch, widen(full_first_gain), widen(full_first_bias)
    )
    first_low = first.astype(jnp.bfloat16)
    hidden = jnp.dot(first_low, full_up_weight, preferred_element_type=jnp.float32) + widen(
        full_up_bias
    )
    gelu_value, gelu_back = jax.vjp(gelu_exact, hidden)
    active = gelu_value.astype(jnp.bfloat16)
    second = jnp.dot(active, full_down_weight, preferred_element_type=jnp.float32) + widen(
        full_down_bias
    )
    final, back_second = jax.vjp(
        norm_rows, first + second, widen(full_second_gain), widen(full_second_bias)
    )
    out_rows = final.astype(jnp.bfloat16)
    grad_final = widen(cotangent) * valid
    grad_pre2, grad_second_gain, grad_second_bias = back_second(grad_final)
    grad_second = grad_pre2.astype(jnp.bfloat16)
    grad_down_weight = jnp.einsum(
        "rf,rd->fd", active, grad_second, preferred_element_type=jnp.float32
    )
    grad_down_bias = jnp.sum(widen(grad_second), axis=0)
    grad_active = jnp.einsum(
        "rd,fd->rf", grad_second, full_down_weight, preferred_element_type=jnp.float32
    )
    grad_hidden = gelu_back(grad_active)[0].astype(jnp.bfloat16)
    grad_up_weight = jnp.einsum(
        "rd,rf->df", first_low, grad_hidden, preferred_element_type=jnp.float32
    )
    grad_up_bias = jnp.sum(widen(grad_hidden), axis=0)
    grad_first = grad_pre2 + jnp.einsum(
        "rf,df->rd", grad_hidden, full_up_weight, preferred_element_type=jnp.float32
    )
    grad_pre1, grad_first_gain, grad_first_bias = back_first(grad_first)
    grad_branch = grad_pre1.astype(jnp.bfloat16)
    grad_out_weight = jnp.einsum(
        "rd,re->de", context, grad_branch, preferred_element_type=jnp.float32
    )
    grad_out_bias = jnp.sum(widen(grad_branch), axis=0)
    grad_context = jnp.einsum(
        "re,de->rd", grad_branch, full_out_weight, preferred_element_type=jnp.float32
    ).astype(jnp.bfloat16)
    grad_mixed = lax.map(
        attend_backward, shaped + (member, logsum, grad_context.reshape(blocks_here, BLOCK, width))
    )
    grad_mixed = grad_mixed.reshape(rows_here, 3 * width)
    grad_in_weight = jnp.einsum(
        "rd,re->de", embedded_low, grad_mixed, preferred_element_type=jnp.float32
    )
    column_sums = jnp.sum(widen(grad_mixed), axis=0)
    grad_in_bias = jnp.concatenate([column_sums[:width], column_sums[2 * width :]])
    grad_embedded = grad_pre1 + jnp.einsum(
        "re,de->rd", grad_mixed, full_in_weight, preferred_element_type=jnp.float32
    )
    grad_start, grad_embed_gain, grad_embed_bias = back_embed(grad_embedded)
    grad_looked = grad_start.astype(jnp.bfloat16)
    column = jnp.arange(lax.axis_size("shard") * vocab_here, dtype=jnp.int32)
    onehot = (column[:, None] == text_ids[None, :]).astype(jnp.bfloat16)
    text_grad = lax.psum_scatter(
        jnp.dot(onehot, grad_looked, preferred_element_type=jnp.float32),
        "shard",
        scatter_dimension=0,
        tiled=True,
    )
    grad_side = jnp.einsum("rs,rd->sd", hits_low, grad_looked, preferred_element_type=jnp.float32)
    shift_sum, scale_sum = lax.psum(
        (jnp.sum(grad_start * valid, axis=0), jnp.sum(grad_start * batch_hat * valid, axis=0)),
        ("rep", "shard"),
    )
    feature_grad = (
        valid
        * gain_wide
        * spread
        * (grad_start - shift_sum / count - batch_hat * scale_sum / count)
    ).astype(jnp.bfloat16)
    small = (
        scale_sum / lax.axis_size(("rep", "shard")),
        shift_sum / lax.axis_size(("rep", "shard")),
        grad_embed_gain, grad_embed_bias, grad_in_bias, grad_out_bias, grad_first_gain,
        grad_first_bias, grad_up_bias, grad_down_bias, grad_second_gain, grad_second_bias,
    )
    joined = jnp.concatenate([v.reshape(shards, -1) for v in small], axis=1).reshape(-1)
    owned = [
        lax.psum_scatter(value, "shard", scatter_dimension=0, tiled=True)
        for value in (
            grad_side, grad_in_weight, grad_out_weight, grad_up_weight, grad_down_weight, joined
        )
    ]
    side_grad, in_weight_grad, out_weight_grad, up_weight_grad, down_weight_grad = [
        widen(v) for v in lax.psum(tuple(v.astype(jnp.bfloat16) for v in owned[:5]), "rep")
    ]
    text_table_grad = widen(lax.psum(text_grad.astype(jnp.bfloat16), "rep"))
    pieces = lax.psum(owned[5], "rep")
    (
        batch_gain_grad,
        batch_bias_grad,
        embed_gain_grad,
        embed_bias_grad,
        in_bias_grad,
        out_bias_grad,
        first_gain_grad,
        first_bias_grad,
        up_bias_grad,
        down_bias_grad,
        second_gain_grad,
        second_bias_grad,
    ) = [pieces[low:high] for low, high in zip(marks, marks[1:])]
    return (
        out_rows,
        feature_grad,
        batch_gain_grad,
        batch_bias_grad,
        text_table_grad,
        side_grad,
        embed_gain_grad,
        embed_bias_grad,
        in_weight_grad,
        in_bias_grad,
        out_weight_grad,
        out_bias_grad,
        first_gain_grad,
        first_bias_grad,
        up_weight_grad,
        up_bias_grad,
        down_weight_grad,
        down_bias_grad,
        second_gain_grad,
        second_bias_grad,
    )


class Scatter:
    def __init__(self, index, total, near, relay, line, done, out, sems):
        self.index, self.total, self.near, self.relay, self.line = index, total, near, relay, line
        self.done, self.out = done, out
        self.send_sem, self.near_sem, self.relay_sem, self.line_sem, self.twin_sem, self.keep_sem = sems
        self.rep, self.z, self.y, self.x = spot()
        self.me = at(self.z, self.y, self.x)
        self.rows, self.half = near.shape[1], near.shape[2]

    def rows_at(self, source):
        return rows_of(source, self.rows, 16)

    def beside(self, plane, swap):
        even = lax.rem(plane + self.y + self.x + swap, 2) == 0
        return jnp.where(even, self.y, 1 - self.y), jnp.where(even, 1 - self.x, self.x)

    def copy(self, source, slot, target, dst, recv_sem):
        return pltpu.make_async_remote_copy(
            src_ref=self.total.at[self.rows_at(source)],
            dst_ref=dst,
            send_sem=self.send_sem.at[self.index, slot],
            recv_sem=recv_sem,
            device_id=(self.rep, target),
            device_id_type=MESH,
        )

    def near_copy(self, plane, kind):
        y, x = self.beside(plane, kind)
        target = at(self.z, y, x)
        source = at(plane, y, x) if kind == 0 else at(plane, 1 - self.y, 1 - self.x)
        slot = 2 * plane + kind
        return self.copy(
            source, slot, target, self.near.at[slot], self.near_sem.at[self.index, slot]
        )

    def relay_copy(self, plane):
        y, x = self.beside(plane, 1)
        return self.copy(
            at(plane, y, x), 8 + plane, at(self.z, y, x), self.relay.at[plane],
            self.relay_sem.at[self.index, plane],
        )

    def line_copy(self, plane):
        there = at(plane, self.y, self.x)
        return self.copy(
            there, 12 + plane, there, self.line.at[self.z], self.line_sem.at[self.index, self.z]
        )

    def line_wait(self, plane):
        self.copy(
            self.me, 12 + plane, self.me, self.line.at[plane], self.line_sem.at[self.index, plane]
        ).wait_recv()

    def hop_one(self):
        def step(k, carry):
            plane = lax.rem(self.z + k + 1, 4)
            self.near_copy(plane, 1).start()
            return carry

        lax.fori_loop(0, 4, step, 0)

        def again(k, carry):
            plane = lax.rem(self.z + k + 1, 4)
            self.near_copy(plane, 0).start()
            return carry

        lax.fori_loop(0, 4, again, 0)

    def hop_two(self):
        def step(k, carry):
            plane = lax.rem(self.z + k + 1, 4)
            self.near_copy(plane, 1).wait_recv()
            y, x = self.beside(plane, 1)
            rows = self.rows_at(at(plane, y, x))
            self.total[rows, :] = (
                widen(self.total[rows, :]) + widen(self.near[2 * plane + 1])
            ).astype(bf16)
            self.relay_copy(plane).start()
            return carry

        lax.fori_loop(0, 4, step, 0)

    def hop_three(self):
        def step(k, carry):
            plane = lax.rem(self.z + k + 1, 4)
            self.near_copy(plane, 0).wait_recv()
            self.relay_copy(plane).wait_recv()
            rows = self.rows_at(at(plane, self.y, self.x))
            self.total[rows, :] = (
                widen(self.total[rows, :]) + widen(self.near[2 * plane]) + widen(self.relay[plane])
            ).astype(bf16)

            @pl.when(k < 3)
            def _():
                self.line_copy(plane).start()

            return carry

        lax.fori_loop(0, 4, step, 0)

    def finals(self):
        columns = rows_of(self.rep, self.half, LANES)
        return (
            pltpu.make_async_copy(
                self.done, self.out.at[:, columns], self.keep_sem.at[self.index]
            ),
            pltpu.make_async_remote_copy(
                src_ref=self.done,
                dst_ref=self.out.at[:, columns],
                send_sem=self.send_sem.at[self.index, 16],
                recv_sem=self.twin_sem.at[self.index],
                device_id=(1 - self.rep, self.me),
                device_id_type=MESH,
            ),
        )

    def finish(self):
        rows = self.rows_at(self.me)
        self.done[...] = widen(self.total[rows, :])

        def add(k, carry):
            plane = lax.rem(self.z + k, 4)
            self.line_wait(plane)
            self.done[...] = self.done[...] + widen(self.line[plane])
            return carry

        lax.fori_loop(1, 4, add, 0)
        for copy in self.finals():
            copy.start()

    def drain(self):
        def step(k, carry):
            self.near_copy(k, 0).wait_send()
            self.near_copy(k, 1).wait_send()
            self.relay_copy(k).wait_send()

            @pl.when(k != self.z)
            def _():
                self.line_copy(k).wait_send()

            return carry

        lax.fori_loop(0, 4, step, 0)
        kept, twin = self.finals()
        kept.wait()
        twin.wait_send()
        twin.wait_recv()


def compress_vectors(narrow, middle, wide):
    shard_of = iota((16, 1), 0).astype(f32)
    owner, _ = remainder((1, 768), 1, 0, 48)
    stacked = jnp.concatenate(
        [jnp.where(owner == shard_of, narrow[k : k + 1, :], 0.0) for k in range(10)], axis=0
    ).astype(bf16)
    _, depth = remainder((768, 1), 0, 0, 48)
    _, want = remainder((1, 768), 1, 0, 48)
    spread = mm(stacked, onehot(depth == want))
    packed = sum(
        jnp.where(owner == k, spread[k * 16 : k * 16 + 16], 0.0) for k in range(10)
    )

    def piece(row, low, offset, size):
        total = size * 16
        holder, _ = remainder((1, total), 1, 0, size)
        _, place = remainder((total, 1), 0, 0, size)
        lane = iota((1, 256), 1).astype(f32) + (low - offset)
        return mm(jnp.where(holder == shard_of, row, 0.0).astype(bf16), onehot(place == lane))

    packed = packed + jnp.concatenate(
        [jnp.zeros((16, 384), f32), piece(middle, 384, 480, 96), jnp.zeros((16, 128), f32)], axis=1
    )
    return packed + jnp.concatenate(
        [jnp.zeros((16, 512), f32), piece(wide, 512, 576, 192)], axis=1
    )


def norm_back(grad, hat, scale, gain):
    gained = grad * gain
    return scale * (
        gained
        - jnp.mean(gained, axis=-1, keepdims=True)
        - hat * jnp.mean(gained * hat, axis=-1, keepdims=True)
    )


def backward_kernel(
    lens_ref, feat_ref, row_ref, twin_ref, cols_ref, lse_ref, vec_ref, last_ref, slot_ref, req_ref, stat_ref,
    w_in, w_out, w_up, w_down, emb_t, ctx_t, first_t, act_t, dgelu_h, xh0_h, xh1_h, gp2_h, qkv_h,
    feat_o, looked_o, text_o, side_o, in_o, out_o, up_o, down_o, vec_o,
    w_in_s, w_out_s, act_b, down_b, up_b, dgelu_b, ctx_s, first_s, xh1, grad, qkv,
    low, low_twin, hidden, hidden_twin, branch, branch_twin, gctx, mixed, mixed_twin,
    looked, looked_twin,
    down_g, up_g, out_g, in_g, side_g,
    down_n, up_n, out_n, in_n, side_n,
    down_r, up_r, out_r, in_r, side_r,
    down_l, up_l, out_l, in_l, side_l,
    down_d, up_d, out_d, in_d, side_d,
    text_u, text_twin, text_half, text_in, ask_s, mask, vectors, in_row, up_row,
    chip_out, chip_in, outbox, inbox, both,
    load_sem, act_sem, tile_sem, pair_send, pair_recv,
    send_sem, near_sem, relay_sem, line_sem, twin_sem, keep_sem,
    small_send, small_recv, text_ssem, text_rsem, text_keep,
):
    rep, z, y, x = spot()
    me = at(z, y, x)
    vocab = text_o.shape[0]
    barrier = greet()

    loads = {}

    def load(name, source, target):
        loads[name] = pltpu.make_async_copy(source, target, load_sem.at[len(loads)])
        loads[name].start()

    load("grad", gp2_h, grad)

    def act_copy(i):
        slot = lax.rem(i, 4)
        return pltpu.make_async_copy(
            act_t.at[rows_of(i, 256, 256)], act_b.at[slot], act_sem.at[slot]
        )

    def tile_of(i):
        return lax.rem(i + 6 * (1 - rep), 12)

    def tile_copies(i):
        slot = lax.rem(i, 4)
        tile = rows_of(tile_of(i), 256, 256)
        return (
            pltpu.make_async_copy(w_down.at[tile], down_b.at[slot], tile_sem.at[0, slot]),
            pltpu.make_async_copy(w_up.at[:, tile], up_b.at[slot], tile_sem.at[1, slot]),
            pltpu.make_async_copy(dgelu_h.at[:, tile], dgelu_b.at[slot], tile_sem.at[2, slot]),
        )

    for k in range(3):
        for copy in tile_copies(k):
            copy.start()
    for k in range(3):
        act_copy(k).start()

    sems = (send_sem, near_sem, relay_sem, line_sem, twin_sem, keep_sem)
    down_a = Scatter(0, down_g, down_n, down_r, down_l, down_d, down_o, sems)
    up_a = Scatter(1, up_g, up_n, up_r, up_l, up_d, up_o, sems)
    out_a = Scatter(2, out_g, out_n, out_r, out_l, out_d, out_o, sems)
    in_a = Scatter(3, in_g, in_n, in_r, in_l, in_d, in_o, sems)
    side_a = Scatter(4, side_g, side_n, side_r, side_l, side_d, side_o, sems)

    paired = []

    def pair(source, target):
        copy = pltpu.make_async_remote_copy(
            src_ref=source,
            dst_ref=target,
            send_sem=pair_send.at[len(paired)],
            recv_sem=pair_recv.at[len(paired)],
            device_id=(1 - rep, me),
            device_id_type=MESH,
        )
        paired.append(copy)
        copy.start()
        return copy

    def half_of(width, core):
        return rows_of(core, width // 2, LANES)

    own_columns = rows_of(rep, BLOCK, LANES)
    twin_columns = rows_of(1 - rep, BLOCK, LANES)

    same = members(lens_ref, (BLOCK, 1), 0) == members(lens_ref, (1, BLOCK), 1)
    mask[...] = jnp.where(same, 0.0, -1e30)
    vectors[...] = jnp.concatenate(
        [jnp.zeros((8, 768), f32), last_ref[0:2, :], jnp.zeros((6, 768), f32)], axis=0
    )

    loads["grad"].wait()

    def second(c, total):
        rows = rows_of(c, 128, 128)
        value = grad[rows, :].astype(bf16)
        low[rows, :] = value
        return total + jnp.sum(widen(value), axis=0, keepdims=True)

    zero = jnp.zeros((1, 768), f32)
    vectors[7:8, :] = lax.fori_loop(0, 4, second, zero)
    pl.semaphore_wait(barrier, 16)
    low_pair = pair(low.at[:, half_of(768, 1 - rep)], low_twin)

    def feed(i, carry):
        slot = lax.rem(i, 4)
        for copy in tile_copies(i):
            copy.wait()

        @pl.when(i < 9)
        def _():
            for copy in tile_copies(i + 3):
                copy.start()

        tile = rows_of(tile_of(i), 256, 256)
        value = (widen(dgelu_b[slot]) * mm_nt(low[...], down_b[slot])).astype(bf16)
        hidden[:, tile] = value
        up_row[0:1, tile] = jnp.sum(widen(value), axis=0, keepdims=True)
        grad[...] = grad[...] + mm_nt(value, up_b[slot])
        return carry

    lax.fori_loop(0, 3, feed, 0)
    low_pair.wait_recv()

    def down_step(i, carry):
        slot = lax.rem(i, 4)
        act_copy(i).wait()

        @pl.when(i < 9)
        def _():
            act_copy(i + 3).start()

        down_g[rows_of(i, 256, 256), :] = (
            mm(act_b[slot, :, own_columns], low[:, half_of(768, rep)])
            + mm(act_b[slot, :, twin_columns], low_twin[...])
        ).astype(bf16)
        return carry

    lax.fori_loop(0, 12, down_step, 0)
    down_a.hop_one()

    load("first", first_t, first_s)
    load("xh1", xh1_h, xh1)
    load("out", w_out, w_out_s)
    load("qkv", qkv_h, qkv)
    load("ctx", ctx_t, ctx_s)
    load("in", w_in, w_in_s)

    lax.fori_loop(3, 6, feed, 0)
    hidden_pair = pair(hidden.at[:, half_of(3072, 1 - rep)], hidden_twin)
    lax.fori_loop(6, 12, feed, 0)
    down_a.hop_two()
    loads["first"].wait()
    hidden_pair.wait_recv()

    def up_step(i, carry):
        tile = rows_of(i, 256, 256)
        own = pl.ds(pl.multiple_of(rep * 1536 + i * 256, 256), 256)
        up_g[:, tile] = (
            mm(first_s[:, own_columns], hidden[:, own])
            + mm(first_s[:, twin_columns], hidden_twin[:, tile])
        ).astype(bf16)
        return carry

    lax.fori_loop(0, 6, up_step, 0)
    load("emb", emb_t, first_s)
    up_a.hop_one()

    loads["xh1"].wait()

    def norm_one(c, carry):
        rows = rows_of(c, 128, 128)
        value, hat = grad[rows, :], xh1[rows, :]
        back = norm_back(value, hat, cols_ref[rows, 1:2], vec_ref[5:6, :])
        grad[rows, :] = back
        rounded = back.astype(bf16)
        branch[rows, :] = rounded
        gain, bias, out = carry
        return (
            gain + jnp.sum(value * hat, axis=0, keepdims=True),
            bias + jnp.sum(value, axis=0, keepdims=True),
            out + jnp.sum(widen(rounded), axis=0, keepdims=True),
        )

    gain, bias, out = lax.fori_loop(0, 4, norm_one, (zero, zero, zero))
    load("xh0", xh0_h, xh1)
    vectors[4:5, :] = out
    vectors[5:6, :] = gain
    vectors[6:7, :] = bias
    branch_pair = pair(branch.at[:, half_of(768, 1 - rep)], branch_twin)
    loads["out"].wait()

    def context_step(i, carry):
        tile = rows_of(i, 256, 256)
        gctx[:, tile] = mm_nt(branch[...], w_out_s[tile, :]).astype(bf16)
        return carry

    lax.fori_loop(0, 3, context_step, 0)
    down_a.hop_three()
    loads["ctx"].wait()
    branch_pair.wait_recv()

    def out_step(i, carry):
        rows = rows_of(i, 256, 256)
        out_g[rows, :] = (
            mm(ctx_s[rows, own_columns], branch[:, half_of(768, rep)])
            + mm(ctx_s[rows, twin_columns], branch_twin[...])
        ).astype(bf16)
        return carry

    lax.fori_loop(0, 3, out_step, 0)
    out_a.hop_one()
    up_a.hop_two()

    loads["qkv"].wait()

    def attend(p, carry):
        pair_lanes = rows_of(p, LANES, LANES)
        query = qkv[:, pair_lanes]
        keys = qkv[:, rows_of(p + 6, LANES, LANES)]
        values = qkv[:, rows_of(p + 12, LANES, LANES)]
        outer = gctx[:, pair_lanes]
        keys_t = jnp.transpose(keys)
        query_t, key_parts, value_parts = [], [], []
        for head in range(2):
            in_head = iota((1, LANES), 1) // HEAD == head
            masked = query * jnp.where(in_head, 0.125, 0.0).astype(bf16)
            outer_masked = outer * jnp.where(in_head, 1.0, 0.0).astype(bf16)
            key_part = jnp.zeros((BLOCK, LANES), f32)
            value_part = jnp.zeros((BLOCK, LANES), f32)
            columns = []
            for part in range(2):
                s = slice(part * 256, part * 256 + 256)
                scores = mm_nt(keys, masked[s, :]) + mask[:, s]
                probs = jnp.exp(scores - lse_ref[pl.ds(2 * p + head, 1), s])
                grads = mm_nt(values, outer_masked[s, :])
                delta = jnp.sum(probs * grads, axis=0, keepdims=True)
                inner = (probs * (grads - delta)).astype(bf16)
                value_part = value_part + mm(probs.astype(bf16), outer[s, :])
                key_part = key_part + mm(inner, query[s, :])
                columns.append(mm(keys_t[head * HEAD : (head + 1) * HEAD, :], inner))
            query_t.append(jnp.concatenate(columns, axis=1))
            key_parts.append(key_part)
            value_parts.append(value_part)
        first_head = iota((1, LANES), 1) < HEAD
        gathered = (jnp.concatenate(query_t, axis=0) * 0.125).astype(bf16)
        mixed[:, pair_lanes] = jnp.transpose(gathered)
        mixed[:, rows_of(p + 6, LANES, LANES)] = (
            jnp.where(first_head, key_parts[0], key_parts[1]) * 0.125
        ).astype(bf16)
        mixed[:, rows_of(p + 12, LANES, LANES)] = jnp.where(
            first_head, value_parts[0], value_parts[1]
        ).astype(bf16)
        return carry

    lax.fori_loop(0, 2, attend, 0)
    out_a.hop_two()
    down_a.finish()
    lax.fori_loop(2, 4, attend, 0)
    up_a.hop_three()
    lax.fori_loop(4, 6, attend, 0)
    out_a.hop_three()
    mixed_pair = pair(mixed.at[:, half_of(2304, 1 - rep)], mixed_twin)

    loads["in"].wait()

    def embed_step(i, carry):
        tile = rows_of(i, 256, 256)
        grad[:, tile] = grad[:, tile] + mm_nt(mixed[...], w_in_s[tile, :])
        return carry

    lax.fori_loop(0, 3, embed_step, 0)

    def bias_step(i, carry):
        tile = rows_of(i, 256, 256)
        in_row[0:1, tile] = jnp.sum(widen(mixed[:, tile]), axis=0, keepdims=True)
        return carry

    lax.fori_loop(0, 9, bias_step, 0)
    loads["emb"].wait()
    mixed_pair.wait_recv()

    def in_step(i, carry):
        tile = rows_of(i, 384, 128)
        own = pl.ds(pl.multiple_of(rep * 1152 + i * 384, 128), 384)
        in_g[:, tile] = (
            mm(first_s[:, own_columns], mixed[:, own])
            + mm(first_s[:, twin_columns], mixed_twin[:, tile])
        ).astype(bf16)
        return carry

    lax.fori_loop(0, 3, in_step, 0)
    in_a.hop_one()

    loads["xh0"].wait()

    def norm_zero(c, carry):
        rows = rows_of(c, 128, 128)
        value, hat = grad[rows, :], xh1[rows, :]
        back = norm_back(value, hat, cols_ref[rows, 0:1], vec_ref[2:3, :])
        grad[rows, :] = back
        looked[rows, :] = back.astype(bf16)
        gain, bias, scales, shifts = carry
        kept = back * cols_ref[rows, 3:4]
        batch_hat = (widen(feat_ref[rows, :]) - stat_ref[0:1, :]) * stat_ref[1:2, :]
        return (
            gain + jnp.sum(value * hat, axis=0, keepdims=True),
            bias + jnp.sum(value, axis=0, keepdims=True),
            scales + jnp.sum(kept * batch_hat, axis=0, keepdims=True),
            shifts + jnp.sum(kept, axis=0, keepdims=True),
        )

    gain, bias, scales, shifts = lax.fori_loop(0, 4, norm_zero, (zero, zero, zero, zero))
    looked_local = pltpu.make_async_copy(looked, looked_o, text_keep.at[0])
    looked_local.start()
    looked_pair = pair(looked.at[:, half_of(768, 1 - rep)], looked_twin)
    vectors[0:1, :] = scales
    vectors[1:2, :] = shifts
    vectors[2:3, :] = gain
    vectors[3:4, :] = bias
    packed = compress_vectors(
        vectors[...],
        jnp.concatenate([in_row[0:1, 0:768], in_row[0:1, 1536:2304]], axis=1),
        up_row[0:1, :],
    )
    chip_out[...] = jnp.concatenate([packed, scales, shifts, jnp.zeros((6, 768), f32)], axis=0)
    chip_pair = pair(chip_out, chip_in)

    def text_sum(i, carry):
        rows = rows_of(i, 256, 256)
        place = (iota((256, 1), 0) + i * 256).astype(f32)
        text_u[rows, :] = mm(onehot(slot_ref[0:1, :] == place), looked[...]).astype(bf16)
        return carry

    lax.fori_loop(0, 16 * CAP // 256, text_sum, 0)

    text_pair_in = pair(text_u.at[:, half_of(768, 1 - rep)], text_twin)
    chip_pair.wait_recv()
    chip_in[...] = chip_out[...] + chip_in[...]
    chip_half = chip_in[:, half_of(768, rep)]
    for t in range(16):
        for j in range(3):
            lanes = slice(j * LANES, (j + 1) * LANES)
            outbox[t, j : j + 1, :] = chip_half[t : t + 1, lanes]
            outbox[t, 3 + j : 4 + j, :] = chip_half[16:17, lanes]
            outbox[t, 6 + j : 7 + j, :] = chip_half[17:18, lanes]
        outbox[t, 9:16, :] = jnp.zeros((7, LANES), f32)
    exchange(outbox, inbox, small_send, small_recv, True)
    inbox[me] = outbox[me]
    text_pair_in.wait_recv()
    for c in range(4):
        rows = slice(c * 256, c * 256 + 256)
        text_half[rows, :] = (
            widen(text_u[rows, half_of(768, rep)]) + widen(text_twin[rows, :])
        ).astype(bf16)

    def text_copy(k, source):
        there = lax.rem(me + k, 16)
        return pltpu.make_async_remote_copy(
            src_ref=text_half.at[rows_of(there, CAP, 16)],
            dst_ref=text_in.at[rows_of(source, CAP, 16)],
            send_sem=text_ssem.at[k],
            recv_sem=text_rsem.at[source],
            device_id=(rep, there),
            device_id_type=MESH,
        )

    def text_start(k, carry):
        text_copy(k, me).start()
        return carry

    lax.fori_loop(1, 16, text_start, 0)
    text_in[rows_of(me, CAP, 16), :] = text_half[rows_of(me, CAP, 16), :]

    looked_pair.wait_recv()
    for tile in range(5):
        base = tile * 512
        kinds = (1, 2) if base < BINS else (3, 4) if base < 2 * BINS else (5,)
        place = iota((512, 1), 0) + base % BINS

        def counted(ref):
            return sum((ref[k : k + 1, :] == place).astype(f32) for k in kinds).astype(bf16)

        side_g[base : base + 512, :] = (
            mm(counted(row_ref), looked[:, half_of(768, rep)])
            + mm(counted(twin_ref), looked_twin[...])
        ).astype(bf16)
    side_a.hop_one()
    in_a.hop_two()
    up_a.finish()
    out_a.finish()

    _, want = remainder((1, 16 * CAP), 1, 0, CAP)
    sender, _ = remainder((1, 16 * CAP), 1, 0, CAP)
    pick = onehot(iota((LANES, 1), 0).astype(f32) == want)
    asked = req_ref[...] + 1.0
    coarse = jnp.floor(asked * (1.0 / 32.0))
    fine = asked - 32.0 * coarse
    place = 32.0 * mm(coarse.astype(bf16), pick) + mm(fine.astype(bf16), pick)
    ours = sender == iota((16, 1), 0).astype(f32)
    ask_s[0:1, :] = jnp.sum(jnp.where(ours, place, 0.0), axis=0, keepdims=True)

    side_a.hop_two()
    in_a.hop_three()

    def text_wait(k, carry):
        text_copy(k, lax.rem(me + k, 16)).wait_recv()
        return carry

    lax.fori_loop(1, 16, text_wait, 0)

    part = vocab // 2

    def text_step(i, carry):
        rows = rows_of(i, 96, 32)
        for k in range(2):
            place = (iota((96, 1), 0) + (i * 96 + 1 + k * part)).astype(f32)
            xh1[rows, k * 384 : k * 384 + 384] = mm(
                onehot(ask_s[0:1, :] == place), text_in[...]
            )
        return carry

    lax.fori_loop(0, part // 96, text_step, 0)
    text_local, text_pairs = [], []
    for k in range(2):
        source = xh1.at[0:part, k * 384 : k * 384 + 384]
        target = text_o.at[k * part : k * part + part, half_of(768, rep)]
        text_local.append(pltpu.make_async_copy(source, target, text_keep.at[2 + k]))
        text_local[k].start()
        text_pairs.append(pair(source, target))

    exchange(outbox, inbox, small_send, small_recv, False)
    both[rep] = sum(inbox[t] for t in range(16))
    both_pair = pair(both.at[rep], both.at[rep])
    both_pair.wait_recv()
    vec_o[...] = jnp.concatenate([both[0, 0:3, :], both[1, 0:3, :], jnp.zeros((2, LANES), f32)], axis=0)
    scale_row = jnp.concatenate(
        [both[j // 3, 3 + j % 3 : 4 + j % 3, :] for j in range(6)], axis=1
    )
    shift_row = jnp.concatenate(
        [both[j // 3, 6 + j % 3 : 7 + j % 3, :] for j in range(6)], axis=1
    )
    scale_row = scale_row / stat_ref[2:3, :]
    shift_row = shift_row / stat_ref[2:3, :]

    def feature(c, carry):
        rows = rows_of(c, 128, 128)
        batch_hat = (widen(feat_ref[rows, :]) - stat_ref[0:1, :]) * stat_ref[1:2, :]
        value = grad[rows, :] - shift_row - batch_hat * scale_row
        gctx[rows, :] = (
            cols_ref[rows, 3:4] * (vec_ref[0:1, :] * stat_ref[1:2, :]) * value
        ).astype(bf16)
        return carry

    lax.fori_loop(0, 4, feature, 0)
    feat_local = pltpu.make_async_copy(gctx, feat_o, text_keep.at[1])
    feat_local.start()
    side_a.hop_three()
    in_a.finish()
    side_a.finish()

    for a in (down_a, up_a, out_a, in_a, side_a):
        a.drain()

    def text_drain(k, carry):
        text_copy(k, me).wait_send()
        return carry

    lax.fori_loop(1, 16, text_drain, 0)
    for copy in paired:
        copy.wait_send()
    for k in range(2):
        text_pairs[k].wait_recv()
        text_local[k].wait()
    feat_local.wait()
    looked_local.wait()


def backward_call(lens, feat, row, made, vocab):
    (
        w_in, w_out, w_up, w_down, emb_t, ctx_t, first_t, act_t, dgelu, xh0, xh1, gp2, qkv, _,
        cols, lse, vec, _, _, last, slot, req, stat, twin,
    ) = made
    vm, hbm = pl.BlockSpec(memory_space=pltpu.VMEM), pl.BlockSpec(memory_space=pl.ANY)
    sm = pl.BlockSpec(memory_space=pltpu.SMEM)
    v = lambda *dims, dtype=bf16: pltpu.VMEM(dims, dtype)
    dma = pltpu.SemaphoreType.DMA
    parts = [(192, 384), (48, 1536), (48, 384), (48, 1152), (160, 384)]
    return pl.pallas_call(
        backward_kernel,
        name="backward",
        out_shape=(
            shape(BLOCK, 768, dtype=bf16), shape(BLOCK, 768, dtype=bf16), shape(vocab, 768), shape(160, 768), shape(48, 2304),
            shape(48, 768), shape(48, 3072), shape(192, 768), shape(8, LANES),
        ),
        in_specs=[sm] + [vm] * 10 + [hbm] * 13,
        out_specs=tuple([hbm] * 8 + [vm]),
        scratch_shapes=[
            v(768, 2304), v(768, 768), v(4, 256, 1024), v(4, 256, 768), v(4, 768, 256),
            v(4, BLOCK, 256), v(768, 1024), v(768, 1024),
            v(BLOCK, 768, dtype=f32), v(BLOCK, 768, dtype=f32),
            v(BLOCK, 2304),
            v(BLOCK, 768), v(BLOCK, 384), v(BLOCK, 3072), v(BLOCK, 1536), v(BLOCK, 768),
            v(BLOCK, 384), v(BLOCK, 768), v(BLOCK, 2304), v(BLOCK, 1152),
            v(BLOCK, 768), v(BLOCK, 384),
            *(v(16 * r, c) for r, c in parts),
            *(v(8, r, c) for r, c in parts),
            *(v(4, r, c) for r, c in parts),
            *(v(4, r, c) for r, c in parts),
            *(v(r, c, dtype=f32) for r, c in parts),
            v(16 * CAP, 768), v(16 * CAP, 384), v(16 * CAP, 384), v(16 * CAP, 384),
            v(8, 16 * CAP, dtype=f32), v(BLOCK, BLOCK, dtype=f32),
            v(16, 768, dtype=f32), v(8, 2304, dtype=f32), v(8, 3072, dtype=f32),
            v(24, 768, dtype=f32), v(24, 768, dtype=f32), v(16, 16, LANES, dtype=f32),
            v(16, 16, LANES, dtype=f32), v(2, 16, LANES, dtype=f32),
            dma((9,)), dma((4,)), dma((3, 4)), dma((10,)), dma((10,)),
            dma((5, 17)), dma((5, 8)), dma((5, 4)), dma((5, 4)), dma((5,)), dma((5,)),
            dma((16,)), dma((16,)), dma((16,)), dma((16,)), dma((4,)),
        ],
        compiler_params=pltpu.CompilerParams(
            collective_id=1, has_side_effects=True, vmem_limit_bytes=62 * 2**20
        ),
    )(
        lens, feat, row, twin, cols, lse, vec, last, slot, req, stat,
        w_in, w_out, w_up, w_down, emb_t, ctx_t, first_t, act_t, dgelu, xh0, xh1, gp2, qkv,
    )


def dense_rows(text_ids, text_table):
    shards, vocab = lax.axis_size("shard"), text_table.shape[0]
    ring = [(k, (k + 1) % shards) for k in range(shards)]
    local = jnp.arange(vocab, dtype=jnp.int32)

    def step(k, carry):
        piece, rows = carry
        owner = lax.rem(lax.axis_index("shard") + shards - k, shards)
        hit = (text_ids - owner * vocab)[:, None] == local[None, :]
        return lax.ppermute(piece, "shard", ring), rows + mm(hit.astype(bf16), piece)

    rows = jnp.zeros((text_ids.shape[0], text_table.shape[1]), f32)
    return lax.fori_loop(0, shards, step, (text_table, rows))[1].astype(bf16)


def dense_sums(text_ids, looked, vocab):
    shards = lax.axis_size("shard")
    ring = [(k, (k + 1) % shards) for k in range(shards)]
    local = jnp.arange(vocab, dtype=jnp.int32)

    def step(k, total):
        owner = lax.rem(lax.axis_index("shard") + 2 * shards - 1 - k, shards)
        hit = local[:, None] == (text_ids - owner * vocab)[None, :]
        return lax.ppermute(total, "shard", ring) + mm(hit.astype(bf16), looked)

    total = lax.fori_loop(0, shards, step, jnp.zeros((vocab, looked.shape[1]), f32))
    return total + lax.ppermute(total, "rep", [(0, 1), (1, 0)])


def once(condition, body, value):
    return lax.while_loop(
        lambda state: state[0],
        lambda state: (jnp.zeros((), bool), body(state[1])),
        (condition, value),
    )[1]


def fast(*args):
    (
        region_features, text_ids, boxes, segment_ids, document_lengths, cotangent,
        batch_gain, batch_bias, text_table, side_table, embed_gain, embed_bias,
        in_weight, in_bias, out_weight, out_bias, first_gain, first_bias,
        up_weight, up_bias, down_weight, down_bias, second_gain, second_bias,
    ) = args
    vocab = text_table.shape[0]
    col = pack_indices(text_ids, boxes, segment_ids, vocab)
    row = col.T
    vec = jnp.stack(
        [
            jnp.pad(widen(v), (0, 256 - v.shape[0]))
            for v in (
                batch_gain, batch_bias, embed_gain, embed_bias, out_bias, first_gain, first_bias,
                down_bias, second_gain, second_bias, in_bias, up_bias,
            )
        ]
    )
    operands = (
        document_lengths, region_features, col, row, vec, cotangent, text_table,
        side_table, in_weight, out_weight, up_weight, down_weight,
    )
    made = forward_call(*operands)
    crowded = made[-2][3, 0] > CAP
    made = once(
        crowded,
        lambda _: tuple(forward_call(*operands, dense_rows(text_ids, text_table))),
        tuple(made),
    )
    feature_grad, looked, g_text, g_side, g_in, g_out, g_up, g_down, pieces = backward_call(
        document_lengths, region_features, row, made, vocab
    )
    g_text = once(crowded, lambda total: total + dense_sums(text_ids, looked, vocab), g_text)
    pieces = pieces.reshape(-1)
    cut = lambda k: pieces[k * 48 : (k + 1) * 48]
    return (
        made[13], feature_grad, cut(0), cut(1), g_text, g_side, cut(2), cut(3), g_in,
        pieces[480:576], g_out, cut(4), cut(5), cut(6), g_up, pieces[576:768], g_down, cut(7),
        cut(8), cut(9),
    )


def fits(mesh):
    return dict(mesh.shape) == {"rep": 2, "shard": 16}


def solution(mesh):
    in_specs = (
        P(("rep", "shard"), None),
        P(("rep", "shard")),
        P(("rep", "shard"), None),
        P(("rep", "shard")),
        P(("rep", "shard"), None),
        P(("rep", "shard"), None),
        P("shard"),
        P("shard"),
        P("shard", None),
        P("shard", None),
        P("shard"),
        P("shard"),
        P("shard", None),
        P("shard"),
        P("shard", None),
        P("shard"),
        P("shard"),
        P("shard"),
        P("shard", None),
        P("shard"),
        P("shard", None),
        P("shard"),
        P("shard"),
        P("shard"),
    )
    out_specs = (
        P(("rep", "shard"), None),
        P(("rep", "shard"), None),
        P("shard"),
        P("shard"),
        P("shard", None),
        P("shard", None),
        P("shard"),
        P("shard"),
        P("shard", None),
        P("shard"),
        P("shard", None),
        P("shard"),
        P("shard"),
        P("shard"),
        P("shard", None),
        P("shard"),
        P("shard", None),
        P("shard"),
        P("shard"),
        P("shard"),
    )
    return jax.shard_map(
        fast if fits(mesh) else general, mesh=mesh, in_specs=in_specs, out_specs=out_specs, check_vma=False
    )
```

```python
import functools
import math

import jax
import jax.numpy as jnp
from jax import lax
from jax.experimental import pallas as pl
from jax.experimental.pallas import tpu as pltpu
from jax.sharding import PartitionSpec as P

HEAD = 64
BINS = 1024
SIDE = 2560
BLOCK = 512
SLOTS = 4
CAP = 64
LANES = 128
MESH = pl.DeviceIdType.MESH
f32 = jnp.float32
bf16 = jnp.bfloat16

epsilon = 1e-05


def widen(value):
    return value.astype(jnp.float32)


def mm(a, b):
    return jnp.dot(a, b, preferred_element_type=f32)


def mm_nt(a, b):
    return lax.dot_general(a, b, (((1,), (1,)), ((), ())), preferred_element_type=f32)


def iota(shape, dim):
    return lax.broadcasted_iota(jnp.int32, shape, dim)


def spot():
    shard = lax.axis_index("shard")
    return lax.axis_index("rep"), shard // 4, (shard // 2) % 2, shard % 2


def at(z, y, x):
    return z * 4 + y * 2 + x


def rows_of(start, size, step):
    return pl.ds(pl.multiple_of(start * size, step), size)


def each(low, high, body):
    def step(k, carry):
        body(k)
        return carry

    lax.fori_loop(low, high, step, 0)


class Gather:
    def __init__(self, index, shard_ref, full_ref, own_sem, send_sem, recv_sem, twin_sem):
        self.index, self.shard, self.full = index, shard_ref, full_ref
        self.own_sem, self.send_sem, self.recv_sem, self.twin_sem = own_sem, send_sem, recv_sem, twin_sem
        self.rep, self.z, self.y, self.x = spot()
        self.me = at(self.z, self.y, self.x)
        self.rows = shard_ref.shape[0]
        self.half = shard_ref.shape[1] // 2

    def block(self, source, half):
        return self.full.at[
            rows_of(source, self.rows, 16), rows_of(half, self.half, LANES)
        ]

    def copy(self, source, slot, target, src=None, twin=False):
        return pltpu.make_async_remote_copy(
            src_ref=self.block(source, self.rep) if src is None else src,
            dst_ref=self.block(source, self.rep),
            send_sem=self.send_sem.at[self.index, slot],
            recv_sem=(self.twin_sem if twin else self.recv_sem).at[self.index, source],
            device_id=target,
            device_id_type=MESH,
        )

    def own(self):
        return pltpu.make_async_copy(
            self.shard, self.full.at[rows_of(self.me, self.rows, 16)], self.own_sem.at[self.index]
        )

    def start_line(self):
        src = self.shard.at[:, rows_of(self.rep, self.half, LANES)]

        def step(k, carry):
            there = lax.rem(self.z + k, 4)
            self.copy(self.me, there, (self.rep, at(there, self.y, self.x)), src=src).start()
            return carry

        lax.fori_loop(1, 4, step, 0)

    def start_own(self):
        src = self.shard.at[:, rows_of(self.rep, self.half, LANES)]
        self.copy(self.me, 4 + self.z, self.beside(self.z, 0), src=src).start()
        self.copy(self.me, 8 + self.z, self.beside(self.z, 1), src=src).start()
        self.own().start()

    def to_twin(self, source):
        self.copy(source, 16 + source, (1 - self.rep, self.me), twin=True).start()

    def beside(self, plane, swap):
        even = lax.rem(plane + self.y + self.x + swap, 2) == 0
        return (
            self.rep,
            at(self.z, jnp.where(even, self.y, 1 - self.y), jnp.where(even, 1 - self.x, self.x)),
        )

    def one(self, k):
        plane = lax.rem(self.z + k, 4)
        source = at(plane, self.y, self.x)
        self.copy(source, 0, (self.rep, self.me)).wait_recv()
        self.copy(source, 4 + plane, self.beside(plane, 0)).start()
        self.copy(source, 8 + plane, self.beside(plane, 1)).start()
        self.to_twin(source)

    def two(self, k):
        plane = lax.rem(self.z + k, 4)
        even = lax.rem(plane + self.y + self.x, 2) == 0
        source = at(
            plane, jnp.where(even, 1 - self.y, self.y), jnp.where(even, self.x, 1 - self.x)
        )
        self.copy(source, 0, (self.rep, self.me)).wait_recv()
        self.copy(source, 12 + plane, self.beside(plane, 0)).start()
        self.to_twin(source)

    def three(self, k):
        plane = lax.rem(self.z + k, 4)
        even = lax.rem(plane + self.y + self.x, 2) == 0
        near = at(
            plane, jnp.where(even, self.y, 1 - self.y), jnp.where(even, 1 - self.x, self.x)
        )
        for source in (near, at(plane, 1 - self.y, 1 - self.x)):
            self.copy(source, 0, (self.rep, self.me)).wait_recv()
            self.to_twin(source)

    def hop_one(self):
        each(1, 4, self.one)

    def hop_two(self):
        each(0, 4, self.two)

    def last(self):
        each(0, 4, self.three)

    def ready(self):
        self.own().wait()

        def step(k, carry):
            source = lax.rem(self.me + k, 16)
            pltpu.make_async_remote_copy(
                src_ref=self.block(source, 1 - self.rep),
                dst_ref=self.block(source, 1 - self.rep),
                send_sem=self.send_sem.at[self.index, 0],
                recv_sem=self.twin_sem.at[self.index, source],
                device_id=(self.rep, self.me),
                device_id_type=MESH,
            ).wait_recv()
            return carry

        lax.fori_loop(1, 16, step, 0)

    def drain(self):
        def step(k, carry):
            @pl.when((k != self.z) & (k != 16 + self.me))
            def _():
                self.copy(self.me, k, (self.rep, self.me)).wait_send()

            return carry

        lax.fori_loop(0, 32, step, 0)


def exchange(outbox, inbox, send_sem, recv_sem, start):
    rep, me = lax.axis_index("rep"), lax.axis_index("shard")
    each = len(outbox.shape) == 3

    def copy(k, source):
        there = lax.rem(me + k, 16)
        return pltpu.make_async_remote_copy(
            src_ref=outbox.at[there] if each else outbox,
            dst_ref=inbox.at[source],
            send_sem=send_sem.at[k],
            recv_sem=recv_sem.at[source],
            device_id=(rep, there),
            device_id_type=MESH,
        )

    def begin(k, carry):
        copy(k, me).start()
        return carry

    def done(k, carry):
        sent = copy(k, lax.rem(me + k, 16))
        sent.wait_send()
        sent.wait_recv()
        return carry

    lax.fori_loop(1, 16, begin if start else done, 0)


def greet():
    barrier = pltpu.get_barrier_semaphore()
    rep, me = lax.axis_index("rep"), lax.axis_index("shard")

    def step(k, carry):
        pl.semaphore_signal(
            barrier, inc=1, device_id=(rep, lax.rem(me + k, 16)), device_id_type=MESH
        )
        return carry

    lax.fori_loop(1, 16, step, 0)
    pl.semaphore_signal(barrier, inc=1, device_id=(1 - rep, me), device_id_type=MESH)
    return barrier


def members(lens_ref, shape, dim):
    place = iota(shape, dim)
    end = jnp.int32(0)
    member = jnp.zeros(shape, jnp.int32)
    for slot in range(SLOTS):
        end = end + lens_ref[0, slot]
        member = member + (place >= end).astype(jnp.int32)
    return member


def spread_rows(value):
    return lax.rsqrt(jnp.mean(value * value, axis=-1, keepdims=True) + epsilon)


def onehot(condition):
    return jnp.where(condition, 1.0, 0.0).astype(bf16)


def remainder(shape, dim, offset, size):
    place = iota(shape, dim).astype(f32) - offset
    group = jnp.floor((place + 0.5) * (1.0 / size))
    return group, place - group * size


def expand_vectors(packed):
    def select(low, width, offset, size):
        _, want = remainder((1, size * 16), 1, 0, size)
        depth = iota((width, 1), 0).astype(f32) + (low - offset)
        return onehot(depth == want)

    kinds, _ = remainder((1, 768), 1, 0, 48)
    stacked = jnp.concatenate(
        [jnp.where(kinds == k, packed, 0.0) for k in range(10)], axis=0
    ).astype(bf16)
    _, depth = remainder((768, 1), 0, 0, 48)
    _, want = remainder((1, 768), 1, 0, 48)
    spread = mm(stacked, onehot(depth == want))
    owner, _ = remainder((1, 768), 1, 0, 48)
    shard_of = iota((16, 1), 0).astype(f32)
    narrow = jnp.concatenate(
        [
            jnp.sum(jnp.where(owner == shard_of, spread[k * 16 : k * 16 + 16], 0.0), axis=0, keepdims=True)
            for k in range(10)
        ],
        axis=0,
    )
    low = packed.astype(bf16)
    owner, _ = remainder((1, 1536), 1, 0, 96)
    middle = mm(low[:, 384:640], select(384, 256, 480, 96))
    middle = jnp.sum(jnp.where(owner == shard_of, middle, 0.0), axis=0, keepdims=True)
    owner, _ = remainder((1, 3072), 1, 0, 192)
    wide = mm(low[:, 512:768], select(512, 256, 576, 192))
    wide = jnp.sum(jnp.where(owner == shard_of, wide, 0.0), axis=0, keepdims=True)
    return narrow, middle, wide


def transpose_to(target, source):
    for j in range(source.shape[1] // LANES):
        target[j * LANES : (j + 1) * LANES, :] = jnp.transpose(
            source[:, j * LANES : (j + 1) * LANES]
        )


def forward_kernel(
    dense, lens_ref, feat_ref, col_ref, row_ref, *rest,
):
    vec_refs, rest = rest[:12], rest[12:]
    cot_ref, text_ref, side_sh, in_sh, out_sh, up_sh, down_sh, *rest = rest
    extra_ref = rest[0] if dense else None
    forward_body(
        dense, extra_ref, lens_ref, feat_ref, col_ref, row_ref, vec_refs, cot_ref, text_ref,
        side_sh, in_sh, out_sh, up_sh, down_sh, *rest[1 if dense else 0 :],
    )


def forward_body(
    dense, extra_ref, lens_ref, feat_ref, col_ref, row_ref, vec_refs, cot_ref, text_ref,
    side_sh, in_sh, out_sh, up_sh, down_sh,
    w_in, w_out, w_up, w_down, emb_t, ctx_t, first_t, act_t,
    dgelu_o, xh0_o, xh1_o, gp2_o, qkv_o, rows_o,
    col_o, lse_o, vec_o, bias1_o, bias2_o, last_o, slot_o, req_o, stat_o, row_o,
    side_f, in_f, out_f, up_f, down_f,
    row_twin, stat_out, stat_twin, ask_out, ask_in, vec_s, outbox, inbox,
    text_send, text_recv, mask,
    low, wide_s, qkv, ctx_s, ctx, act, act_s, dgelu, emb_s, first_s, xh0, xh1, first, gp2, rows_s,
    own_sem, send_sem, recv_sem, twin_sem, ask_send, ask_recv, small_send, small_recv,
    text_ssem, text_rsem, text_tsend, text_trecv, two_send, two_recv,
    keep_sem, pair_send, pair_recv,
):
    rep, z, y, x = spot()
    me = at(z, y, x)
    vocab = text_ref.shape[0]
    barrier = greet()

    side_a, in_a, out_a, up_a, down_a = arrays = [
        Gather(i, sh, full, own_sem, send_sem, recv_sem, twin_sem)
        for i, (sh, full) in enumerate(
            ((side_sh, side_f), (in_sh, in_f), (out_sh, out_f), (up_sh, up_f), (down_sh, down_f))
        )
    ]

    kept = []

    def keep(source, target):
        copy = pltpu.make_async_copy(source, target, keep_sem.at[len(kept)])
        kept.append(copy)
        copy.start()

    paired = []

    def pair(source, target):
        columns = target.at[:, rows_of(rep, BLOCK, LANES)]
        keep(source, columns)
        copy = pltpu.make_async_remote_copy(
            src_ref=source,
            dst_ref=columns,
            send_sem=pair_send.at[len(paired)],
            recv_sem=pair_recv.at[len(paired)],
            device_id=(1 - rep, me),
            device_id_type=MESH,
        )
        paired.append(copy)
        copy.start()

    twins = []

    def to_twin(source, target):
        copy = pltpu.make_async_remote_copy(
            src_ref=source,
            dst_ref=target,
            send_sem=two_send.at[len(twins)],
            recv_sem=two_recv.at[len(twins)],
            device_id=(1 - rep, me),
            device_id_type=MESH,
        )
        twins.append(copy)
        copy.start()
        return copy

    valid = (members(lens_ref, (BLOCK, 1), 0) < SLOTS).astype(f32)
    count = jnp.sum(valid, axis=0, keepdims=True)
    col_o[:, 3:4] = valid

    def add_total(c, total):
        rows = rows_of(c, 64, 64)
        return total + jnp.sum(widen(feat_ref[rows, :]) * col_o[rows, 3:4], axis=0, keepdims=True)

    local = lax.fori_loop(0, 8, add_total, jnp.zeros((1, 768), f32)) / jnp.maximum(count, 1.0)

    def add_square(c, square):
        rows = rows_of(c, 64, 64)
        center = widen(feat_ref[rows, :]) - local
        return square + jnp.sum(center * center * col_o[rows, 3:4], axis=0, keepdims=True)

    square = lax.fori_loop(0, 8, add_square, jnp.zeros((1, 768), f32))

    for j in range(6):
        stat_out[j : j + 1, :] = local[:, j * LANES : (j + 1) * LANES]
        stat_out[6 + j : 7 + j, :] = square[:, j * LANES : (j + 1) * LANES]
    stat_out[12:16, :] = jnp.broadcast_to(count, (4, LANES))
    pl.semaphore_wait(barrier, 16)
    row_pair = to_twin(row_ref, row_twin)
    stat_pair = to_twin(stat_out, stat_twin)

    side_a.start_own()
    side_a.start_line()
    in_a.start_own()
    in_a.start_line()
    limit = 0 if dense else CAP
    row_pair.wait_recv()
    row_o[...] = row_twin[...]
    twin_columns = jnp.transpose(
        jnp.concatenate([widen(row_twin[...]), jnp.zeros((LANES - 8, BLOCK), f32)], axis=0)
    )
    all_c = jnp.concatenate([widen(col_ref[...]), twin_columns[:, 0:8]], axis=0)
    ids_c, base_c, owner_c = all_c[:, 0:1], all_c[:, 6:7], all_c[:, 7:8]
    ids_r = widen(jnp.concatenate([row_ref[0:1, :], row_twin[0:1, :]], axis=1))
    earlier = iota((2 * BLOCK, 1), 0) < iota((1, 2 * BLOCK), 1)
    first_r = 1.0 - jnp.max(
        jnp.where(earlier & (ids_c == ids_r), 1.0, 0.0), axis=0, keepdims=True
    )
    rank_c = jnp.sum(
        jnp.where((ids_r < ids_c) & (ids_r >= base_c), first_r, 0.0), axis=1, keepdims=True
    )
    most = jnp.max(rank_c, axis=0, keepdims=True) + 1.0
    slot_c = jnp.where(rank_c < limit, owner_c * CAP + rank_c, -1.0)
    col_o[:, 2:3] = slot_c[0:BLOCK]
    slot_o[...] = jnp.transpose(jnp.broadcast_to(slot_c[0:BLOCK], (BLOCK, LANES)))[0:8, :]
    within = ids_c - base_c
    lane = iota((1, LANES), 1).astype(f32)
    for t in range(16):
        hit = jnp.where((owner_c == t) & (rank_c < limit), rank_c, -1.0) == lane
        ask = jnp.max(jnp.where(hit, within, -1.0), axis=0, keepdims=True)
        ask_out[t] = jnp.broadcast_to(ask, (8, LANES))
    exchange(ask_out, ask_in, ask_send, ask_recv, True)
    ask_in[me] = ask_out[me]

    pieces = jnp.concatenate([widen(v[...]) for v in vec_refs], axis=1)
    for j in range(6):
        vec_s[j : j + 1, :] = pieces[:, j * LANES : (j + 1) * LANES]
    stat_pair.wait_recv()
    count_one, count_two = stat_out[12:13, :], stat_twin[12:13, :]
    both = jnp.maximum(count_one + count_two, 1.0)
    part = pl.ds(rep * 3, 3)
    part_two = pl.ds(6 + rep * 3, 3)
    mean_one, mean_two = stat_out[part, :], stat_twin[part, :]
    mean = (mean_one * count_one + mean_two * count_two) / both
    outbox[0:3, :] = mean
    outbox[3:6, :] = (
        stat_out[part_two, :]
        + stat_twin[part_two, :]
        + count_one * (mean_one - mean) * (mean_one - mean)
        + count_two * (mean_two - mean) * (mean_two - mean)
    )
    outbox[6:7, :] = jnp.where(lane == 1.0, most, count_one + count_two)
    outbox[7:10, :] = vec_s[part, :]
    outbox[10:16, :] = jnp.zeros((6, LANES), f32)
    exchange(outbox, inbox.at[rep], small_send, small_recv, True)
    inbox[rep, me] = outbox[...]
    out_a.start_own()
    up_a.start_own()
    down_a.start_own()
    same = members(lens_ref, (BLOCK, 1), 0) == members(lens_ref, (1, BLOCK), 1)
    mask[...] = jnp.where(same, 0.0, -1e30)

    side_a.hop_one()
    exchange(ask_out, ask_in, ask_send, ask_recv, False)

    asked = jnp.concatenate([ask_in[t, 0:1, :] for t in range(16)], axis=0)
    req_o[...] = asked
    asked = jnp.concatenate([asked, jnp.full((LANES - 16, LANES), -1.0, f32)], axis=0)
    asked = jnp.transpose(asked)
    column = iota((1, vocab), 1).astype(f32)
    half = rows_of(rep, 384, LANES)
    for c in range(4):
        pick = jnp.concatenate(
            [onehot(asked[:CAP, t : t + 1] == column) for t in range(4 * c, 4 * c + 4)], axis=0
        )
        text_send[c * 256 : c * 256 + 256, :] = mm(pick, text_ref[:, half]).astype(bf16)

    def text_copy(t, source):
        return pltpu.make_async_remote_copy(
            src_ref=text_send.at[rows_of(t, CAP, 16)],
            dst_ref=text_recv.at[rows_of(source, CAP, 16), half],
            send_sem=text_ssem.at[t],
            recv_sem=text_rsem.at[source],
            device_id=(rep, t),
            device_id_type=MESH,
        )

    def text_twin(source, core):
        block = text_recv.at[rows_of(source, CAP, 16), rows_of(core, 384, LANES)]
        return pltpu.make_async_remote_copy(
            src_ref=block,
            dst_ref=block,
            send_sem=text_tsend.at[source],
            recv_sem=text_trecv.at[source],
            device_id=(1 - rep, me),
            device_id_type=MESH,
        )

    def text_start(k, carry):
        text_copy(lax.rem(me + k, 16), me).start()
        return carry

    lax.fori_loop(1, 16, text_start, 0)
    out_a.start_line()
    up_a.start_line()
    text_recv[rows_of(me, CAP, 16), half] = text_send[rows_of(me, CAP, 16), :]
    text_twin(me, rep).start()

    exchange(outbox, inbox.at[rep], small_send, small_recv, False)
    to_twin(inbox.at[rep], inbox.at[rep]).wait_recv()

    def gathered(j):
        return jnp.concatenate([inbox[0, t, j : j + 1, :] for t in range(16)], axis=0)

    def gathered_half(core, j):
        return jnp.concatenate([inbox[core, t, j : j + 1, :] for t in range(16)], axis=0)

    tail = gathered(6)
    counts = tail[:, 0:1]
    all_rows = jnp.sum(counts, axis=0, keepdims=True)
    means, spreads = [], []
    for j in range(6):
        part = gathered_half(j // 3, j % 3)
        mean = jnp.sum(part * counts, axis=0, keepdims=True) / all_rows
        shift = part - mean
        variance = (
            jnp.sum(gathered_half(j // 3, 3 + j % 3) + counts * shift * shift, axis=0, keepdims=True)
            / all_rows
        )
        means.append(mean)
        spreads.append(lax.rsqrt(variance + epsilon))
    mean = jnp.concatenate(means, axis=1)
    spread = jnp.concatenate(spreads, axis=1)
    most = jnp.max(tail[:, 1:2], axis=0, keepdims=True)
    stat_o[...] = jnp.concatenate(
        [
            mean,
            spread,
            jnp.broadcast_to(all_rows, (1, 768)),
            jnp.broadcast_to(most, (1, 768)),
            jnp.zeros((4, 768), f32),
        ],
        axis=0,
    )
    packed = jnp.concatenate([gathered_half(j // 3, 7 + j % 3) for j in range(6)], axis=1)
    narrow, middle, wide = expand_vectors(packed)
    vec_o[...] = jnp.concatenate([narrow, jnp.zeros((6, 768), f32)], axis=0)
    bias1_o[...] = jnp.broadcast_to(middle, (8, 1536))
    bias2_o[...] = jnp.broadcast_to(wide, (8, 3072))


    side_a.hop_two()
    in_a.hop_one()
    side_a.last()
    side_a.ready()
    def embed(c, carry):
        rows = rows_of(c, 128, 128)
        hat = (widen(feat_ref[rows, :]) - stat_o[0:1, :]) * stat_o[1:2, :]
        begin = hat * vec_o[0:1, :] + vec_o[1:2, :]
        where = col_ref[rows, :]
        bins = iota((1, BINS), 1)
        hits = (where[:, 1:2] == bins).astype(f32) + (where[:, 2:3] == bins).astype(f32)
        begin = begin + mm(hits.astype(bf16), side_f[0:BINS, :])
        hits = (where[:, 3:4] == bins).astype(f32) + (where[:, 4:5] == bins).astype(f32)
        begin = begin + mm(hits.astype(bf16), side_f[BINS : 2 * BINS, :])
        segments = iota((1, SIDE - 2 * BINS), 1)
        begin = begin + mm(onehot(where[:, 5:6] == segments), side_f[2 * BINS :, :])
        if dense:
            begin = begin + widen(extra_ref[rows, :])
        wide_s[rows, :] = begin
        return carry

    lax.fori_loop(0, 4, embed, 0)

    in_a.hop_two()
    out_a.hop_one()
    in_a.last()
    def text_wait(k, carry):
        there = lax.rem(me + k, 16)
        text_copy(there, there).wait_recv()
        text_twin(there, rep).start()
        return carry

    lax.fori_loop(1, 16, text_wait, 0)

    def text_ready(k, carry):
        text_twin(k, 1 - rep).wait_recv()
        return carry

    lax.fori_loop(0, 16, text_ready, 0)

    down_a.start_line()
    def embed_norm(c, carry):
        rows = rows_of(c, 128, 128)
        slots = iota((1, 16 * CAP), 1).astype(f32)
        begin = wide_s[rows, :] + mm(onehot(col_o[rows, 2:3] == slots), text_recv[...])
        center = begin - jnp.mean(begin, axis=-1, keepdims=True)
        scale = spread_rows(center)
        hat = center * scale
        xh0[rows, :] = hat
        col_o[rows, 0:1] = scale
        value = hat * vec_o[2:3, :] + vec_o[3:4, :]
        wide_s[rows, :] = value
        low[rows, :] = value.astype(bf16)
        return carry

    lax.fori_loop(0, 4, embed_norm, 0)
    keep(xh0, xh0_o)
    transpose_to(emb_s, low)
    pair(emb_s, emb_t)
    out_a.hop_two()
    up_a.hop_one()
    in_a.ready()
    keep(in_f, w_in)

    def project(i, carry):
        columns = rows_of(i, 256, 256)
        qkv[:, columns] = mm(low[...], in_f[:, columns]).astype(bf16)
        return carry

    def project_biased(i, carry):
        columns = rows_of(i, 256, 256)
        source = rows_of(lax.rem(i, 6), 256, 256)
        qkv[:, columns] = (mm(low[...], in_f[:, columns]) + bias1_o[0:1, source]).astype(bf16)
        return carry

    lax.fori_loop(0, 3, project_biased, 0)
    lax.fori_loop(3, 6, project, 0)

    def project_values(i, carry):
        columns = rows_of(i + 6, 256, 256)
        source = rows_of(i + 3, 256, 256)
        qkv[:, columns] = (mm(low[...], in_f[:, columns]) + bias1_o[0:1, source]).astype(bf16)
        return carry

    lax.fori_loop(0, 3, project_values, 0)
    keep(qkv, qkv_o)

    def attend(p, carry):
        query = qkv[:, rows_of(p, LANES, LANES)]
        keys = qkv[:, rows_of(p + 6, LANES, LANES)]
        values = jnp.transpose(qkv[:, rows_of(p + 12, LANES, LANES)])
        for head in range(2):
            low_lanes = iota((1, LANES), 1) // HEAD == head
            masked = query * jnp.where(low_lanes, 0.125, 0.0).astype(bf16)
            for part in range(2):
                scores = mm_nt(keys, masked[part * 256 : part * 256 + 256, :])
                scores = scores + mask[:, part * 256 : part * 256 + 256]
                top = jnp.max(scores, axis=0, keepdims=True)
                expo = jnp.exp(scores - top)
                total = jnp.sum(expo, axis=0, keepdims=True)
                got = mm(values[head * HEAD : (head + 1) * HEAD, :], expo.astype(bf16))
                ctx_s[
                    pl.ds(pl.multiple_of(p * LANES + head * HEAD, HEAD), HEAD),
                    part * 256 : part * 256 + 256,
                ] = (got * (1.0 / total)).astype(bf16)
                lse_o[pl.ds(2 * p + head, 1), part * 256 : part * 256 + 256] = top + jnp.log(total)
        ctx[:, rows_of(p, LANES, LANES)] = jnp.transpose(ctx_s[rows_of(p, LANES, LANES), :])

        @pl.when(p < 4)
        def _():
            up_a.two(p)

        @pl.when(p >= 2)
        def _():
            @pl.when(p < 5)
            def _():
                down_a.one(p - 1)

        return carry

    lax.fori_loop(0, 6, attend, 0)
    lse_o[12:16, :] = jnp.zeros((4, BLOCK), f32)
    pair(ctx_s, ctx_t)
    out_a.last()
    out_a.ready()
    keep(out_f, w_out)

    def attention_norm(c, carry):
        rows = rows_of(c, 128, 128)
        value = wide_s[rows, :] + mm(ctx[rows, :], out_f[...]) + vec_o[4:5, :]
        center = value - jnp.mean(value, axis=-1, keepdims=True)
        scale = spread_rows(center)
        hat = center * scale
        xh1[rows, :] = hat
        col_o[rows, 1:2] = scale
        value = hat * vec_o[5:6, :] + vec_o[6:7, :]
        first[rows, :] = value
        low[rows, :] = value.astype(bf16)
        up_a.three(c)
        return carry

    lax.fori_loop(0, 4, attention_norm, 0)
    keep(xh1, xh1_o)
    transpose_to(first_s, low)
    pair(first_s, first_t)
    up_a.ready()
    keep(up_f, w_up)

    def feed(i, carry):
        columns = rows_of(i, 256, 256)
        hidden = mm(low[...], up_f[:, columns]) + bias2_o[0:1, columns]
        part = 0.5 + 0.5 * lax.erf(hidden * (1.0 / math.sqrt(2.0)))
        value = (hidden * part).astype(bf16)
        act[:, columns] = value
        act_s[columns, :] = jnp.transpose(value)
        bell = jnp.exp(hidden * hidden * -0.5) * (1.0 / math.sqrt(2.0 * math.pi))
        dgelu[:, columns] = (part + hidden * bell).astype(bf16)

        @pl.when(lax.rem(i, 3) == 2)
        def _():
            down_a.two(i // 3)

        return carry

    lax.fori_loop(0, 12, feed, 0)
    keep(dgelu, dgelu_o)
    pair(act_s, act_t)
    down_a.last()
    down_a.ready()
    keep(down_f, w_down)

    def second_part(i, carry):
        columns = rows_of(i, 256, 256)
        wide_s[:, columns] = mm(act[...], down_f[:, columns]) + vec_o[7:8, columns]
        return carry

    lax.fori_loop(0, 3, second_part, 0)

    def last_norm(c, carry):
        rows = rows_of(c, 128, 128)
        value = first[rows, :] + wide_s[rows, :]
        center = value - jnp.mean(value, axis=-1, keepdims=True)
        scale = spread_rows(center)
        hat = center * scale
        rows_s[rows, :] = (hat * vec_o[8:9, :] + vec_o[9:10, :]).astype(bf16)
        grad = widen(cot_ref[rows, :]) * col_o[rows, 3:4]
        gained = grad * vec_o[8:9, :]
        gp2[rows, :] = scale * (
            gained
            - jnp.mean(gained, axis=-1, keepdims=True)
            - hat * jnp.mean(gained * hat, axis=-1, keepdims=True)
        )
        gain, bias = carry
        return (
            gain + jnp.sum(grad * hat, axis=0, keepdims=True),
            bias + jnp.sum(grad, axis=0, keepdims=True),
        )

    zero = jnp.zeros((1, 768), f32)
    gain, bias = lax.fori_loop(0, 4, last_norm, (zero, zero))
    last_o[...] = jnp.concatenate([gain, bias, jnp.zeros((6, 768), f32)], axis=0)
    keep(gp2, gp2_o)
    keep(rows_s, rows_o)

    for a in arrays:
        a.drain()

    def text_drain(k, carry):
        text_copy(lax.rem(me + k, 16), me).wait_send()
        return carry

    lax.fori_loop(1, 16, text_drain, 0)

    def twin_drain(k, carry):
        text_twin(k, rep).wait_send()
        return carry

    lax.fori_loop(0, 16, twin_drain, 0)
    for copy in twins:
        copy.wait_send()
    for copy in paired:
        copy.wait_send()
        copy.wait_recv()
    for copy in kept:
        copy.wait()


def shape(*dims, dtype=f32):
    return jax.ShapeDtypeStruct(dims, dtype)


def forward_call(lens, feat, col, row, vec, cot, text, side, w_in, w_out, w_up, w_down, extra=None):
    dense = extra is not None
    vm, hbm = pl.BlockSpec(memory_space=pltpu.VMEM), pl.BlockSpec(memory_space=pl.ANY)
    sm = pl.BlockSpec(memory_space=pltpu.SMEM)
    full = [(16 * w.shape[0], w.shape[1]) for w in (side, w_in, w_out, w_up, w_down)]
    out_shape = (
        *(shape(*dims, dtype=bf16) for dims in full[1:]),
        shape(768, 1024, dtype=bf16), shape(768, 1024, dtype=bf16), shape(768, 1024, dtype=bf16),
        shape(3072, 1024, dtype=bf16),
        shape(BLOCK, 3072, dtype=bf16),
        shape(BLOCK, 768), shape(BLOCK, 768), shape(BLOCK, 768),
        shape(BLOCK, 2304, dtype=bf16), shape(BLOCK, 768, dtype=bf16),
        shape(BLOCK, LANES), shape(16, BLOCK), shape(16, 768), shape(8, 1536), shape(8, 3072),
        shape(8, 768), shape(8, BLOCK), shape(16, LANES), shape(8, 768),
        shape(8, BLOCK, dtype=jnp.int32),
    )
    v = lambda *dims, dtype=bf16: pltpu.VMEM(dims, dtype)
    dma = pltpu.SemaphoreType.DMA
    return pl.pallas_call(
        functools.partial(forward_kernel, dense),
        name="forward_dense" if dense else "forward",
        out_shape=out_shape,
        in_specs=[sm] + [vm] * 17 + [hbm] * 5 + [vm] * dense,
        out_specs=tuple([hbm] * 14 + [vm] * 10),
        scratch_shapes=[
            *(v(*dims) for dims in full),
            pltpu.VMEM((8, BLOCK), jnp.int32), v(16, LANES, dtype=f32), v(16, LANES, dtype=f32),
            v(16, 8, LANES, dtype=f32), v(16, 8, LANES, dtype=f32), v(8, LANES, dtype=f32),
            v(16, LANES, dtype=f32), v(2, 16, 16, LANES, dtype=f32),
            v(16 * CAP, 384), v(16 * CAP, 768), v(BLOCK, BLOCK, dtype=f32),
            v(BLOCK, 768), v(BLOCK, 768, dtype=f32), v(BLOCK, 2304), v(768, BLOCK), v(BLOCK, 768),
            v(BLOCK, 3072), v(3072, BLOCK), v(BLOCK, 3072), v(768, BLOCK), v(768, BLOCK),
            v(BLOCK, 768, dtype=f32), v(BLOCK, 768, dtype=f32), v(BLOCK, 768, dtype=f32),
            v(BLOCK, 768, dtype=f32), v(BLOCK, 768),
            dma((5,)), dma((5, 32)), dma((5, 16)), dma((5, 16)), dma((16,)), dma((16,)), dma((16,)), dma((16,)),
            dma((16,)), dma((16,)), dma((16,)), dma((16,)), dma((3,)), dma((3,)), dma((14,)), dma((4,)), dma((4,)),
        ],
        compiler_params=pltpu.CompilerParams(
            collective_id=2 if dense else 0, has_side_effects=True, vmem_limit_bytes=62 * 2**20
        ),
    )(lens, feat, col, row, *vec, cot, text, side, w_in, w_out, w_up, w_down, *([extra] if dense else []))


def pack_indices(text_ids, boxes, segment_ids, vocab):
    owner = text_ids // vocab
    return jnp.stack(
        [
            text_ids, boxes[:, 0], boxes[:, 2], boxes[:, 1], boxes[:, 3], segment_ids,
            owner * vocab, owner,
        ],
        axis=1,
    )


def norm_rows(value, gain, shift):
    center = value - jnp.mean(value, axis=-1, keepdims=True)
    spread = lax.rsqrt(jnp.mean(center * center, axis=-1, keepdims=True) + epsilon)
    return center * spread * gain + shift


def gelu_exact(value):
    return jax.nn.gelu(value, approximate=False)


def block_scores(query, keys, member):
    query_heads = query.reshape(BLOCK, -1, HEAD)
    key_heads = keys.reshape(BLOCK, -1, HEAD)
    scores = (
        jnp.einsum("qhd,khd->hqk", query_heads, key_heads, preferred_element_type=jnp.float32)
        * 0.125
    )
    same = member[:, None] == member[None, :]
    return jnp.where(same[None], scores, -1e30)


def attend_forward(operands):
    query, keys, values, member = operands
    scores = block_scores(query, keys, member)
    top = jnp.max(scores, axis=-1, keepdims=True)
    expo = jnp.exp(scores - top)
    total = jnp.sum(expo, axis=-1, keepdims=True)
    probs_low = (expo / total).astype(jnp.bfloat16)
    context = jnp.einsum(
        "hqk,khd->qhd",
        probs_low,
        values.reshape(BLOCK, -1, HEAD),
        preferred_element_type=jnp.float32,
    )
    return (context.reshape(BLOCK, -1).astype(jnp.bfloat16), top + jnp.log(total))


def attend_backward(operands):
    query, keys, values, member, logsum, grad_context = operands
    scores = block_scores(query, keys, member)
    probs = jnp.exp(scores - logsum)
    probs_low = probs.astype(jnp.bfloat16)
    value_heads = values.reshape(BLOCK, -1, HEAD)
    grad_heads = grad_context.reshape(BLOCK, -1, HEAD)
    grad_values = jnp.einsum(
        "hqk,qhd->khd", probs_low, grad_heads, preferred_element_type=jnp.float32
    )
    grad_probs = jnp.einsum(
        "qhd,khd->hqk", grad_heads, value_heads, preferred_element_type=jnp.float32
    )
    delta = jnp.sum(grad_probs * probs, axis=-1, keepdims=True)
    grad_scores = (probs * (grad_probs - delta)).astype(jnp.bfloat16)
    grad_query = (
        jnp.einsum(
            "hqk,khd->qhd",
            grad_scores,
            keys.reshape(BLOCK, -1, HEAD),
            preferred_element_type=jnp.float32,
        )
        * 0.125
    )
    grad_keys = (
        jnp.einsum(
            "hqk,qhd->khd",
            grad_scores,
            query.reshape(BLOCK, -1, HEAD),
            preferred_element_type=jnp.float32,
        )
        * 0.125
    )
    joined = jnp.concatenate(
        [
            grad_query.reshape(BLOCK, -1),
            grad_keys.reshape(BLOCK, -1),
            grad_values.reshape(BLOCK, -1),
        ],
        axis=1,
    )
    return joined.astype(jnp.bfloat16)


def general(
    region_features,
    text_ids,
    boxes,
    segment_ids,
    document_lengths,
    cotangent,
    batch_gain,
    batch_bias,
    text_table,
    side_table,
    embed_gain,
    embed_bias,
    in_weight,
    in_bias,
    out_weight,
    out_bias,
    first_gain,
    first_bias,
    up_weight,
    up_bias,
    down_weight,
    down_bias,
    second_gain,
    second_bias,
):
    rows_here, width = region_features.shape
    blocks_here = document_lengths.shape[0]
    vocab_here = text_table.shape[0]
    ends = jnp.cumsum(document_lengths, axis=1)
    place = jnp.arange(BLOCK, dtype=jnp.int32)
    member = jnp.sum((place[None, :, None] >= ends[:, None, :]).astype(jnp.int32), axis=2)
    valid = (member < SLOTS).astype(jnp.float32).reshape(rows_here, 1)
    shards = lax.axis_size("shard")
    vectors = (
        batch_gain, batch_bias, embed_gain, embed_bias, in_bias, out_bias, first_gain, first_bias,
        up_bias, down_bias, second_gain, second_bias,
    )
    sizes = [v.shape[0] for v in vectors]
    marks = [sum(sizes[:k]) for k in range(len(sizes) + 1)]
    joined = lax.all_gather(jnp.concatenate(vectors), "shard", axis=0)
    (
        full_batch_gain,
        full_batch_bias,
        full_embed_gain,
        full_embed_bias,
        full_in_bias,
        full_out_bias,
        full_first_gain,
        full_first_bias,
        full_up_bias,
        full_down_bias,
        full_second_gain,
        full_second_bias,
    ) = [joined[:, low:high].reshape(-1) for low, high in zip(marks, marks[1:])]
    full_side, full_in_weight, full_out_weight, full_up_weight, full_down_weight = [
        lax.all_gather(w, "shard", axis=0, tiled=True)
        for w in (side_table, in_weight, out_weight, up_weight, down_weight)
    ]
    features = widen(region_features)
    masked = features * valid
    total, count = lax.psum((jnp.sum(masked, axis=0), jnp.sum(valid)), ("rep", "shard"))
    mean = total / count
    center = features - mean
    variance = lax.psum(jnp.sum(center * center * valid, axis=0), ("rep", "shard")) / count
    spread = lax.rsqrt(variance + epsilon)
    batch_hat = center * spread
    gain_wide = widen(full_batch_gain)
    batch_out = batch_hat * gain_wide + widen(full_batch_bias)
    piece = lax.all_gather(text_table, "shard", axis=0, tiled=True)
    add_column = jnp.arange(piece.shape[0], dtype=jnp.int32)
    onehot = (text_ids[:, None] == add_column[None, :]).astype(jnp.bfloat16)
    text_rows = jnp.dot(onehot, piece, preferred_element_type=jnp.float32)
    side_column = jnp.arange(SIDE, dtype=jnp.int32)
    hits = jnp.zeros((rows_here, SIDE), jnp.float32)
    for column in (
        boxes[:, 0],
        boxes[:, 2],
        boxes[:, 1] + BINS,
        boxes[:, 3] + BINS,
        segment_ids + 2 * BINS,
    ):
        hits = hits + (column[:, None] == side_column[None, :]).astype(jnp.float32)
    hits_low = hits.astype(jnp.bfloat16)
    looked = text_rows + jnp.dot(hits_low, full_side, preferred_element_type=jnp.float32)
    start_rows = batch_out + looked
    embedded, back_embed = jax.vjp(
        norm_rows, start_rows, widen(full_embed_gain), widen(full_embed_bias)
    )
    embedded_low = embedded.astype(jnp.bfloat16)
    mixed = jnp.dot(embedded_low, full_in_weight, preferred_element_type=jnp.float32)
    bias_wide = widen(full_in_bias)
    query = (mixed[:, :width] + bias_wide[:width]).astype(jnp.bfloat16)
    keys = mixed[:, width : 2 * width].astype(jnp.bfloat16)
    values = (mixed[:, 2 * width :] + bias_wide[width:]).astype(jnp.bfloat16)
    shaped = (
        query.reshape(blocks_here, BLOCK, width),
        keys.reshape(blocks_here, BLOCK, width),
        values.reshape(blocks_here, BLOCK, width),
    )
    context, logsum = lax.map(attend_forward, shaped + (member,))
    context = context.reshape(rows_here, width)
    branch = jnp.dot(context, full_out_weight, preferred_element_type=jnp.float32) + widen(
        full_out_bias
    )
    first, back_first = jax.vjp(
        norm_rows, embedded + branch, widen(full_first_gain), widen(full_first_bias)
    )
    first_low = first.astype(jnp.bfloat16)
    hidden = jnp.dot(first_low, full_up_weight, preferred_element_type=jnp.float32) + widen(
        full_up_bias
    )
    gelu_value, gelu_back = jax.vjp(gelu_exact, hidden)
    active = gelu_value.astype(jnp.bfloat16)
    second = jnp.dot(active, full_down_weight, preferred_element_type=jnp.float32) + widen(
        full_down_bias
    )
    final, back_second = jax.vjp(
        norm_rows, first + second, widen(full_second_gain), widen(full_second_bias)
    )
    out_rows = final.astype(jnp.bfloat16)
    grad_final = widen(cotangent) * valid
    grad_pre2, grad_second_gain, grad_second_bias = back_second(grad_final)
    grad_second = grad_pre2.astype(jnp.bfloat16)
    grad_down_weight = jnp.einsum(
        "rf,rd->fd", active, grad_second, preferred_element_type=jnp.float32
    )
    grad_down_bias = jnp.sum(widen(grad_second), axis=0)
    grad_active = jnp.einsum(
        "rd,fd->rf", grad_second, full_down_weight, preferred_element_type=jnp.float32
    )
    grad_hidden = gelu_back(grad_active)[0].astype(jnp.bfloat16)
    grad_up_weight = jnp.einsum(
        "rd,rf->df", first_low, grad_hidden, preferred_element_type=jnp.float32
    )
    grad_up_bias = jnp.sum(widen(grad_hidden), axis=0)
    grad_first = grad_pre2 + jnp.einsum(
        "rf,df->rd", grad_hidden, full_up_weight, preferred_element_type=jnp.float32
    )
    grad_pre1, grad_first_gain, grad_first_bias = back_first(grad_first)
    grad_branch = grad_pre1.astype(jnp.bfloat16)
    grad_out_weight = jnp.einsum(
        "rd,re->de", context, grad_branch, preferred_element_type=jnp.float32
    )
    grad_out_bias = jnp.sum(widen(grad_branch), axis=0)
    grad_context = jnp.einsum(
        "re,de->rd", grad_branch, full_out_weight, preferred_element_type=jnp.float32
    ).astype(jnp.bfloat16)
    grad_mixed = lax.map(
        attend_backward, shaped + (member, logsum, grad_context.reshape(blocks_here, BLOCK, width))
    )
    grad_mixed = grad_mixed.reshape(rows_here, 3 * width)
    grad_in_weight = jnp.einsum(
        "rd,re->de", embedded_low, grad_mixed, preferred_element_type=jnp.float32
    )
    column_sums = jnp.sum(widen(grad_mixed), axis=0)
    grad_in_bias = jnp.concatenate([column_sums[:width], column_sums[2 * width :]])
    grad_embedded = grad_pre1 + jnp.einsum(
        "re,de->rd", grad_mixed, full_in_weight, preferred_element_type=jnp.float32
    )
    grad_start, grad_embed_gain, grad_embed_bias = back_embed(grad_embedded)
    grad_looked = grad_start.astype(jnp.bfloat16)
    column = jnp.arange(lax.axis_size("shard") * vocab_here, dtype=jnp.int32)
    onehot = (column[:, None] == text_ids[None, :]).astype(jnp.bfloat16)
    text_grad = lax.psum_scatter(
        jnp.dot(onehot, grad_looked, preferred_element_type=jnp.float32),
        "shard",
        scatter_dimension=0,
        tiled=True,
    )
    grad_side = jnp.einsum("rs,rd->sd", hits_low, grad_looked, preferred_element_type=jnp.float32)
    shift_sum, scale_sum = lax.psum(
        (jnp.sum(grad_start * valid, axis=0), jnp.sum(grad_start * batch_hat * valid, axis=0)),
        ("rep", "shard"),
    )
    feature_grad = (
        valid
        * gain_wide
        * spread
        * (grad_start - shift_sum / count - batch_hat * scale_sum / count)
    ).astype(jnp.bfloat16)
    small = (
        scale_sum / lax.axis_size(("rep", "shard")),
        shift_sum / lax.axis_size(("rep", "shard")),
        grad_embed_gain, grad_embed_bias, grad_in_bias, grad_out_bias, grad_first_gain,
        grad_first_bias, grad_up_bias, grad_down_bias, grad_second_gain, grad_second_bias,
    )
    joined = jnp.concatenate([v.reshape(shards, -1) for v in small], axis=1).reshape(-1)
    owned = [
        lax.psum_scatter(value, "shard", scatter_dimension=0, tiled=True)
        for value in (
            grad_side, grad_in_weight, grad_out_weight, grad_up_weight, grad_down_weight, joined
        )
    ]
    side_grad, in_weight_grad, out_weight_grad, up_weight_grad, down_weight_grad = [
        widen(v) for v in lax.psum(tuple(v.astype(jnp.bfloat16) for v in owned[:5]), "rep")
    ]
    text_table_grad = widen(lax.psum(text_grad.astype(jnp.bfloat16), "rep"))
    pieces = lax.psum(owned[5], "rep")
    (
        batch_gain_grad,
        batch_bias_grad,
        embed_gain_grad,
        embed_bias_grad,
        in_bias_grad,
        out_bias_grad,
        first_gain_grad,
        first_bias_grad,
        up_bias_grad,
        down_bias_grad,
        second_gain_grad,
        second_bias_grad,
    ) = [pieces[low:high] for low, high in zip(marks, marks[1:])]
    return (
        out_rows,
        feature_grad,
        batch_gain_grad,
        batch_bias_grad,
        text_table_grad,
        side_grad,
        embed_gain_grad,
        embed_bias_grad,
        in_weight_grad,
        in_bias_grad,
        out_weight_grad,
        out_bias_grad,
        first_gain_grad,
        first_bias_grad,
        up_weight_grad,
        up_bias_grad,
        down_weight_grad,
        down_bias_grad,
        second_gain_grad,
        second_bias_grad,
    )


class Scatter:
    def __init__(self, index, total, near, relay, line, done, out, sems):
        self.index, self.total, self.near, self.relay, self.line = index, total, near, relay, line
        self.done, self.out = done, out
        self.send_sem, self.near_sem, self.relay_sem, self.line_sem, self.twin_sem, self.keep_sem = sems
        self.rep, self.z, self.y, self.x = spot()
        self.me = at(self.z, self.y, self.x)
        self.rows, self.half = near.shape[1], near.shape[2]

    def rows_at(self, source):
        return rows_of(source, self.rows, 16)

    def beside(self, plane, swap):
        even = lax.rem(plane + self.y + self.x + swap, 2) == 0
        return jnp.where(even, self.y, 1 - self.y), jnp.where(even, 1 - self.x, self.x)

    def copy(self, source, slot, target, dst, recv_sem):
        return pltpu.make_async_remote_copy(
            src_ref=self.total.at[self.rows_at(source)],
            dst_ref=dst,
            send_sem=self.send_sem.at[self.index, slot],
            recv_sem=recv_sem,
            device_id=(self.rep, target),
            device_id_type=MESH,
        )

    def near_copy(self, plane, kind):
        y, x = self.beside(plane, kind)
        target = at(self.z, y, x)
        source = at(plane, y, x) if kind == 0 else at(plane, 1 - self.y, 1 - self.x)
        slot = 2 * plane + kind
        return self.copy(
            source, slot, target, self.near.at[slot], self.near_sem.at[self.index, slot]
        )

    def relay_copy(self, plane):
        y, x = self.beside(plane, 1)
        return self.copy(
            at(plane, y, x), 8 + plane, at(self.z, y, x), self.relay.at[plane],
            self.relay_sem.at[self.index, plane],
        )

    def line_copy(self, plane):
        there = at(plane, self.y, self.x)
        return self.copy(
            there, 12 + plane, there, self.line.at[self.z], self.line_sem.at[self.index, self.z]
        )

    def line_wait(self, plane):
        self.copy(
            self.me, 12 + plane, self.me, self.line.at[plane], self.line_sem.at[self.index, plane]
        ).wait_recv()

    def hop_one(self):
        def step(k, carry):
            plane = lax.rem(self.z + k + 1, 4)
            self.near_copy(plane, 1).start()
            return carry

        lax.fori_loop(0, 4, step, 0)

        def again(k, carry):
            plane = lax.rem(self.z + k + 1, 4)
            self.near_copy(plane, 0).start()
            return carry

        lax.fori_loop(0, 4, again, 0)

    def two(self, k):
        plane = lax.rem(self.z + k + 1, 4)
        self.near_copy(plane, 1).wait_recv()
        y, x = self.beside(plane, 1)
        rows = self.rows_at(at(plane, y, x))
        self.total[rows, :] = (
            widen(self.total[rows, :]) + widen(self.near[2 * plane + 1])
        ).astype(bf16)
        self.relay_copy(plane).start()

    def three(self, k):
        plane = lax.rem(self.z + k + 1, 4)
        self.near_copy(plane, 0).wait_recv()
        self.relay_copy(plane).wait_recv()
        rows = self.rows_at(at(plane, self.y, self.x))
        self.total[rows, :] = (
            widen(self.total[rows, :]) + widen(self.near[2 * plane]) + widen(self.relay[plane])
        ).astype(bf16)

        @pl.when(k < 3)
        def _():
            self.line_copy(plane).start()

    def hop_two(self):
        each(0, 4, self.two)

    def hop_three(self):
        each(0, 4, self.three)

    def finals(self):
        columns = rows_of(self.rep, self.half, LANES)
        return (
            pltpu.make_async_copy(
                self.done, self.out.at[:, columns], self.keep_sem.at[self.index]
            ),
            pltpu.make_async_remote_copy(
                src_ref=self.done,
                dst_ref=self.out.at[:, columns],
                send_sem=self.send_sem.at[self.index, 16],
                recv_sem=self.twin_sem.at[self.index],
                device_id=(1 - self.rep, self.me),
                device_id_type=MESH,
            ),
        )

    def finish(self):
        rows = self.rows_at(self.me)
        self.done[...] = widen(self.total[rows, :])

        def add(k, carry):
            plane = lax.rem(self.z + k, 4)
            self.line_wait(plane)
            self.done[...] = self.done[...] + widen(self.line[plane])
            return carry

        lax.fori_loop(1, 4, add, 0)
        for copy in self.finals():
            copy.start()

    def drain(self):
        def step(k, carry):
            self.near_copy(k, 0).wait_send()
            self.near_copy(k, 1).wait_send()
            self.relay_copy(k).wait_send()

            @pl.when(k != self.z)
            def _():
                self.line_copy(k).wait_send()

            return carry

        lax.fori_loop(0, 4, step, 0)
        kept, twin = self.finals()
        kept.wait()
        twin.wait_send()
        twin.wait_recv()


def compress_vectors(narrow, middle, wide):
    shard_of = iota((16, 1), 0).astype(f32)
    owner, _ = remainder((1, 768), 1, 0, 48)
    stacked = jnp.concatenate(
        [jnp.where(owner == shard_of, narrow[k : k + 1, :], 0.0) for k in range(10)], axis=0
    ).astype(bf16)
    _, depth = remainder((768, 1), 0, 0, 48)
    _, want = remainder((1, 768), 1, 0, 48)
    spread = mm(stacked, onehot(depth == want))
    packed = sum(
        jnp.where(owner == k, spread[k * 16 : k * 16 + 16], 0.0) for k in range(10)
    )

    def piece(row, low, offset, size):
        total = size * 16
        holder, _ = remainder((1, total), 1, 0, size)
        _, place = remainder((total, 1), 0, 0, size)
        lane = iota((1, 256), 1).astype(f32) + (low - offset)
        return mm(jnp.where(holder == shard_of, row, 0.0).astype(bf16), onehot(place == lane))

    packed = packed + jnp.concatenate(
        [jnp.zeros((16, 384), f32), piece(middle, 384, 480, 96), jnp.zeros((16, 128), f32)], axis=1
    )
    return packed + jnp.concatenate(
        [jnp.zeros((16, 512), f32), piece(wide, 512, 576, 192)], axis=1
    )


def norm_back(grad, hat, scale, gain):
    gained = grad * gain
    return scale * (
        gained
        - jnp.mean(gained, axis=-1, keepdims=True)
        - hat * jnp.mean(gained * hat, axis=-1, keepdims=True)
    )


def backward_kernel(
    lens_ref, feat_ref, row_ref, twin_ref, cols_ref, lse_ref, vec_ref, last_ref, slot_ref, req_ref, stat_ref,
    w_in, w_out, w_up, w_down, emb_t, ctx_t, first_t, act_t, dgelu_h, xh0_h, xh1_h, gp2_h, qkv_h,
    feat_o, looked_o, text_o, side_o, in_o, out_o, up_o, down_o, vec_o,
    w_in_s, w_out_s, act_b, down_b, up_b, dgelu_b, ctx_s, first_s, xh1, grad, qkv,
    low, low_twin, hidden, hidden_twin, branch, branch_twin, gctx, mixed, mixed_twin,
    looked, looked_twin,
    down_g, up_g, out_g, in_g, side_g,
    down_n, up_n, out_n, in_n, side_n,
    down_r, up_r, out_r, in_r, side_r,
    down_l, up_l, out_l, in_l, side_l,
    down_d, up_d, out_d, in_d, side_d,
    text_u, text_twin, text_half, text_in, ask_s, mask, vectors, in_row, up_row,
    chip_out, chip_in, outbox, inbox, both,
    load_sem, act_sem, tile_sem, pair_send, pair_recv,
    send_sem, near_sem, relay_sem, line_sem, twin_sem, keep_sem,
    small_send, small_recv, text_ssem, text_rsem, text_keep,
):
    rep, z, y, x = spot()
    me = at(z, y, x)
    vocab = text_o.shape[0]
    barrier = greet()

    loads = {}

    def load(name, source, target):
        loads[name] = pltpu.make_async_copy(source, target, load_sem.at[len(loads)])
        loads[name].start()

    load("grad", gp2_h, grad)

    def act_copy(i):
        slot = lax.rem(i, 4)
        return pltpu.make_async_copy(
            act_t.at[rows_of(i, 256, 256)], act_b.at[slot], act_sem.at[slot]
        )

    def tile_of(i):
        return lax.rem(i + 6 * (1 - rep), 12)

    def tile_copies(i):
        slot = lax.rem(i, 4)
        tile = rows_of(tile_of(i), 256, 256)
        return (
            pltpu.make_async_copy(w_down.at[tile], down_b.at[slot], tile_sem.at[0, slot]),
            pltpu.make_async_copy(w_up.at[:, tile], up_b.at[slot], tile_sem.at[1, slot]),
            pltpu.make_async_copy(dgelu_h.at[:, tile], dgelu_b.at[slot], tile_sem.at[2, slot]),
        )

    for k in range(3):
        for copy in tile_copies(k):
            copy.start()
    for k in range(3):
        act_copy(k).start()

    sems = (send_sem, near_sem, relay_sem, line_sem, twin_sem, keep_sem)
    down_a = Scatter(0, down_g, down_n, down_r, down_l, down_d, down_o, sems)
    up_a = Scatter(1, up_g, up_n, up_r, up_l, up_d, up_o, sems)
    out_a = Scatter(2, out_g, out_n, out_r, out_l, out_d, out_o, sems)
    in_a = Scatter(3, in_g, in_n, in_r, in_l, in_d, in_o, sems)
    side_a = Scatter(4, side_g, side_n, side_r, side_l, side_d, side_o, sems)

    paired = []

    def pair(source, target):
        copy = pltpu.make_async_remote_copy(
            src_ref=source,
            dst_ref=target,
            send_sem=pair_send.at[len(paired)],
            recv_sem=pair_recv.at[len(paired)],
            device_id=(1 - rep, me),
            device_id_type=MESH,
        )
        paired.append(copy)
        copy.start()
        return copy

    def half_of(width, core):
        return rows_of(core, width // 2, LANES)

    own_columns = rows_of(rep, BLOCK, LANES)
    twin_columns = rows_of(1 - rep, BLOCK, LANES)

    same = members(lens_ref, (BLOCK, 1), 0) == members(lens_ref, (1, BLOCK), 1)
    mask[...] = jnp.where(same, 0.0, -1e30)
    vectors[...] = jnp.concatenate(
        [jnp.zeros((8, 768), f32), last_ref[0:2, :], jnp.zeros((6, 768), f32)], axis=0
    )

    loads["grad"].wait()

    def second(c, total):
        rows = rows_of(c, 128, 128)
        value = grad[rows, :].astype(bf16)
        low[rows, :] = value
        return total + jnp.sum(widen(value), axis=0, keepdims=True)

    zero = jnp.zeros((1, 768), f32)
    vectors[7:8, :] = lax.fori_loop(0, 4, second, zero)
    pl.semaphore_wait(barrier, 16)
    low_pair = pair(low.at[:, half_of(768, 1 - rep)], low_twin)

    def feed(i, carry):
        slot = lax.rem(i, 4)
        for copy in tile_copies(i):
            copy.wait()

        @pl.when(i < 9)
        def _():
            for copy in tile_copies(i + 3):
                copy.start()

        tile = rows_of(tile_of(i), 256, 256)
        value = (widen(dgelu_b[slot]) * mm_nt(low[...], down_b[slot])).astype(bf16)
        hidden[:, tile] = value
        up_row[0:1, tile] = jnp.sum(widen(value), axis=0, keepdims=True)
        grad[...] = grad[...] + mm_nt(value, up_b[slot])
        return carry

    low_pair.wait_recv()

    def down_step(i, carry):
        slot = lax.rem(i, 4)
        act_copy(i).wait()

        @pl.when(i < 9)
        def _():
            act_copy(i + 3).start()

        down_g[rows_of(i, 256, 256), :] = (
            mm(act_b[slot, :, own_columns], low[:, half_of(768, rep)])
            + mm(act_b[slot, :, twin_columns], low_twin[...])
        ).astype(bf16)
        return carry

    lax.fori_loop(0, 12, down_step, 0)
    down_a.hop_one()

    load("first", first_t, first_s)
    load("xh1", xh1_h, xh1)
    load("out", w_out, w_out_s)
    load("qkv", qkv_h, qkv)
    load("ctx", ctx_t, ctx_s)
    load("in", w_in, w_in_s)

    lax.fori_loop(0, 6, feed, 0)
    hidden_pair = pair(hidden.at[:, half_of(3072, 1 - rep)], hidden_twin)
    lax.fori_loop(6, 12, feed, 0)
    loads["first"].wait()
    hidden_pair.wait_recv()

    def up_step(i, carry):
        tile = rows_of(i, 256, 256)
        own = pl.ds(pl.multiple_of(rep * 1536 + i * 256, 256), 256)
        up_g[:, tile] = (
            mm(first_s[:, own_columns], hidden[:, own])
            + mm(first_s[:, twin_columns], hidden_twin[:, tile])
        ).astype(bf16)

        @pl.when(i >= 2)
        def _():
            down_a.two(i - 2)

        return carry

    lax.fori_loop(0, 6, up_step, 0)
    load("emb", emb_t, first_s)
    up_a.hop_one()

    loads["xh1"].wait()

    def norm_one(c, carry):
        rows = rows_of(c, 128, 128)
        value, hat = grad[rows, :], xh1[rows, :]
        back = norm_back(value, hat, cols_ref[rows, 1:2], vec_ref[5:6, :])
        grad[rows, :] = back
        rounded = back.astype(bf16)
        branch[rows, :] = rounded
        gain, bias, out = carry
        return (
            gain + jnp.sum(value * hat, axis=0, keepdims=True),
            bias + jnp.sum(value, axis=0, keepdims=True),
            out + jnp.sum(widen(rounded), axis=0, keepdims=True),
        )

    gain, bias, out = lax.fori_loop(0, 4, norm_one, (zero, zero, zero))
    load("xh0", xh0_h, xh1)
    vectors[4:5, :] = out
    vectors[5:6, :] = gain
    vectors[6:7, :] = bias
    branch_pair = pair(branch.at[:, half_of(768, 1 - rep)], branch_twin)
    loads["out"].wait()

    def context_step(i, carry):
        tile = rows_of(i, 256, 256)
        gctx[:, tile] = mm_nt(branch[...], w_out_s[tile, :]).astype(bf16)
        return carry

    lax.fori_loop(0, 3, context_step, 0)
    loads["ctx"].wait()
    branch_pair.wait_recv()

    def out_step(i, carry):
        rows = rows_of(i, 256, 256)
        out_g[rows, :] = (
            mm(ctx_s[rows, own_columns], branch[:, half_of(768, rep)])
            + mm(ctx_s[rows, twin_columns], branch_twin[...])
        ).astype(bf16)
        return carry

    lax.fori_loop(0, 3, out_step, 0)
    out_a.hop_one()

    loads["qkv"].wait()

    def attend(p, carry):
        pair_lanes = rows_of(p, LANES, LANES)
        query = qkv[:, pair_lanes]
        keys = qkv[:, rows_of(p + 6, LANES, LANES)]
        values = qkv[:, rows_of(p + 12, LANES, LANES)]
        outer = gctx[:, pair_lanes]
        keys_t = jnp.transpose(keys)
        query_t, key_parts, value_parts = [], [], []
        for head in range(2):
            in_head = iota((1, LANES), 1) // HEAD == head
            masked = query * jnp.where(in_head, 0.125, 0.0).astype(bf16)
            outer_masked = outer * jnp.where(in_head, 1.0, 0.0).astype(bf16)
            key_part = jnp.zeros((BLOCK, LANES), f32)
            value_part = jnp.zeros((BLOCK, LANES), f32)
            columns = []
            for part in range(2):
                s = slice(part * 256, part * 256 + 256)
                scores = mm_nt(keys, masked[s, :]) + mask[:, s]
                probs = jnp.exp(scores - lse_ref[pl.ds(2 * p + head, 1), s])
                grads = mm_nt(values, outer_masked[s, :])
                delta = jnp.sum(probs * grads, axis=0, keepdims=True)
                inner = (probs * (grads - delta)).astype(bf16)
                value_part = value_part + mm(probs.astype(bf16), outer[s, :])
                key_part = key_part + mm(inner, query[s, :])
                columns.append(mm(keys_t[head * HEAD : (head + 1) * HEAD, :], inner))
            query_t.append(jnp.concatenate(columns, axis=1))
            key_parts.append(key_part)
            value_parts.append(value_part)
        first_head = iota((1, LANES), 1) < HEAD
        gathered = (jnp.concatenate(query_t, axis=0) * 0.125).astype(bf16)
        mixed[:, pair_lanes] = jnp.transpose(gathered)
        mixed[:, rows_of(p + 6, LANES, LANES)] = (
            jnp.where(first_head, key_parts[0], key_parts[1]) * 0.125
        ).astype(bf16)
        mixed[:, rows_of(p + 12, LANES, LANES)] = jnp.where(
            first_head, value_parts[0], value_parts[1]
        ).astype(bf16)

        @pl.when(p < 4)
        def _():
            up_a.two(p)

        @pl.when(p >= 2)
        def _():
            down_a.three(p - 2)

        return carry

    lax.fori_loop(0, 6, attend, 0)
    out_a.hop_two()
    mixed_pair = pair(mixed.at[:, half_of(2304, 1 - rep)], mixed_twin)

    loads["in"].wait()

    def embed_step(i, carry):
        tile = rows_of(i, 256, 256)
        grad[:, tile] = grad[:, tile] + mm_nt(mixed[...], w_in_s[tile, :])
        return carry

    lax.fori_loop(0, 3, embed_step, 0)

    def bias_step(i, carry):
        tile = rows_of(i, 256, 256)
        in_row[0:1, tile] = jnp.sum(widen(mixed[:, tile]), axis=0, keepdims=True)
        return carry

    lax.fori_loop(0, 9, bias_step, 0)
    loads["emb"].wait()
    mixed_pair.wait_recv()

    def in_step(i, carry):
        tile = rows_of(i, 384, 128)
        own = pl.ds(pl.multiple_of(rep * 1152 + i * 384, 128), 384)
        in_g[:, tile] = (
            mm(first_s[:, own_columns], mixed[:, own])
            + mm(first_s[:, twin_columns], mixed_twin[:, tile])
        ).astype(bf16)
        return carry

    lax.fori_loop(0, 3, in_step, 0)
    in_a.hop_one()

    up_a.hop_three()
    loads["xh0"].wait()

    def norm_zero(c, carry):
        rows = rows_of(c, 128, 128)
        value, hat = grad[rows, :], xh1[rows, :]
        back = norm_back(value, hat, cols_ref[rows, 0:1], vec_ref[2:3, :])
        grad[rows, :] = back
        looked[rows, :] = back.astype(bf16)
        gain, bias, scales, shifts = carry
        kept = back * cols_ref[rows, 3:4]
        batch_hat = (widen(feat_ref[rows, :]) - stat_ref[0:1, :]) * stat_ref[1:2, :]
        return (
            gain + jnp.sum(value * hat, axis=0, keepdims=True),
            bias + jnp.sum(value, axis=0, keepdims=True),
            scales + jnp.sum(kept * batch_hat, axis=0, keepdims=True),
            shifts + jnp.sum(kept, axis=0, keepdims=True),
        )

    gain, bias, scales, shifts = lax.fori_loop(0, 4, norm_zero, (zero, zero, zero, zero))
    looked_local = pltpu.make_async_copy(looked, looked_o, text_keep.at[0])
    looked_local.start()
    looked_pair = pair(looked.at[:, half_of(768, 1 - rep)], looked_twin)
    vectors[0:1, :] = scales
    vectors[1:2, :] = shifts
    vectors[2:3, :] = gain
    vectors[3:4, :] = bias
    packed = compress_vectors(
        vectors[...],
        jnp.concatenate([in_row[0:1, 0:768], in_row[0:1, 1536:2304]], axis=1),
        up_row[0:1, :],
    )
    chip_out[...] = jnp.concatenate([packed, scales, shifts, jnp.zeros((6, 768), f32)], axis=0)
    chip_pair = pair(chip_out, chip_in)

    def text_sum(i, carry):
        rows = rows_of(i, 256, 256)
        place = (iota((256, 1), 0) + i * 256).astype(f32)
        text_u[rows, :] = mm(onehot(slot_ref[0:1, :] == place), looked[...]).astype(bf16)
        return carry

    lax.fori_loop(0, 16 * CAP // 256, text_sum, 0)

    text_pair_in = pair(text_u.at[:, half_of(768, 1 - rep)], text_twin)
    chip_pair.wait_recv()
    chip_in[...] = chip_out[...] + chip_in[...]
    chip_half = chip_in[:, half_of(768, rep)]
    for t in range(16):
        for j in range(3):
            lanes = slice(j * LANES, (j + 1) * LANES)
            outbox[t, j : j + 1, :] = chip_half[t : t + 1, lanes]
            outbox[t, 3 + j : 4 + j, :] = chip_half[16:17, lanes]
            outbox[t, 6 + j : 7 + j, :] = chip_half[17:18, lanes]
        outbox[t, 9:16, :] = jnp.zeros((7, LANES), f32)
    exchange(outbox, inbox, small_send, small_recv, True)
    inbox[me] = outbox[me]
    text_pair_in.wait_recv()
    for c in range(4):
        rows = slice(c * 256, c * 256 + 256)
        text_half[rows, :] = (
            widen(text_u[rows, half_of(768, rep)]) + widen(text_twin[rows, :])
        ).astype(bf16)

    def text_copy(k, source):
        there = lax.rem(me + k, 16)
        return pltpu.make_async_remote_copy(
            src_ref=text_half.at[rows_of(there, CAP, 16)],
            dst_ref=text_in.at[rows_of(source, CAP, 16)],
            send_sem=text_ssem.at[k],
            recv_sem=text_rsem.at[source],
            device_id=(rep, there),
            device_id_type=MESH,
        )

    def text_start(k, carry):
        text_copy(k, me).start()
        return carry

    lax.fori_loop(1, 16, text_start, 0)
    text_in[rows_of(me, CAP, 16), :] = text_half[rows_of(me, CAP, 16), :]

    looked_pair.wait_recv()
    for tile in range(5):
        base = tile * 512
        kinds = (1, 2) if base < BINS else (3, 4) if base < 2 * BINS else (5,)
        place = iota((512, 1), 0) + base % BINS

        def counted(ref):
            return sum((ref[k : k + 1, :] == place).astype(f32) for k in kinds).astype(bf16)

        side_g[base : base + 512, :] = (
            mm(counted(row_ref), looked[:, half_of(768, rep)])
            + mm(counted(twin_ref), looked_twin[...])
        ).astype(bf16)
    side_a.hop_one()

    out_a.hop_three()
    in_a.hop_two()
    down_a.finish()
    up_a.finish()
    _, want = remainder((1, 16 * CAP), 1, 0, CAP)
    sender, _ = remainder((1, 16 * CAP), 1, 0, CAP)
    pick = onehot(iota((LANES, 1), 0).astype(f32) == want)
    asked = req_ref[...] + 1.0
    coarse = jnp.floor(asked * (1.0 / 32.0))
    fine = asked - 32.0 * coarse
    place = 32.0 * mm(coarse.astype(bf16), pick) + mm(fine.astype(bf16), pick)
    ours = sender == iota((16, 1), 0).astype(f32)
    ask_s[0:1, :] = jnp.sum(jnp.where(ours, place, 0.0), axis=0, keepdims=True)


    side_a.hop_two()
    in_a.hop_three()
    out_a.finish()
    def text_wait(k, carry):
        text_copy(k, lax.rem(me + k, 16)).wait_recv()
        return carry

    lax.fori_loop(1, 16, text_wait, 0)

    part = vocab // 2

    def text_step(i, carry):
        rows = rows_of(i, 96, 32)
        for k in range(2):
            place = (iota((96, 1), 0) + (i * 96 + 1 + k * part)).astype(f32)
            xh1[rows, k * 384 : k * 384 + 384] = mm(
                onehot(ask_s[0:1, :] == place), text_in[...]
            )
        return carry

    lax.fori_loop(0, part // 96, text_step, 0)
    text_local, text_pairs = [], []
    for k in range(2):
        source = xh1.at[0:part, k * 384 : k * 384 + 384]
        target = text_o.at[k * part : k * part + part, half_of(768, rep)]
        text_local.append(pltpu.make_async_copy(source, target, text_keep.at[2 + k]))
        text_local[k].start()
        text_pairs.append(pair(source, target))

    side_a.hop_three()
    exchange(outbox, inbox, small_send, small_recv, False)
    both[rep] = sum(inbox[t] for t in range(16))
    both_pair = pair(both.at[rep], both.at[rep])
    both_pair.wait_recv()
    vec_o[...] = jnp.concatenate([both[0, 0:3, :], both[1, 0:3, :], jnp.zeros((2, LANES), f32)], axis=0)
    scale_row = jnp.concatenate(
        [both[j // 3, 3 + j % 3 : 4 + j % 3, :] for j in range(6)], axis=1
    )
    shift_row = jnp.concatenate(
        [both[j // 3, 6 + j % 3 : 7 + j % 3, :] for j in range(6)], axis=1
    )
    scale_row = scale_row / stat_ref[2:3, :]
    shift_row = shift_row / stat_ref[2:3, :]

    def feature(c, carry):
        rows = rows_of(c, 128, 128)
        batch_hat = (widen(feat_ref[rows, :]) - stat_ref[0:1, :]) * stat_ref[1:2, :]
        value = grad[rows, :] - shift_row - batch_hat * scale_row
        gctx[rows, :] = (
            cols_ref[rows, 3:4] * (vec_ref[0:1, :] * stat_ref[1:2, :]) * value
        ).astype(bf16)
        return carry

    lax.fori_loop(0, 4, feature, 0)
    feat_local = pltpu.make_async_copy(gctx, feat_o, text_keep.at[1])
    feat_local.start()

    in_a.finish()
    side_a.finish()
    for a in (down_a, up_a, out_a, in_a, side_a):
        a.drain()

    def text_drain(k, carry):
        text_copy(k, me).wait_send()
        return carry

    lax.fori_loop(1, 16, text_drain, 0)
    for copy in paired:
        copy.wait_send()
    for k in range(2):
        text_pairs[k].wait_recv()
        text_local[k].wait()
    feat_local.wait()
    looked_local.wait()


def backward_call(lens, feat, row, made, vocab):
    (
        w_in, w_out, w_up, w_down, emb_t, ctx_t, first_t, act_t, dgelu, xh0, xh1, gp2, qkv, _,
        cols, lse, vec, _, _, last, slot, req, stat, twin,
    ) = made
    vm, hbm = pl.BlockSpec(memory_space=pltpu.VMEM), pl.BlockSpec(memory_space=pl.ANY)
    sm = pl.BlockSpec(memory_space=pltpu.SMEM)
    v = lambda *dims, dtype=bf16: pltpu.VMEM(dims, dtype)
    dma = pltpu.SemaphoreType.DMA
    parts = [(192, 384), (48, 1536), (48, 384), (48, 1152), (160, 384)]
    return pl.pallas_call(
        backward_kernel,
        name="backward",
        out_shape=(
            shape(BLOCK, 768, dtype=bf16), shape(BLOCK, 768, dtype=bf16), shape(vocab, 768), shape(160, 768), shape(48, 2304),
            shape(48, 768), shape(48, 3072), shape(192, 768), shape(8, LANES),
        ),
        in_specs=[sm] + [vm] * 10 + [hbm] * 13,
        out_specs=tuple([hbm] * 8 + [vm]),
        scratch_shapes=[
            v(768, 2304), v(768, 768), v(4, 256, 1024), v(4, 256, 768), v(4, 768, 256),
            v(4, BLOCK, 256), v(768, 1024), v(768, 1024),
            v(BLOCK, 768, dtype=f32), v(BLOCK, 768, dtype=f32),
            v(BLOCK, 2304),
            v(BLOCK, 768), v(BLOCK, 384), v(BLOCK, 3072), v(BLOCK, 1536), v(BLOCK, 768),
            v(BLOCK, 384), v(BLOCK, 768), v(BLOCK, 2304), v(BLOCK, 1152),
            v(BLOCK, 768), v(BLOCK, 384),
            *(v(16 * r, c) for r, c in parts),
            *(v(8, r, c) for r, c in parts),
            *(v(4, r, c) for r, c in parts),
            *(v(4, r, c) for r, c in parts),
            *(v(r, c, dtype=f32) for r, c in parts),
            v(16 * CAP, 768), v(16 * CAP, 384), v(16 * CAP, 384), v(16 * CAP, 384),
            v(8, 16 * CAP, dtype=f32), v(BLOCK, BLOCK, dtype=f32),
            v(16, 768, dtype=f32), v(8, 2304, dtype=f32), v(8, 3072, dtype=f32),
            v(24, 768, dtype=f32), v(24, 768, dtype=f32), v(16, 16, LANES, dtype=f32),
            v(16, 16, LANES, dtype=f32), v(2, 16, LANES, dtype=f32),
            dma((9,)), dma((4,)), dma((3, 4)), dma((10,)), dma((10,)),
            dma((5, 17)), dma((5, 8)), dma((5, 4)), dma((5, 4)), dma((5,)), dma((5,)),
            dma((16,)), dma((16,)), dma((16,)), dma((16,)), dma((4,)),
        ],
        compiler_params=pltpu.CompilerParams(
            collective_id=1, has_side_effects=True, vmem_limit_bytes=62 * 2**20
        ),
    )(
        lens, feat, row, twin, cols, lse, vec, last, slot, req, stat,
        w_in, w_out, w_up, w_down, emb_t, ctx_t, first_t, act_t, dgelu, xh0, xh1, gp2, qkv,
    )


def dense_rows(text_ids, text_table):
    shards, vocab = lax.axis_size("shard"), text_table.shape[0]
    ring = [(k, (k + 1) % shards) for k in range(shards)]
    local = jnp.arange(vocab, dtype=jnp.int32)

    def step(k, carry):
        piece, rows = carry
        owner = lax.rem(lax.axis_index("shard") + shards - k, shards)
        hit = (text_ids - owner * vocab)[:, None] == local[None, :]
        return lax.ppermute(piece, "shard", ring), rows + mm(hit.astype(bf16), piece)

    rows = jnp.zeros((text_ids.shape[0], text_table.shape[1]), f32)
    return lax.fori_loop(0, shards, step, (text_table, rows))[1].astype(bf16)


def dense_sums(text_ids, looked, vocab):
    shards = lax.axis_size("shard")
    ring = [(k, (k + 1) % shards) for k in range(shards)]
    local = jnp.arange(vocab, dtype=jnp.int32)

    def step(k, total):
        owner = lax.rem(lax.axis_index("shard") + 2 * shards - 1 - k, shards)
        hit = local[:, None] == (text_ids - owner * vocab)[None, :]
        return lax.ppermute(total, "shard", ring) + mm(hit.astype(bf16), looked)

    total = lax.fori_loop(0, shards, step, jnp.zeros((vocab, looked.shape[1]), f32))
    return total + lax.ppermute(total, "rep", [(0, 1), (1, 0)])


def once(condition, body, value):
    return lax.while_loop(
        lambda state: state[0],
        lambda state: (jnp.zeros((), bool), body(state[1])),
        (condition, value),
    )[1]


def fast(*args):
    (
        region_features, text_ids, boxes, segment_ids, document_lengths, cotangent,
        batch_gain, batch_bias, text_table, side_table, embed_gain, embed_bias,
        in_weight, in_bias, out_weight, out_bias, first_gain, first_bias,
        up_weight, up_bias, down_weight, down_bias, second_gain, second_bias,
    ) = args
    vocab = text_table.shape[0]
    col = pack_indices(text_ids, boxes, segment_ids, vocab)
    row = col.T
    vec = [
        v.reshape(1, -1)
        for v in (
            batch_gain, batch_bias, embed_gain, embed_bias, out_bias, first_gain, first_bias,
            down_bias, second_gain, second_bias, in_bias, up_bias,
        )
    ]
    operands = (
        document_lengths, region_features, col, row, vec, cotangent, text_table,
        side_table, in_weight, out_weight, up_weight, down_weight,
    )
    made = forward_call(*operands)
    crowded = made[-2][3, 0] > CAP
    made = once(
        crowded,
        lambda _: tuple(forward_call(*operands, dense_rows(text_ids, text_table))),
        tuple(made),
    )
    feature_grad, looked, g_text, g_side, g_in, g_out, g_up, g_down, pieces = backward_call(
        document_lengths, region_features, row, made, vocab
    )
    g_text = once(crowded, lambda total: total + dense_sums(text_ids, looked, vocab), g_text)
    pieces = pieces.reshape(-1)
    cut = lambda k: pieces[k * 48 : (k + 1) * 48]
    return (
        made[13], feature_grad, cut(0), cut(1), g_text, g_side, cut(2), cut(3), g_in,
        pieces[480:576], g_out, cut(4), cut(5), cut(6), g_up, pieces[576:768], g_down, cut(7),
        cut(8), cut(9),
    )


def fits(mesh):
    return dict(mesh.shape) == {"rep": 2, "shard": 16}


def solution(mesh):
    in_specs = (
        P(("rep", "shard"), None),
        P(("rep", "shard")),
        P(("rep", "shard"), None),
        P(("rep", "shard")),
        P(("rep", "shard"), None),
        P(("rep", "shard"), None),
        P("shard"),
        P("shard"),
        P("shard", None),
        P("shard", None),
        P("shard"),
        P("shard"),
        P("shard", None),
        P("shard"),
        P("shard", None),
        P("shard"),
        P("shard"),
        P("shard"),
        P("shard", None),
        P("shard"),
        P("shard", None),
        P("shard"),
        P("shard"),
        P("shard"),
    )
    out_specs = (
        P(("rep", "shard"), None),
        P(("rep", "shard"), None),
        P("shard"),
        P("shard"),
        P("shard", None),
        P("shard", None),
        P("shard"),
        P("shard"),
        P("shard", None),
        P("shard"),
        P("shard", None),
        P("shard"),
        P("shard"),
        P("shard"),
        P("shard", None),
        P("shard"),
        P("shard", None),
        P("shard"),
        P("shard"),
        P("shard"),
    )
    return jax.shard_map(
        fast if fits(mesh) else general, mesh=mesh, in_specs=in_specs, out_specs=out_specs, check_vma=False
    )
```

```python
import functools
import math

import jax
import jax.numpy as jnp
from jax import lax
from jax.experimental import pallas as pl
from jax.experimental.pallas import tpu as pltpu
from jax.sharding import PartitionSpec as P

HEAD = 64
BINS = 1024
SIDE = 2560
BLOCK = 512
SLOTS = 4
CAP = 64
LANES = 128
MESH = pl.DeviceIdType.MESH
f32 = jnp.float32
bf16 = jnp.bfloat16

epsilon = 1e-05


def widen(value):
    return value.astype(jnp.float32)


def mm(a, b):
    return jnp.dot(a, b, preferred_element_type=f32)


def mm_nt(a, b):
    return lax.dot_general(a, b, (((1,), (1,)), ((), ())), preferred_element_type=f32)


def iota(shape, dim):
    return lax.broadcasted_iota(jnp.int32, shape, dim)


def spot():
    shard = lax.axis_index("shard")
    return lax.axis_index("rep"), shard // 4, (shard // 2) % 2, shard % 2


def at(z, y, x):
    return z * 4 + y * 2 + x


def rows_of(start, size, step):
    return pl.ds(pl.multiple_of(start * size, step), size)


def each(low, high, body):
    def step(k, carry):
        body(k)
        return carry

    lax.fori_loop(low, high, step, 0)


class Gather:
    def __init__(self, index, shard_ref, full_ref, own_sem, send_sem, recv_sem, twin_sem):
        self.index, self.shard, self.full = index, shard_ref, full_ref
        self.own_sem, self.send_sem, self.recv_sem, self.twin_sem = own_sem, send_sem, recv_sem, twin_sem
        self.rep, self.z, self.y, self.x = spot()
        self.me = at(self.z, self.y, self.x)
        self.rows = shard_ref.shape[0]
        self.half = shard_ref.shape[1] // 2

    def block(self, source, half):
        return self.full.at[
            rows_of(source, self.rows, 16), rows_of(half, self.half, LANES)
        ]

    def copy(self, source, slot, target, src=None, twin=False):
        return pltpu.make_async_remote_copy(
            src_ref=self.block(source, self.rep) if src is None else src,
            dst_ref=self.block(source, self.rep),
            send_sem=self.send_sem.at[self.index, slot],
            recv_sem=(self.twin_sem if twin else self.recv_sem).at[self.index, source],
            device_id=target,
            device_id_type=MESH,
        )

    def own(self):
        return pltpu.make_async_copy(
            self.shard, self.full.at[rows_of(self.me, self.rows, 16)], self.own_sem.at[self.index]
        )

    def start_line(self):
        src = self.shard.at[:, rows_of(self.rep, self.half, LANES)]

        def step(k, carry):
            there = lax.rem(self.z + k, 4)
            self.copy(self.me, there, (self.rep, at(there, self.y, self.x)), src=src).start()
            return carry

        lax.fori_loop(1, 4, step, 0)

    def start_own(self):
        src = self.shard.at[:, rows_of(self.rep, self.half, LANES)]
        self.copy(self.me, 4 + self.z, self.beside(self.z, 0), src=src).start()
        self.copy(self.me, 8 + self.z, self.beside(self.z, 1), src=src).start()
        self.own().start()

    def to_twin(self, source):
        self.copy(source, 16 + source, (1 - self.rep, self.me), twin=True).start()

    def beside(self, plane, swap):
        even = lax.rem(plane + self.y + self.x + swap, 2) == 0
        return (
            self.rep,
            at(self.z, jnp.where(even, self.y, 1 - self.y), jnp.where(even, 1 - self.x, self.x)),
        )

    def one(self, k):
        plane = lax.rem(self.z + k, 4)
        source = at(plane, self.y, self.x)
        self.copy(source, 0, (self.rep, self.me)).wait_recv()
        self.copy(source, 4 + plane, self.beside(plane, 0)).start()
        self.copy(source, 8 + plane, self.beside(plane, 1)).start()
        self.to_twin(source)

    def two(self, k):
        plane = lax.rem(self.z + k, 4)
        even = lax.rem(plane + self.y + self.x, 2) == 0
        source = at(
            plane, jnp.where(even, 1 - self.y, self.y), jnp.where(even, self.x, 1 - self.x)
        )
        self.copy(source, 0, (self.rep, self.me)).wait_recv()
        self.copy(source, 12 + plane, self.beside(plane, 0)).start()
        self.to_twin(source)

    def three(self, k):
        plane = lax.rem(self.z + k, 4)
        even = lax.rem(plane + self.y + self.x, 2) == 0
        near = at(
            plane, jnp.where(even, self.y, 1 - self.y), jnp.where(even, 1 - self.x, self.x)
        )
        for source in (near, at(plane, 1 - self.y, 1 - self.x)):
            self.copy(source, 0, (self.rep, self.me)).wait_recv()
            self.to_twin(source)

    def hop_one(self):
        each(1, 4, self.one)

    def hop_two(self):
        each(0, 4, self.two)

    def last(self):
        each(0, 4, self.three)

    def ready(self):
        self.own().wait()

        def step(k, carry):
            source = lax.rem(self.me + k, 16)
            pltpu.make_async_remote_copy(
                src_ref=self.block(source, 1 - self.rep),
                dst_ref=self.block(source, 1 - self.rep),
                send_sem=self.send_sem.at[self.index, 0],
                recv_sem=self.twin_sem.at[self.index, source],
                device_id=(self.rep, self.me),
                device_id_type=MESH,
            ).wait_recv()
            return carry

        lax.fori_loop(1, 16, step, 0)

    def drain(self):
        def step(k, carry):
            @pl.when((k != self.z) & (k != 16 + self.me))
            def _():
                self.copy(self.me, k, (self.rep, self.me)).wait_send()

            return carry

        lax.fori_loop(0, 32, step, 0)


def exchange(outbox, inbox, send_sem, recv_sem, start):
    rep, me = lax.axis_index("rep"), lax.axis_index("shard")
    each = len(outbox.shape) == 3

    def copy(k, source):
        there = lax.rem(me + k, 16)
        return pltpu.make_async_remote_copy(
            src_ref=outbox.at[there] if each else outbox,
            dst_ref=inbox.at[source],
            send_sem=send_sem.at[k],
            recv_sem=recv_sem.at[source],
            device_id=(rep, there),
            device_id_type=MESH,
        )

    def begin(k, carry):
        copy(k, me).start()
        return carry

    def done(k, carry):
        sent = copy(k, lax.rem(me + k, 16))
        sent.wait_send()
        sent.wait_recv()
        return carry

    lax.fori_loop(1, 16, begin if start else done, 0)


def greet():
    barrier = pltpu.get_barrier_semaphore()
    rep, me = lax.axis_index("rep"), lax.axis_index("shard")

    def step(k, carry):
        pl.semaphore_signal(
            barrier, inc=1, device_id=(rep, lax.rem(me + k, 16)), device_id_type=MESH
        )
        return carry

    lax.fori_loop(1, 16, step, 0)
    pl.semaphore_signal(barrier, inc=1, device_id=(1 - rep, me), device_id_type=MESH)
    return barrier


def members(lens_ref, shape, dim):
    place = iota(shape, dim)
    end = jnp.int32(0)
    member = jnp.zeros(shape, jnp.int32)
    for slot in range(SLOTS):
        end = end + lens_ref[0, slot]
        member = member + (place >= end).astype(jnp.int32)
    return member


def spread_rows(value):
    return lax.rsqrt(jnp.mean(value * value, axis=-1, keepdims=True) + epsilon)


def onehot(condition):
    return jnp.where(condition, 1.0, 0.0).astype(bf16)


def remainder(shape, dim, offset, size):
    place = iota(shape, dim).astype(f32) - offset
    group = jnp.floor((place + 0.5) * (1.0 / size))
    return group, place - group * size


def expand_vectors(packed):
    def select(low, width, offset, size):
        _, want = remainder((1, size * 16), 1, 0, size)
        depth = iota((width, 1), 0).astype(f32) + (low - offset)
        return onehot(depth == want)

    kinds, _ = remainder((1, 768), 1, 0, 48)
    stacked = jnp.concatenate(
        [jnp.where(kinds == k, packed, 0.0) for k in range(10)], axis=0
    ).astype(bf16)
    _, depth = remainder((768, 1), 0, 0, 48)
    _, want = remainder((1, 768), 1, 0, 48)
    spread = mm(stacked, onehot(depth == want))
    owner, _ = remainder((1, 768), 1, 0, 48)
    shard_of = iota((16, 1), 0).astype(f32)
    narrow = jnp.concatenate(
        [
            jnp.sum(jnp.where(owner == shard_of, spread[k * 16 : k * 16 + 16], 0.0), axis=0, keepdims=True)
            for k in range(10)
        ],
        axis=0,
    )
    low = packed.astype(bf16)
    owner, _ = remainder((1, 1536), 1, 0, 96)
    middle = mm(low[:, 384:640], select(384, 256, 480, 96))
    middle = jnp.sum(jnp.where(owner == shard_of, middle, 0.0), axis=0, keepdims=True)
    owner, _ = remainder((1, 3072), 1, 0, 192)
    wide = mm(low[:, 512:768], select(512, 256, 576, 192))
    wide = jnp.sum(jnp.where(owner == shard_of, wide, 0.0), axis=0, keepdims=True)
    return narrow, middle, wide


def transpose_to(target, source):
    for j in range(source.shape[1] // LANES):
        target[j * LANES : (j + 1) * LANES, :] = jnp.transpose(
            source[:, j * LANES : (j + 1) * LANES]
        )


def forward_kernel(
    dense, lens_ref, feat_ref, col_ref, row_ref, *rest,
):
    vec_refs, rest = rest[:12], rest[12:]
    cot_ref, text_ref, side_sh, in_sh, out_sh, up_sh, down_sh, *rest = rest
    extra_ref = rest[0] if dense else None
    forward_body(
        dense, extra_ref, lens_ref, feat_ref, col_ref, row_ref, vec_refs, cot_ref, text_ref,
        side_sh, in_sh, out_sh, up_sh, down_sh, *rest[1 if dense else 0 :],
    )


def forward_body(
    dense, extra_ref, lens_ref, feat_ref, col_ref, row_ref, vec_refs, cot_ref, text_ref,
    side_sh, in_sh, out_sh, up_sh, down_sh,
    w_in, w_out, w_up, w_down, emb_t, ctx_t, first_t, act_t,
    dgelu_o, xh0_o, xh1_o, gp2_o, qkv_o, rows_o,
    col_o, lse_o, vec_o, bias1_o, bias2_o, last_o, slot_o, req_o, stat_o, row_o,
    side_f, in_f, out_f, up_f, down_f,
    row_twin, stat_out, stat_twin, ask_out, ask_in, vec_s, outbox, inbox,
    text_send, text_recv, mask,
    low, wide_s, qkv, ctx_s, ctx, act, act_s, dgelu, emb_s, first_s, xh0, xh1, first, gp2, rows_s,
    own_sem, send_sem, recv_sem, twin_sem, ask_send, ask_recv, small_send, small_recv,
    text_ssem, text_rsem, text_tsend, text_trecv, two_send, two_recv,
    keep_sem, pair_send, pair_recv,
):
    rep, z, y, x = spot()
    me = at(z, y, x)
    vocab = text_ref.shape[0]
    barrier = greet()

    side_a, in_a, out_a, up_a, down_a = arrays = [
        Gather(i, sh, full, own_sem, send_sem, recv_sem, twin_sem)
        for i, (sh, full) in enumerate(
            ((side_sh, side_f), (in_sh, in_f), (out_sh, out_f), (up_sh, up_f), (down_sh, down_f))
        )
    ]

    kept = []

    def keep(source, target):
        copy = pltpu.make_async_copy(source, target, keep_sem.at[len(kept)])
        kept.append(copy)
        copy.start()

    paired = []

    def pair(source, target):
        columns = target.at[:, rows_of(rep, BLOCK, LANES)]
        keep(source, columns)
        copy = pltpu.make_async_remote_copy(
            src_ref=source,
            dst_ref=columns,
            send_sem=pair_send.at[len(paired)],
            recv_sem=pair_recv.at[len(paired)],
            device_id=(1 - rep, me),
            device_id_type=MESH,
        )
        paired.append(copy)
        copy.start()

    twins = []

    def to_twin(source, target):
        copy = pltpu.make_async_remote_copy(
            src_ref=source,
            dst_ref=target,
            send_sem=two_send.at[len(twins)],
            recv_sem=two_recv.at[len(twins)],
            device_id=(1 - rep, me),
            device_id_type=MESH,
        )
        twins.append(copy)
        copy.start()
        return copy

    valid = (members(lens_ref, (BLOCK, 1), 0) < SLOTS).astype(f32)
    count = jnp.sum(valid, axis=0, keepdims=True)
    col_o[:, 3:4] = valid

    def add_total(c, total):
        rows = rows_of(c, 64, 64)
        return total + jnp.sum(widen(feat_ref[rows, :]) * col_o[rows, 3:4], axis=0, keepdims=True)

    local = lax.fori_loop(0, 8, add_total, jnp.zeros((1, 768), f32)) / jnp.maximum(count, 1.0)

    def add_square(c, square):
        rows = rows_of(c, 64, 64)
        center = widen(feat_ref[rows, :]) - local
        return square + jnp.sum(center * center * col_o[rows, 3:4], axis=0, keepdims=True)

    square = lax.fori_loop(0, 8, add_square, jnp.zeros((1, 768), f32))

    for j in range(6):
        stat_out[j : j + 1, :] = local[:, j * LANES : (j + 1) * LANES]
        stat_out[6 + j : 7 + j, :] = square[:, j * LANES : (j + 1) * LANES]
    stat_out[12:16, :] = jnp.broadcast_to(count, (4, LANES))
    pl.semaphore_wait(barrier, 16)
    row_pair = to_twin(row_ref, row_twin)
    stat_pair = to_twin(stat_out, stat_twin)

    side_a.start_own()
    side_a.start_line()
    in_a.start_own()
    in_a.start_line()
    limit = 0 if dense else CAP
    row_pair.wait_recv()
    row_o[...] = row_twin[...]
    twin_columns = jnp.transpose(
        jnp.concatenate([widen(row_twin[...]), jnp.zeros((LANES - 8, BLOCK), f32)], axis=0)
    )
    all_c = jnp.concatenate([widen(col_ref[...]), twin_columns[:, 0:8]], axis=0)
    ids_c, base_c, owner_c = all_c[:, 0:1], all_c[:, 6:7], all_c[:, 7:8]
    ids_r = widen(jnp.concatenate([row_ref[0:1, :], row_twin[0:1, :]], axis=1))
    earlier = iota((2 * BLOCK, 1), 0) < iota((1, 2 * BLOCK), 1)
    first_r = 1.0 - jnp.max(
        jnp.where(earlier & (ids_c == ids_r), 1.0, 0.0), axis=0, keepdims=True
    )
    rank_c = jnp.sum(
        jnp.where((ids_r < ids_c) & (ids_r >= base_c), first_r, 0.0), axis=1, keepdims=True
    )
    most = jnp.max(rank_c, axis=0, keepdims=True) + 1.0
    slot_c = jnp.where(rank_c < limit, owner_c * CAP + rank_c, -1.0)
    col_o[:, 2:3] = slot_c[0:BLOCK]
    slot_o[...] = jnp.transpose(jnp.broadcast_to(slot_c[0:BLOCK], (BLOCK, LANES)))[0:8, :]
    within = ids_c - base_c
    lane = iota((1, LANES), 1).astype(f32)
    for t in range(16):
        hit = jnp.where((owner_c == t) & (rank_c < limit), rank_c, -1.0) == lane
        ask = jnp.max(jnp.where(hit, within, -1.0), axis=0, keepdims=True)
        ask_out[t] = jnp.broadcast_to(ask, (8, LANES))
    exchange(ask_out, ask_in, ask_send, ask_recv, True)
    ask_in[me] = ask_out[me]

    pieces = jnp.concatenate([widen(v[...]) for v in vec_refs], axis=1)
    for j in range(6):
        vec_s[j : j + 1, :] = pieces[:, j * LANES : (j + 1) * LANES]
    stat_pair.wait_recv()
    count_one, count_two = stat_out[12:13, :], stat_twin[12:13, :]
    both = jnp.maximum(count_one + count_two, 1.0)
    part = pl.ds(rep * 3, 3)
    part_two = pl.ds(6 + rep * 3, 3)
    mean_one, mean_two = stat_out[part, :], stat_twin[part, :]
    mean = (mean_one * count_one + mean_two * count_two) / both
    outbox[0:3, :] = mean
    outbox[3:6, :] = (
        stat_out[part_two, :]
        + stat_twin[part_two, :]
        + count_one * (mean_one - mean) * (mean_one - mean)
        + count_two * (mean_two - mean) * (mean_two - mean)
    )
    outbox[6:7, :] = jnp.where(lane == 1.0, most, count_one + count_two)
    outbox[7:10, :] = vec_s[part, :]
    outbox[10:16, :] = jnp.zeros((6, LANES), f32)
    exchange(outbox, inbox.at[rep], small_send, small_recv, True)
    inbox[rep, me] = outbox[...]
    out_a.start_own()
    up_a.start_own()
    down_a.start_own()
    same = members(lens_ref, (BLOCK, 1), 0) == members(lens_ref, (1, BLOCK), 1)
    mask[...] = jnp.where(same, 0.0, -1e30)

    side_a.hop_one()
    exchange(ask_out, ask_in, ask_send, ask_recv, False)

    asked = jnp.concatenate([ask_in[t, 0:1, :] for t in range(16)], axis=0)
    req_o[...] = asked
    asked = jnp.concatenate([asked, jnp.full((LANES - 16, LANES), -1.0, f32)], axis=0)
    asked = jnp.transpose(asked)
    column = iota((1, vocab), 1).astype(f32)
    half = rows_of(rep, 384, LANES)
    for c in range(4):
        pick = jnp.concatenate(
            [onehot(asked[:CAP, t : t + 1] == column) for t in range(4 * c, 4 * c + 4)], axis=0
        )
        text_send[c * 256 : c * 256 + 256, :] = mm(pick, text_ref[:, half]).astype(bf16)

    def text_copy(t, source):
        return pltpu.make_async_remote_copy(
            src_ref=text_send.at[rows_of(t, CAP, 16)],
            dst_ref=text_recv.at[rows_of(source, CAP, 16), half],
            send_sem=text_ssem.at[t],
            recv_sem=text_rsem.at[source],
            device_id=(rep, t),
            device_id_type=MESH,
        )

    def text_twin(source, core):
        block = text_recv.at[rows_of(source, CAP, 16), rows_of(core, 384, LANES)]
        return pltpu.make_async_remote_copy(
            src_ref=block,
            dst_ref=block,
            send_sem=text_tsend.at[source],
            recv_sem=text_trecv.at[source],
            device_id=(1 - rep, me),
            device_id_type=MESH,
        )

    def text_start(k, carry):
        text_copy(lax.rem(me + k, 16), me).start()
        return carry

    lax.fori_loop(1, 16, text_start, 0)
    out_a.start_line()
    up_a.start_line()
    text_recv[rows_of(me, CAP, 16), half] = text_send[rows_of(me, CAP, 16), :]
    text_twin(me, rep).start()

    exchange(outbox, inbox.at[rep], small_send, small_recv, False)
    to_twin(inbox.at[rep], inbox.at[rep]).wait_recv()

    def gathered(j):
        return jnp.concatenate([inbox[0, t, j : j + 1, :] for t in range(16)], axis=0)

    def gathered_half(core, j):
        return jnp.concatenate([inbox[core, t, j : j + 1, :] for t in range(16)], axis=0)

    tail = gathered(6)
    counts = tail[:, 0:1]
    all_rows = jnp.sum(counts, axis=0, keepdims=True)
    means, spreads = [], []
    for j in range(6):
        part = gathered_half(j // 3, j % 3)
        mean = jnp.sum(part * counts, axis=0, keepdims=True) / all_rows
        shift = part - mean
        variance = (
            jnp.sum(gathered_half(j // 3, 3 + j % 3) + counts * shift * shift, axis=0, keepdims=True)
            / all_rows
        )
        means.append(mean)
        spreads.append(lax.rsqrt(variance + epsilon))
    mean = jnp.concatenate(means, axis=1)
    spread = jnp.concatenate(spreads, axis=1)
    most = jnp.max(tail[:, 1:2], axis=0, keepdims=True)
    stat_o[...] = jnp.concatenate(
        [
            mean,
            spread,
            jnp.broadcast_to(all_rows, (1, 768)),
            jnp.broadcast_to(most, (1, 768)),
            jnp.zeros((4, 768), f32),
        ],
        axis=0,
    )
    packed = jnp.concatenate([gathered_half(j // 3, 7 + j % 3) for j in range(6)], axis=1)
    narrow, middle, wide = expand_vectors(packed)
    vec_o[...] = jnp.concatenate([narrow, jnp.zeros((6, 768), f32)], axis=0)
    bias1_o[...] = jnp.broadcast_to(middle, (8, 1536))
    bias2_o[...] = jnp.broadcast_to(wide, (8, 3072))


    side_a.hop_two()
    in_a.hop_one()
    side_a.last()
    side_a.ready()
    def embed(c, carry):
        rows = rows_of(c, 128, 128)
        hat = (widen(feat_ref[rows, :]) - stat_o[0:1, :]) * stat_o[1:2, :]
        begin = hat * vec_o[0:1, :] + vec_o[1:2, :]
        where = col_ref[rows, :]
        bins = iota((1, BINS), 1)
        hits = (where[:, 1:2] == bins).astype(f32) + (where[:, 2:3] == bins).astype(f32)
        begin = begin + mm(hits.astype(bf16), side_f[0:BINS, :])
        hits = (where[:, 3:4] == bins).astype(f32) + (where[:, 4:5] == bins).astype(f32)
        begin = begin + mm(hits.astype(bf16), side_f[BINS : 2 * BINS, :])
        segments = iota((1, SIDE - 2 * BINS), 1)
        begin = begin + mm(onehot(where[:, 5:6] == segments), side_f[2 * BINS :, :])
        if dense:
            begin = begin + widen(extra_ref[rows, :])
        wide_s[rows, :] = begin
        return carry

    lax.fori_loop(0, 4, embed, 0)

    in_a.hop_two()
    out_a.hop_one()
    in_a.last()
    def text_wait(k, carry):
        there = lax.rem(me + k, 16)
        text_copy(there, there).wait_recv()
        text_twin(there, rep).start()
        return carry

    lax.fori_loop(1, 16, text_wait, 0)

    def text_ready(k, carry):
        text_twin(k, 1 - rep).wait_recv()
        return carry

    lax.fori_loop(0, 16, text_ready, 0)

    down_a.start_line()
    def embed_norm(c, carry):
        rows = rows_of(c, 128, 128)
        slots = iota((1, 16 * CAP), 1).astype(f32)
        begin = wide_s[rows, :] + mm(onehot(col_o[rows, 2:3] == slots), text_recv[...])
        center = begin - jnp.mean(begin, axis=-1, keepdims=True)
        scale = spread_rows(center)
        hat = center * scale
        xh0[rows, :] = hat
        col_o[rows, 0:1] = scale
        value = hat * vec_o[2:3, :] + vec_o[3:4, :]
        wide_s[rows, :] = value
        low[rows, :] = value.astype(bf16)
        return carry

    lax.fori_loop(0, 4, embed_norm, 0)
    keep(xh0, xh0_o)
    transpose_to(emb_s, low)
    pair(emb_s, emb_t)
    out_a.hop_two()
    up_a.hop_one()
    in_a.ready()
    keep(in_f, w_in)

    def project(i, carry):
        columns = rows_of(i, 256, 256)
        qkv[:, columns] = mm(low[...], in_f[:, columns]).astype(bf16)
        return carry

    def project_biased(i, carry):
        columns = rows_of(i, 256, 256)
        source = rows_of(lax.rem(i, 6), 256, 256)
        qkv[:, columns] = (mm(low[...], in_f[:, columns]) + bias1_o[0:1, source]).astype(bf16)
        return carry

    lax.fori_loop(0, 3, project_biased, 0)
    lax.fori_loop(3, 6, project, 0)

    def project_values(i, carry):
        columns = rows_of(i + 6, 256, 256)
        source = rows_of(i + 3, 256, 256)
        qkv[:, columns] = (mm(low[...], in_f[:, columns]) + bias1_o[0:1, source]).astype(bf16)
        return carry

    lax.fori_loop(0, 3, project_values, 0)
    keep(qkv, qkv_o)

    def attend(p, carry):
        query = qkv[:, rows_of(p, LANES, LANES)]
        keys = qkv[:, rows_of(p + 6, LANES, LANES)]
        values = jnp.transpose(qkv[:, rows_of(p + 12, LANES, LANES)])
        for head in range(2):
            low_lanes = iota((1, LANES), 1) // HEAD == head
            masked = query * jnp.where(low_lanes, 0.125, 0.0).astype(bf16)
            for part in range(2):
                scores = mm_nt(keys, masked[part * 256 : part * 256 + 256, :])
                scores = scores + mask[:, part * 256 : part * 256 + 256]
                top = jnp.max(scores, axis=0, keepdims=True)
                expo = jnp.exp(scores - top)
                total = jnp.sum(expo, axis=0, keepdims=True)
                got = mm(values[head * HEAD : (head + 1) * HEAD, :], expo.astype(bf16))
                ctx_s[
                    pl.ds(pl.multiple_of(p * LANES + head * HEAD, HEAD), HEAD),
                    part * 256 : part * 256 + 256,
                ] = (got * (1.0 / total)).astype(bf16)
                lse_o[pl.ds(2 * p + head, 1), part * 256 : part * 256 + 256] = top + jnp.log(total)
        ctx[:, rows_of(p, LANES, LANES)] = jnp.transpose(ctx_s[rows_of(p, LANES, LANES), :])

        @pl.when(p < 4)
        def _():
            up_a.two(p)

        @pl.when(p >= 2)
        def _():
            @pl.when(p < 5)
            def _():
                down_a.one(p - 1)

        return carry

    lax.fori_loop(0, 6, attend, 0)
    lse_o[12:16, :] = jnp.zeros((4, BLOCK), f32)
    pair(ctx_s, ctx_t)
    out_a.last()
    out_a.ready()
    keep(out_f, w_out)

    def attention_norm(c, carry):
        rows = rows_of(c, 128, 128)
        value = wide_s[rows, :] + mm(ctx[rows, :], out_f[...]) + vec_o[4:5, :]
        center = value - jnp.mean(value, axis=-1, keepdims=True)
        scale = spread_rows(center)
        hat = center * scale
        xh1[rows, :] = hat
        col_o[rows, 1:2] = scale
        value = hat * vec_o[5:6, :] + vec_o[6:7, :]
        first[rows, :] = value
        low[rows, :] = value.astype(bf16)
        up_a.three(c)
        return carry

    lax.fori_loop(0, 4, attention_norm, 0)
    keep(xh1, xh1_o)
    transpose_to(first_s, low)
    pair(first_s, first_t)
    up_a.ready()
    keep(up_f, w_up)

    def feed(i, carry):
        columns = rows_of(i, 256, 256)
        hidden = mm(low[...], up_f[:, columns]) + bias2_o[0:1, columns]
        part = 0.5 + 0.5 * lax.erf(hidden * (1.0 / math.sqrt(2.0)))
        value = (hidden * part).astype(bf16)
        act[:, columns] = value
        act_s[columns, :] = jnp.transpose(value)
        bell = jnp.exp(hidden * hidden * -0.5) * (1.0 / math.sqrt(2.0 * math.pi))
        dgelu[:, columns] = (part + hidden * bell).astype(bf16)

        @pl.when(lax.rem(i, 3) == 2)
        def _():
            down_a.two(i // 3)

        return carry

    lax.fori_loop(0, 12, feed, 0)
    keep(dgelu, dgelu_o)
    pair(act_s, act_t)
    down_a.last()
    down_a.ready()
    keep(down_f, w_down)

    def second_part(i, carry):
        columns = rows_of(i, 256, 256)
        wide_s[:, columns] = mm(act[...], down_f[:, columns]) + vec_o[7:8, columns]
        return carry

    lax.fori_loop(0, 3, second_part, 0)

    def last_norm(c, carry):
        rows = rows_of(c, 128, 128)
        value = first[rows, :] + wide_s[rows, :]
        center = value - jnp.mean(value, axis=-1, keepdims=True)
        scale = spread_rows(center)
        hat = center * scale
        rows_s[rows, :] = (hat * vec_o[8:9, :] + vec_o[9:10, :]).astype(bf16)
        grad = widen(cot_ref[rows, :]) * col_o[rows, 3:4]
        gained = grad * vec_o[8:9, :]
        gp2[rows, :] = scale * (
            gained
            - jnp.mean(gained, axis=-1, keepdims=True)
            - hat * jnp.mean(gained * hat, axis=-1, keepdims=True)
        )
        gain, bias = carry
        return (
            gain + jnp.sum(grad * hat, axis=0, keepdims=True),
            bias + jnp.sum(grad, axis=0, keepdims=True),
        )

    zero = jnp.zeros((1, 768), f32)
    gain, bias = lax.fori_loop(0, 4, last_norm, (zero, zero))
    last_o[...] = jnp.concatenate([gain, bias, jnp.zeros((6, 768), f32)], axis=0)
    keep(gp2, gp2_o)
    keep(rows_s, rows_o)

    for a in arrays:
        a.drain()

    def text_drain(k, carry):
        text_copy(lax.rem(me + k, 16), me).wait_send()
        return carry

    lax.fori_loop(1, 16, text_drain, 0)

    def twin_drain(k, carry):
        text_twin(k, rep).wait_send()
        return carry

    lax.fori_loop(0, 16, twin_drain, 0)
    for copy in twins:
        copy.wait_send()
    for copy in paired:
        copy.wait_send()
        copy.wait_recv()
    for copy in kept:
        copy.wait()


def shape(*dims, dtype=f32):
    return jax.ShapeDtypeStruct(dims, dtype)


def forward_call(lens, feat, col, row, vec, cot, text, side, w_in, w_out, w_up, w_down, extra=None):
    dense = extra is not None
    vm, hbm = pl.BlockSpec(memory_space=pltpu.VMEM), pl.BlockSpec(memory_space=pl.ANY)
    sm = pl.BlockSpec(memory_space=pltpu.SMEM)
    full = [(16 * w.shape[0], w.shape[1]) for w in (side, w_in, w_out, w_up, w_down)]
    out_shape = (
        *(shape(*dims, dtype=bf16) for dims in full[1:]),
        shape(768, 1024, dtype=bf16), shape(768, 1024, dtype=bf16), shape(768, 1024, dtype=bf16),
        shape(3072, 1024, dtype=bf16),
        shape(BLOCK, 3072, dtype=bf16),
        shape(BLOCK, 768), shape(BLOCK, 768), shape(BLOCK, 768),
        shape(BLOCK, 2304, dtype=bf16), shape(BLOCK, 768, dtype=bf16),
        shape(BLOCK, LANES), shape(16, BLOCK), shape(16, 768), shape(8, 1536), shape(8, 3072),
        shape(8, 768), shape(8, BLOCK), shape(16, LANES), shape(8, 768),
        shape(8, BLOCK, dtype=jnp.int32),
    )
    v = lambda *dims, dtype=bf16: pltpu.VMEM(dims, dtype)
    dma = pltpu.SemaphoreType.DMA
    return pl.pallas_call(
        functools.partial(forward_kernel, dense),
        name="forward_dense" if dense else "forward",
        out_shape=out_shape,
        in_specs=[sm] + [vm] * 17 + [hbm] * 5 + [vm] * dense,
        out_specs=tuple([hbm] * 14 + [vm] * 10),
        scratch_shapes=[
            *(v(*dims) for dims in full),
            pltpu.VMEM((8, BLOCK), jnp.int32), v(16, LANES, dtype=f32), v(16, LANES, dtype=f32),
            v(16, 8, LANES, dtype=f32), v(16, 8, LANES, dtype=f32), v(8, LANES, dtype=f32),
            v(16, LANES, dtype=f32), v(2, 16, 16, LANES, dtype=f32),
            v(16 * CAP, 384), v(16 * CAP, 768), v(BLOCK, BLOCK, dtype=f32),
            v(BLOCK, 768), v(BLOCK, 768, dtype=f32), v(BLOCK, 2304), v(768, BLOCK), v(BLOCK, 768),
            v(BLOCK, 3072), v(3072, BLOCK), v(BLOCK, 3072), v(768, BLOCK), v(768, BLOCK),
            v(BLOCK, 768, dtype=f32), v(BLOCK, 768, dtype=f32), v(BLOCK, 768, dtype=f32),
            v(BLOCK, 768, dtype=f32), v(BLOCK, 768),
            dma((5,)), dma((5, 32)), dma((5, 16)), dma((5, 16)), dma((16,)), dma((16,)), dma((16,)), dma((16,)),
            dma((16,)), dma((16,)), dma((16,)), dma((16,)), dma((3,)), dma((3,)), dma((14,)), dma((4,)), dma((4,)),
        ],
        compiler_params=pltpu.CompilerParams(
            collective_id=2 if dense else 0, has_side_effects=True, vmem_limit_bytes=62 * 2**20
        ),
    )(lens, feat, col, row, *vec, cot, text, side, w_in, w_out, w_up, w_down, *([extra] if dense else []))


def pack_indices(text_ids, boxes, segment_ids, vocab):
    owner = text_ids // vocab
    return jnp.stack(
        [
            text_ids, boxes[:, 0], boxes[:, 2], boxes[:, 1], boxes[:, 3], segment_ids,
            owner * vocab, owner,
        ],
        axis=1,
    )


def norm_rows(value, gain, shift):
    center = value - jnp.mean(value, axis=-1, keepdims=True)
    spread = lax.rsqrt(jnp.mean(center * center, axis=-1, keepdims=True) + epsilon)
    return center * spread * gain + shift


def gelu_exact(value):
    return jax.nn.gelu(value, approximate=False)


def block_scores(query, keys, member):
    query_heads = query.reshape(BLOCK, -1, HEAD)
    key_heads = keys.reshape(BLOCK, -1, HEAD)
    scores = (
        jnp.einsum("qhd,khd->hqk", query_heads, key_heads, preferred_element_type=jnp.float32)
        * 0.125
    )
    same = member[:, None] == member[None, :]
    return jnp.where(same[None], scores, -1e30)


def attend_forward(operands):
    query, keys, values, member = operands
    scores = block_scores(query, keys, member)
    top = jnp.max(scores, axis=-1, keepdims=True)
    expo = jnp.exp(scores - top)
    total = jnp.sum(expo, axis=-1, keepdims=True)
    probs_low = (expo / total).astype(jnp.bfloat16)
    context = jnp.einsum(
        "hqk,khd->qhd",
        probs_low,
        values.reshape(BLOCK, -1, HEAD),
        preferred_element_type=jnp.float32,
    )
    return (context.reshape(BLOCK, -1).astype(jnp.bfloat16), top + jnp.log(total))


def attend_backward(operands):
    query, keys, values, member, logsum, grad_context = operands
    scores = block_scores(query, keys, member)
    probs = jnp.exp(scores - logsum)
    probs_low = probs.astype(jnp.bfloat16)
    value_heads = values.reshape(BLOCK, -1, HEAD)
    grad_heads = grad_context.reshape(BLOCK, -1, HEAD)
    grad_values = jnp.einsum(
        "hqk,qhd->khd", probs_low, grad_heads, preferred_element_type=jnp.float32
    )
    grad_probs = jnp.einsum(
        "qhd,khd->hqk", grad_heads, value_heads, preferred_element_type=jnp.float32
    )
    delta = jnp.sum(grad_probs * probs, axis=-1, keepdims=True)
    grad_scores = (probs * (grad_probs - delta)).astype(jnp.bfloat16)
    grad_query = (
        jnp.einsum(
            "hqk,khd->qhd",
            grad_scores,
            keys.reshape(BLOCK, -1, HEAD),
            preferred_element_type=jnp.float32,
        )
        * 0.125
    )
    grad_keys = (
        jnp.einsum(
            "hqk,qhd->khd",
            grad_scores,
            query.reshape(BLOCK, -1, HEAD),
            preferred_element_type=jnp.float32,
        )
        * 0.125
    )
    joined = jnp.concatenate(
        [
            grad_query.reshape(BLOCK, -1),
            grad_keys.reshape(BLOCK, -1),
            grad_values.reshape(BLOCK, -1),
        ],
        axis=1,
    )
    return joined.astype(jnp.bfloat16)


def general(
    region_features,
    text_ids,
    boxes,
    segment_ids,
    document_lengths,
    cotangent,
    batch_gain,
    batch_bias,
    text_table,
    side_table,
    embed_gain,
    embed_bias,
    in_weight,
    in_bias,
    out_weight,
    out_bias,
    first_gain,
    first_bias,
    up_weight,
    up_bias,
    down_weight,
    down_bias,
    second_gain,
    second_bias,
):
    rows_here, width = region_features.shape
    blocks_here = document_lengths.shape[0]
    vocab_here = text_table.shape[0]
    ends = jnp.cumsum(document_lengths, axis=1)
    place = jnp.arange(BLOCK, dtype=jnp.int32)
    member = jnp.sum((place[None, :, None] >= ends[:, None, :]).astype(jnp.int32), axis=2)
    valid = (member < SLOTS).astype(jnp.float32).reshape(rows_here, 1)
    shards = lax.axis_size("shard")
    vectors = (
        batch_gain, batch_bias, embed_gain, embed_bias, in_bias, out_bias, first_gain, first_bias,
        up_bias, down_bias, second_gain, second_bias,
    )
    sizes = [v.shape[0] for v in vectors]
    marks = [sum(sizes[:k]) for k in range(len(sizes) + 1)]
    joined = lax.all_gather(jnp.concatenate(vectors), "shard", axis=0)
    (
        full_batch_gain,
        full_batch_bias,
        full_embed_gain,
        full_embed_bias,
        full_in_bias,
        full_out_bias,
        full_first_gain,
        full_first_bias,
        full_up_bias,
        full_down_bias,
        full_second_gain,
        full_second_bias,
    ) = [joined[:, low:high].reshape(-1) for low, high in zip(marks, marks[1:])]
    full_side, full_in_weight, full_out_weight, full_up_weight, full_down_weight = [
        lax.all_gather(w, "shard", axis=0, tiled=True)
        for w in (side_table, in_weight, out_weight, up_weight, down_weight)
    ]
    features = widen(region_features)
    masked = features * valid
    total, count = lax.psum((jnp.sum(masked, axis=0), jnp.sum(valid)), ("rep", "shard"))
    mean = total / count
    center = features - mean
    variance = lax.psum(jnp.sum(center * center * valid, axis=0), ("rep", "shard")) / count
    spread = lax.rsqrt(variance + epsilon)
    batch_hat = center * spread
    gain_wide = widen(full_batch_gain)
    batch_out = batch_hat * gain_wide + widen(full_batch_bias)
    piece = lax.all_gather(text_table, "shard", axis=0, tiled=True)
    add_column = jnp.arange(piece.shape[0], dtype=jnp.int32)
    onehot = (text_ids[:, None] == add_column[None, :]).astype(jnp.bfloat16)
    text_rows = jnp.dot(onehot, piece, preferred_element_type=jnp.float32)
    side_column = jnp.arange(SIDE, dtype=jnp.int32)
    hits = jnp.zeros((rows_here, SIDE), jnp.float32)
    for column in (
        boxes[:, 0],
        boxes[:, 2],
        boxes[:, 1] + BINS,
        boxes[:, 3] + BINS,
        segment_ids + 2 * BINS,
    ):
        hits = hits + (column[:, None] == side_column[None, :]).astype(jnp.float32)
    hits_low = hits.astype(jnp.bfloat16)
    looked = text_rows + jnp.dot(hits_low, full_side, preferred_element_type=jnp.float32)
    start_rows = batch_out + looked
    embedded, back_embed = jax.vjp(
        norm_rows, start_rows, widen(full_embed_gain), widen(full_embed_bias)
    )
    embedded_low = embedded.astype(jnp.bfloat16)
    mixed = jnp.dot(embedded_low, full_in_weight, preferred_element_type=jnp.float32)
    bias_wide = widen(full_in_bias)
    query = (mixed[:, :width] + bias_wide[:width]).astype(jnp.bfloat16)
    keys = mixed[:, width : 2 * width].astype(jnp.bfloat16)
    values = (mixed[:, 2 * width :] + bias_wide[width:]).astype(jnp.bfloat16)
    shaped = (
        query.reshape(blocks_here, BLOCK, width),
        keys.reshape(blocks_here, BLOCK, width),
        values.reshape(blocks_here, BLOCK, width),
    )
    context, logsum = lax.map(attend_forward, shaped + (member,))
    context = context.reshape(rows_here, width)
    branch = jnp.dot(context, full_out_weight, preferred_element_type=jnp.float32) + widen(
        full_out_bias
    )
    first, back_first = jax.vjp(
        norm_rows, embedded + branch, widen(full_first_gain), widen(full_first_bias)
    )
    first_low = first.astype(jnp.bfloat16)
    hidden = jnp.dot(first_low, full_up_weight, preferred_element_type=jnp.float32) + widen(
        full_up_bias
    )
    gelu_value, gelu_back = jax.vjp(gelu_exact, hidden)
    active = gelu_value.astype(jnp.bfloat16)
    second = jnp.dot(active, full_down_weight, preferred_element_type=jnp.float32) + widen(
        full_down_bias
    )
    final, back_second = jax.vjp(
        norm_rows, first + second, widen(full_second_gain), widen(full_second_bias)
    )
    out_rows = final.astype(jnp.bfloat16)
    grad_final = widen(cotangent) * valid
    grad_pre2, grad_second_gain, grad_second_bias = back_second(grad_final)
    grad_second = grad_pre2.astype(jnp.bfloat16)
    grad_down_weight = jnp.einsum(
        "rf,rd->fd", active, grad_second, preferred_element_type=jnp.float32
    )
    grad_down_bias = jnp.sum(widen(grad_second), axis=0)
    grad_active = jnp.einsum(
        "rd,fd->rf", grad_second, full_down_weight, preferred_element_type=jnp.float32
    )
    grad_hidden = gelu_back(grad_active)[0].astype(jnp.bfloat16)
    grad_up_weight = jnp.einsum(
        "rd,rf->df", first_low, grad_hidden, preferred_element_type=jnp.float32
    )
    grad_up_bias = jnp.sum(widen(grad_hidden), axis=0)
    grad_first = grad_pre2 + jnp.einsum(
        "rf,df->rd", grad_hidden, full_up_weight, preferred_element_type=jnp.float32
    )
    grad_pre1, grad_first_gain, grad_first_bias = back_first(grad_first)
    grad_branch = grad_pre1.astype(jnp.bfloat16)
    grad_out_weight = jnp.einsum(
        "rd,re->de", context, grad_branch, preferred_element_type=jnp.float32
    )
    grad_out_bias = jnp.sum(widen(grad_branch), axis=0)
    grad_context = jnp.einsum(
        "re,de->rd", grad_branch, full_out_weight, preferred_element_type=jnp.float32
    ).astype(jnp.bfloat16)
    grad_mixed = lax.map(
        attend_backward, shaped + (member, logsum, grad_context.reshape(blocks_here, BLOCK, width))
    )
    grad_mixed = grad_mixed.reshape(rows_here, 3 * width)
    grad_in_weight = jnp.einsum(
        "rd,re->de", embedded_low, grad_mixed, preferred_element_type=jnp.float32
    )
    column_sums = jnp.sum(widen(grad_mixed), axis=0)
    grad_in_bias = jnp.concatenate([column_sums[:width], column_sums[2 * width :]])
    grad_embedded = grad_pre1 + jnp.einsum(
        "re,de->rd", grad_mixed, full_in_weight, preferred_element_type=jnp.float32
    )
    grad_start, grad_embed_gain, grad_embed_bias = back_embed(grad_embedded)
    grad_looked = grad_start.astype(jnp.bfloat16)
    column = jnp.arange(lax.axis_size("shard") * vocab_here, dtype=jnp.int32)
    onehot = (column[:, None] == text_ids[None, :]).astype(jnp.bfloat16)
    text_grad = lax.psum_scatter(
        jnp.dot(onehot, grad_looked, preferred_element_type=jnp.float32),
        "shard",
        scatter_dimension=0,
        tiled=True,
    )
    grad_side = jnp.einsum("rs,rd->sd", hits_low, grad_looked, preferred_element_type=jnp.float32)
    shift_sum, scale_sum = lax.psum(
        (jnp.sum(grad_start * valid, axis=0), jnp.sum(grad_start * batch_hat * valid, axis=0)),
        ("rep", "shard"),
    )
    feature_grad = (
        valid
        * gain_wide
        * spread
        * (grad_start - shift_sum / count - batch_hat * scale_sum / count)
    ).astype(jnp.bfloat16)
    small = (
        scale_sum / lax.axis_size(("rep", "shard")),
        shift_sum / lax.axis_size(("rep", "shard")),
        grad_embed_gain, grad_embed_bias, grad_in_bias, grad_out_bias, grad_first_gain,
        grad_first_bias, grad_up_bias, grad_down_bias, grad_second_gain, grad_second_bias,
    )
    joined = jnp.concatenate([v.reshape(shards, -1) for v in small], axis=1).reshape(-1)
    owned = [
        lax.psum_scatter(value, "shard", scatter_dimension=0, tiled=True)
        for value in (
            grad_side, grad_in_weight, grad_out_weight, grad_up_weight, grad_down_weight, joined
        )
    ]
    side_grad, in_weight_grad, out_weight_grad, up_weight_grad, down_weight_grad = [
        widen(v) for v in lax.psum(tuple(v.astype(jnp.bfloat16) for v in owned[:5]), "rep")
    ]
    text_table_grad = widen(lax.psum(text_grad.astype(jnp.bfloat16), "rep"))
    pieces = lax.psum(owned[5], "rep")
    (
        batch_gain_grad,
        batch_bias_grad,
        embed_gain_grad,
        embed_bias_grad,
        in_bias_grad,
        out_bias_grad,
        first_gain_grad,
        first_bias_grad,
        up_bias_grad,
        down_bias_grad,
        second_gain_grad,
        second_bias_grad,
    ) = [pieces[low:high] for low, high in zip(marks, marks[1:])]
    return (
        out_rows,
        feature_grad,
        batch_gain_grad,
        batch_bias_grad,
        text_table_grad,
        side_grad,
        embed_gain_grad,
        embed_bias_grad,
        in_weight_grad,
        in_bias_grad,
        out_weight_grad,
        out_bias_grad,
        first_gain_grad,
        first_bias_grad,
        up_weight_grad,
        up_bias_grad,
        down_weight_grad,
        down_bias_grad,
        second_gain_grad,
        second_bias_grad,
    )


class Scatter:
    def __init__(self, index, total, near, relay, line, done, out, sems):
        self.index, self.total, self.near, self.relay, self.line = index, total, near, relay, line
        self.done, self.out = done, out
        self.send_sem, self.near_sem, self.relay_sem, self.line_sem, self.twin_sem, self.keep_sem = sems
        self.rep, self.z, self.y, self.x = spot()
        self.me = at(self.z, self.y, self.x)
        self.rows, self.half = near.shape[1], near.shape[2]

    def rows_at(self, source):
        return rows_of(source, self.rows, 16)

    def beside(self, plane, swap):
        even = lax.rem(plane + self.y + self.x + swap, 2) == 0
        return jnp.where(even, self.y, 1 - self.y), jnp.where(even, 1 - self.x, self.x)

    def copy(self, source, slot, target, dst, recv_sem):
        return pltpu.make_async_remote_copy(
            src_ref=self.total.at[self.rows_at(source)],
            dst_ref=dst,
            send_sem=self.send_sem.at[self.index, slot],
            recv_sem=recv_sem,
            device_id=(self.rep, target),
            device_id_type=MESH,
        )

    def near_copy(self, plane, kind):
        y, x = self.beside(plane, kind)
        target = at(self.z, y, x)
        source = at(plane, y, x) if kind == 0 else at(plane, 1 - self.y, 1 - self.x)
        slot = 2 * plane + kind
        return self.copy(
            source, slot, target, self.near.at[slot], self.near_sem.at[self.index, slot]
        )

    def relay_copy(self, plane):
        y, x = self.beside(plane, 1)
        return self.copy(
            at(plane, y, x), 8 + plane, at(self.z, y, x), self.relay.at[plane],
            self.relay_sem.at[self.index, plane],
        )

    def line_copy(self, plane):
        there = at(plane, self.y, self.x)
        return self.copy(
            there, 12 + plane, there, self.line.at[self.z], self.line_sem.at[self.index, self.z]
        )

    def line_wait(self, plane):
        self.copy(
            self.me, 12 + plane, self.me, self.line.at[plane], self.line_sem.at[self.index, plane]
        ).wait_recv()

    def hop_one(self):
        def step(k, carry):
            plane = lax.rem(self.z + k + 1, 4)
            self.near_copy(plane, 1).start()
            return carry

        lax.fori_loop(0, 4, step, 0)

        def again(k, carry):
            plane = lax.rem(self.z + k + 1, 4)
            self.near_copy(plane, 0).start()
            return carry

        lax.fori_loop(0, 4, again, 0)

    def two(self, k):
        plane = lax.rem(self.z + k + 1, 4)
        self.near_copy(plane, 1).wait_recv()
        y, x = self.beside(plane, 1)
        rows = self.rows_at(at(plane, y, x))
        self.total[rows, :] = (
            widen(self.total[rows, :]) + widen(self.near[2 * plane + 1])
        ).astype(bf16)
        self.relay_copy(plane).start()

    def three(self, k):
        plane = lax.rem(self.z + k + 1, 4)
        self.near_copy(plane, 0).wait_recv()
        self.relay_copy(plane).wait_recv()
        rows = self.rows_at(at(plane, self.y, self.x))
        self.total[rows, :] = (
            widen(self.total[rows, :]) + widen(self.near[2 * plane]) + widen(self.relay[plane])
        ).astype(bf16)

        @pl.when(k < 3)
        def _():
            self.line_copy(plane).start()

    def hop_two(self):
        each(0, 4, self.two)

    def hop_three(self):
        each(0, 4, self.three)

    def finals(self):
        columns = rows_of(self.rep, self.half, LANES)
        return (
            pltpu.make_async_copy(
                self.done, self.out.at[:, columns], self.keep_sem.at[self.index]
            ),
            pltpu.make_async_remote_copy(
                src_ref=self.done,
                dst_ref=self.out.at[:, columns],
                send_sem=self.send_sem.at[self.index, 16],
                recv_sem=self.twin_sem.at[self.index],
                device_id=(1 - self.rep, self.me),
                device_id_type=MESH,
            ),
        )

    def finish(self):
        rows = self.rows_at(self.me)
        self.done[...] = widen(self.total[rows, :])

        def add(k, carry):
            plane = lax.rem(self.z + k, 4)
            self.line_wait(plane)
            self.done[...] = self.done[...] + widen(self.line[plane])
            return carry

        lax.fori_loop(1, 4, add, 0)
        for copy in self.finals():
            copy.start()

    def drain(self):
        def step(k, carry):
            self.near_copy(k, 0).wait_send()
            self.near_copy(k, 1).wait_send()
            self.relay_copy(k).wait_send()

            @pl.when(k != self.z)
            def _():
                self.line_copy(k).wait_send()

            return carry

        lax.fori_loop(0, 4, step, 0)
        kept, twin = self.finals()
        kept.wait()
        twin.wait_send()
        twin.wait_recv()


def compress_vectors(narrow, middle, wide):
    shard_of = iota((16, 1), 0).astype(f32)
    owner, _ = remainder((1, 768), 1, 0, 48)
    stacked = jnp.concatenate(
        [jnp.where(owner == shard_of, narrow[k : k + 1, :], 0.0) for k in range(10)], axis=0
    ).astype(bf16)
    _, depth = remainder((768, 1), 0, 0, 48)
    _, want = remainder((1, 768), 1, 0, 48)
    spread = mm(stacked, onehot(depth == want))
    packed = sum(
        jnp.where(owner == k, spread[k * 16 : k * 16 + 16], 0.0) for k in range(10)
    )

    def piece(row, low, offset, size):
        total = size * 16
        holder, _ = remainder((1, total), 1, 0, size)
        _, place = remainder((total, 1), 0, 0, size)
        lane = iota((1, 256), 1).astype(f32) + (low - offset)
        return mm(jnp.where(holder == shard_of, row, 0.0).astype(bf16), onehot(place == lane))

    packed = packed + jnp.concatenate(
        [jnp.zeros((16, 384), f32), piece(middle, 384, 480, 96), jnp.zeros((16, 128), f32)], axis=1
    )
    return packed + jnp.concatenate(
        [jnp.zeros((16, 512), f32), piece(wide, 512, 576, 192)], axis=1
    )


def norm_back(grad, hat, scale, gain):
    gained = grad * gain
    return scale * (
        gained
        - jnp.mean(gained, axis=-1, keepdims=True)
        - hat * jnp.mean(gained * hat, axis=-1, keepdims=True)
    )


def backward_kernel(
    lens_ref, feat_ref, row_ref, twin_ref, cols_ref, lse_ref, vec_ref, last_ref, slot_ref, req_ref, stat_ref,
    w_in, w_out, w_up, w_down, emb_t, ctx_t, first_t, act_t, dgelu_h, xh0_h, xh1_h, gp2_h, qkv_h,
    feat_o, looked_o, text_o, side_o, in_o, out_o, up_o, down_o, vec_o,
    w_in_s, w_out_s, act_b, down_b, up_b, dgelu_b, ctx_s, first_s, xh1, grad, qkv,
    low, low_twin, hidden, hidden_twin, branch, branch_twin, gctx, mixed, mixed_twin,
    looked, looked_twin,
    down_g, up_g, out_g, in_g, side_g,
    down_n, up_n, out_n, in_n, side_n,
    down_r, up_r, out_r, in_r, side_r,
    down_l, up_l, out_l, in_l, side_l,
    down_d, up_d, out_d, in_d, side_d,
    text_u, text_twin, text_half, text_in, ask_s, mask, vectors, in_row, up_row,
    chip_out, chip_in, outbox, inbox, both,
    load_sem, act_sem, tile_sem, pair_send, pair_recv,
    send_sem, near_sem, relay_sem, line_sem, twin_sem, keep_sem,
    small_send, small_recv, text_ssem, text_rsem, text_keep,
):
    rep, z, y, x = spot()
    me = at(z, y, x)
    vocab = text_o.shape[0]
    barrier = greet()

    loads = {}

    def load(name, source, target):
        loads[name] = pltpu.make_async_copy(source, target, load_sem.at[len(loads)])
        loads[name].start()

    load("grad", gp2_h, grad)

    def act_copy(i):
        slot = lax.rem(i, 4)
        return pltpu.make_async_copy(
            act_t.at[rows_of(i, 256, 256)], act_b.at[slot], act_sem.at[slot]
        )

    def tile_of(i):
        return lax.rem(i + 6 * (1 - rep), 12)

    def tile_copies(i):
        slot = lax.rem(i, 4)
        tile = rows_of(tile_of(i), 256, 256)
        return (
            pltpu.make_async_copy(w_down.at[tile], down_b.at[slot], tile_sem.at[0, slot]),
            pltpu.make_async_copy(w_up.at[:, tile], up_b.at[slot], tile_sem.at[1, slot]),
            pltpu.make_async_copy(dgelu_h.at[:, tile], dgelu_b.at[slot], tile_sem.at[2, slot]),
        )

    for k in range(3):
        for copy in tile_copies(k):
            copy.start()
    for k in range(3):
        act_copy(k).start()

    sems = (send_sem, near_sem, relay_sem, line_sem, twin_sem, keep_sem)
    down_a = Scatter(0, down_g, down_n, down_r, down_l, down_d, down_o, sems)
    up_a = Scatter(1, up_g, up_n, up_r, up_l, up_d, up_o, sems)
    out_a = Scatter(2, out_g, out_n, out_r, out_l, out_d, out_o, sems)
    in_a = Scatter(3, in_g, in_n, in_r, in_l, in_d, in_o, sems)
    side_a = Scatter(4, side_g, side_n, side_r, side_l, side_d, side_o, sems)

    paired = []

    def pair(source, target):
        copy = pltpu.make_async_remote_copy(
            src_ref=source,
            dst_ref=target,
            send_sem=pair_send.at[len(paired)],
            recv_sem=pair_recv.at[len(paired)],
            device_id=(1 - rep, me),
            device_id_type=MESH,
        )
        paired.append(copy)
        copy.start()
        return copy

    def half_of(width, core):
        return rows_of(core, width // 2, LANES)

    own_columns = rows_of(rep, BLOCK, LANES)
    twin_columns = rows_of(1 - rep, BLOCK, LANES)

    same = members(lens_ref, (BLOCK, 1), 0) == members(lens_ref, (1, BLOCK), 1)
    mask[...] = jnp.where(same, 0.0, -1e30)
    vectors[...] = jnp.concatenate(
        [jnp.zeros((8, 768), f32), last_ref[0:2, :], jnp.zeros((6, 768), f32)], axis=0
    )

    loads["grad"].wait()

    def second(c, total):
        rows = rows_of(c, 128, 128)
        value = grad[rows, :].astype(bf16)
        low[rows, :] = value
        return total + jnp.sum(widen(value), axis=0, keepdims=True)

    zero = jnp.zeros((1, 768), f32)
    vectors[7:8, :] = lax.fori_loop(0, 4, second, zero)
    pl.semaphore_wait(barrier, 16)
    low_pair = pair(low.at[:, half_of(768, 1 - rep)], low_twin)

    def feed(i, carry):
        slot = lax.rem(i, 4)
        for copy in tile_copies(i):
            copy.wait()

        @pl.when(i < 9)
        def _():
            for copy in tile_copies(i + 3):
                copy.start()

        tile = rows_of(tile_of(i), 256, 256)
        value = (widen(dgelu_b[slot]) * mm_nt(low[...], down_b[slot])).astype(bf16)
        hidden[:, tile] = value
        up_row[0:1, tile] = jnp.sum(widen(value), axis=0, keepdims=True)
        grad[...] = grad[...] + mm_nt(value, up_b[slot])
        return carry

    low_pair.wait_recv()

    def down_step(i, carry):
        slot = lax.rem(i, 4)
        act_copy(i).wait()

        @pl.when(i < 9)
        def _():
            act_copy(i + 3).start()

        down_g[rows_of(i, 256, 256), :] = (
            mm(act_b[slot, :, own_columns], low[:, half_of(768, rep)])
            + mm(act_b[slot, :, twin_columns], low_twin[...])
        ).astype(bf16)
        return carry

    lax.fori_loop(0, 12, down_step, 0)
    down_a.hop_one()

    load("first", first_t, first_s)
    load("xh1", xh1_h, xh1)
    load("out", w_out, w_out_s)
    load("qkv", qkv_h, qkv)
    load("ctx", ctx_t, ctx_s)
    load("in", w_in, w_in_s)

    lax.fori_loop(0, 6, feed, 0)
    hidden_pair = pair(hidden.at[:, half_of(3072, 1 - rep)], hidden_twin)
    lax.fori_loop(6, 12, feed, 0)
    loads["first"].wait()
    hidden_pair.wait_recv()

    def up_step(i, carry):
        tile = rows_of(i, 256, 256)
        own = pl.ds(pl.multiple_of(rep * 1536 + i * 256, 256), 256)
        up_g[:, tile] = (
            mm(first_s[:, own_columns], hidden[:, own])
            + mm(first_s[:, twin_columns], hidden_twin[:, tile])
        ).astype(bf16)

        @pl.when(i >= 2)
        def _():
            down_a.two(i - 2)

        return carry

    lax.fori_loop(0, 6, up_step, 0)
    load("emb", emb_t, first_s)
    up_a.hop_one()

    loads["xh1"].wait()

    def norm_one(c, carry):
        rows = rows_of(c, 128, 128)
        value, hat = grad[rows, :], xh1[rows, :]
        back = norm_back(value, hat, cols_ref[rows, 1:2], vec_ref[5:6, :])
        grad[rows, :] = back
        rounded = back.astype(bf16)
        branch[rows, :] = rounded
        gain, bias, out = carry
        return (
            gain + jnp.sum(value * hat, axis=0, keepdims=True),
            bias + jnp.sum(value, axis=0, keepdims=True),
            out + jnp.sum(widen(rounded), axis=0, keepdims=True),
        )

    gain, bias, out = lax.fori_loop(0, 4, norm_one, (zero, zero, zero))
    load("xh0", xh0_h, xh1)
    vectors[4:5, :] = out
    vectors[5:6, :] = gain
    vectors[6:7, :] = bias
    branch_pair = pair(branch.at[:, half_of(768, 1 - rep)], branch_twin)
    loads["out"].wait()

    def context_step(i, carry):
        tile = rows_of(i, 256, 256)
        gctx[:, tile] = mm_nt(branch[...], w_out_s[tile, :]).astype(bf16)
        return carry

    lax.fori_loop(0, 3, context_step, 0)
    loads["ctx"].wait()
    branch_pair.wait_recv()

    def out_step(i, carry):
        rows = rows_of(i, 256, 256)
        out_g[rows, :] = (
            mm(ctx_s[rows, own_columns], branch[:, half_of(768, rep)])
            + mm(ctx_s[rows, twin_columns], branch_twin[...])
        ).astype(bf16)
        return carry

    lax.fori_loop(0, 3, out_step, 0)
    out_a.hop_one()

    loads["qkv"].wait()

    def attend(p, carry):
        pair_lanes = rows_of(p, LANES, LANES)
        query = qkv[:, pair_lanes]
        keys = qkv[:, rows_of(p + 6, LANES, LANES)]
        values = qkv[:, rows_of(p + 12, LANES, LANES)]
        outer = gctx[:, pair_lanes]
        keys_t = jnp.transpose(keys)
        query_t, key_parts, value_parts = [], [], []
        for head in range(2):
            in_head = iota((1, LANES), 1) // HEAD == head
            masked = query * jnp.where(in_head, 0.125, 0.0).astype(bf16)
            outer_masked = outer * jnp.where(in_head, 1.0, 0.0).astype(bf16)
            key_part = jnp.zeros((BLOCK, LANES), f32)
            value_part = jnp.zeros((BLOCK, LANES), f32)
            columns = []
            for part in range(2):
                s = slice(part * 256, part * 256 + 256)
                scores = mm_nt(keys, masked[s, :]) + mask[:, s]
                probs = jnp.exp(scores - lse_ref[pl.ds(2 * p + head, 1), s])
                grads = mm_nt(values, outer_masked[s, :])
                delta = jnp.sum(probs * grads, axis=0, keepdims=True)
                inner = (probs * (grads - delta)).astype(bf16)
                value_part = value_part + mm(probs.astype(bf16), outer[s, :])
                key_part = key_part + mm(inner, query[s, :])
                columns.append(mm(keys_t[head * HEAD : (head + 1) * HEAD, :], inner))
            query_t.append(jnp.concatenate(columns, axis=1))
            key_parts.append(key_part)
            value_parts.append(value_part)
        first_head = iota((1, LANES), 1) < HEAD
        gathered = (jnp.concatenate(query_t, axis=0) * 0.125).astype(bf16)
        mixed[:, pair_lanes] = jnp.transpose(gathered)
        mixed[:, rows_of(p + 6, LANES, LANES)] = (
            jnp.where(first_head, key_parts[0], key_parts[1]) * 0.125
        ).astype(bf16)
        mixed[:, rows_of(p + 12, LANES, LANES)] = jnp.where(
            first_head, value_parts[0], value_parts[1]
        ).astype(bf16)

        @pl.when(p < 4)
        def _():
            up_a.two(p)

        @pl.when(p >= 2)
        def _():
            down_a.three(p - 2)

        return carry

    lax.fori_loop(0, 6, attend, 0)
    out_a.hop_two()
    mixed_pair = pair(mixed.at[:, half_of(2304, 1 - rep)], mixed_twin)

    loads["in"].wait()

    def embed_step(i, carry):
        tile = rows_of(i, 256, 256)
        grad[:, tile] = grad[:, tile] + mm_nt(mixed[...], w_in_s[tile, :])
        return carry

    lax.fori_loop(0, 3, embed_step, 0)

    def bias_step(i, carry):
        tile = rows_of(i, 256, 256)
        in_row[0:1, tile] = jnp.sum(widen(mixed[:, tile]), axis=0, keepdims=True)
        return carry

    lax.fori_loop(0, 9, bias_step, 0)
    loads["emb"].wait()
    mixed_pair.wait_recv()

    def in_step(i, carry):
        tile = rows_of(i, 384, 128)
        own = pl.ds(pl.multiple_of(rep * 1152 + i * 384, 128), 384)
        in_g[:, tile] = (
            mm(first_s[:, own_columns], mixed[:, own])
            + mm(first_s[:, twin_columns], mixed_twin[:, tile])
        ).astype(bf16)
        return carry

    lax.fori_loop(0, 3, in_step, 0)
    in_a.hop_one()

    up_a.hop_three()
    loads["xh0"].wait()

    def norm_zero(c, carry):
        rows = rows_of(c, 128, 128)
        value, hat = grad[rows, :], xh1[rows, :]
        back = norm_back(value, hat, cols_ref[rows, 0:1], vec_ref[2:3, :])
        grad[rows, :] = back
        looked[rows, :] = back.astype(bf16)
        gain, bias, scales, shifts = carry
        kept = back * cols_ref[rows, 3:4]
        batch_hat = (widen(feat_ref[rows, :]) - stat_ref[0:1, :]) * stat_ref[1:2, :]
        return (
            gain + jnp.sum(value * hat, axis=0, keepdims=True),
            bias + jnp.sum(value, axis=0, keepdims=True),
            scales + jnp.sum(kept * batch_hat, axis=0, keepdims=True),
            shifts + jnp.sum(kept, axis=0, keepdims=True),
        )

    gain, bias, scales, shifts = lax.fori_loop(0, 4, norm_zero, (zero, zero, zero, zero))
    looked_local = pltpu.make_async_copy(looked, looked_o, text_keep.at[0])
    looked_local.start()
    looked_pair = pair(looked.at[:, half_of(768, 1 - rep)], looked_twin)
    vectors[0:1, :] = scales
    vectors[1:2, :] = shifts
    vectors[2:3, :] = gain
    vectors[3:4, :] = bias
    packed = compress_vectors(
        vectors[...],
        jnp.concatenate([in_row[0:1, 0:768], in_row[0:1, 1536:2304]], axis=1),
        up_row[0:1, :],
    )
    chip_out[...] = jnp.concatenate([packed, scales, shifts, jnp.zeros((6, 768), f32)], axis=0)
    chip_pair = pair(chip_out, chip_in)

    def text_sum(i, carry):
        rows = rows_of(i, 256, 256)
        place = (iota((256, 1), 0) + i * 256).astype(f32)
        text_u[rows, :] = mm(onehot(slot_ref[0:1, :] == place), looked[...]).astype(bf16)
        return carry

    lax.fori_loop(0, 16 * CAP // 256, text_sum, 0)

    text_pair_in = pair(text_u.at[:, half_of(768, 1 - rep)], text_twin)
    chip_pair.wait_recv()
    chip_in[...] = chip_out[...] + chip_in[...]
    chip_half = chip_in[:, half_of(768, rep)]
    for t in range(16):
        for j in range(3):
            lanes = slice(j * LANES, (j + 1) * LANES)
            outbox[t, j : j + 1, :] = chip_half[t : t + 1, lanes]
            outbox[t, 3 + j : 4 + j, :] = chip_half[16:17, lanes]
            outbox[t, 6 + j : 7 + j, :] = chip_half[17:18, lanes]
        outbox[t, 9:16, :] = jnp.zeros((7, LANES), f32)
    exchange(outbox, inbox, small_send, small_recv, True)
    inbox[me] = outbox[me]
    text_pair_in.wait_recv()
    for c in range(4):
        rows = slice(c * 256, c * 256 + 256)
        text_half[rows, :] = (
            widen(text_u[rows, half_of(768, rep)]) + widen(text_twin[rows, :])
        ).astype(bf16)

    def text_copy(k, source):
        there = lax.rem(me + k, 16)
        return pltpu.make_async_remote_copy(
            src_ref=text_half.at[rows_of(there, CAP, 16)],
            dst_ref=text_in.at[rows_of(source, CAP, 16)],
            send_sem=text_ssem.at[k],
            recv_sem=text_rsem.at[source],
            device_id=(rep, there),
            device_id_type=MESH,
        )

    def text_start(k, carry):
        text_copy(k, me).start()
        return carry

    lax.fori_loop(1, 16, text_start, 0)
    text_in[rows_of(me, CAP, 16), :] = text_half[rows_of(me, CAP, 16), :]

    looked_pair.wait_recv()
    for tile in range(5):
        base = tile * 512
        kinds = (1, 2) if base < BINS else (3, 4) if base < 2 * BINS else (5,)
        place = iota((512, 1), 0) + base % BINS

        def counted(ref):
            return sum((ref[k : k + 1, :] == place).astype(f32) for k in kinds).astype(bf16)

        side_g[base : base + 512, :] = (
            mm(counted(row_ref), looked[:, half_of(768, rep)])
            + mm(counted(twin_ref), looked_twin[...])
        ).astype(bf16)
    side_a.hop_one()

    out_a.hop_three()
    in_a.hop_two()
    down_a.finish()
    up_a.finish()
    _, want = remainder((1, 16 * CAP), 1, 0, CAP)
    sender, _ = remainder((1, 16 * CAP), 1, 0, CAP)
    pick = onehot(iota((LANES, 1), 0).astype(f32) == want)
    asked = req_ref[...] + 1.0
    coarse = jnp.floor(asked * (1.0 / 32.0))
    fine = asked - 32.0 * coarse
    place = 32.0 * mm(coarse.astype(bf16), pick) + mm(fine.astype(bf16), pick)
    ours = sender == iota((16, 1), 0).astype(f32)
    ask_s[0:1, :] = jnp.sum(jnp.where(ours, place, 0.0), axis=0, keepdims=True)


    side_a.hop_two()
    in_a.hop_three()
    out_a.finish()
    def text_wait(k, carry):
        text_copy(k, lax.rem(me + k, 16)).wait_recv()
        return carry

    lax.fori_loop(1, 16, text_wait, 0)

    part = vocab // 2

    def text_step(i, carry):
        rows = rows_of(i, 96, 32)
        for k in range(2):
            place = (iota((96, 1), 0) + (i * 96 + 1 + k * part)).astype(f32)
            xh1[rows, k * 384 : k * 384 + 384] = mm(
                onehot(ask_s[0:1, :] == place), text_in[...]
            )
        return carry

    lax.fori_loop(0, part // 96, text_step, 0)
    text_local, text_pairs = [], []
    for k in range(2):
        source = xh1.at[0:part, k * 384 : k * 384 + 384]
        target = text_o.at[k * part : k * part + part, half_of(768, rep)]
        text_local.append(pltpu.make_async_copy(source, target, text_keep.at[2 + k]))
        text_local[k].start()
        text_pairs.append(pair(source, target))

    side_a.hop_three()
    exchange(outbox, inbox, small_send, small_recv, False)
    both[rep] = sum(inbox[t] for t in range(16))
    both_pair = pair(both.at[rep], both.at[rep])
    both_pair.wait_recv()
    vec_o[...] = jnp.concatenate([both[0, 0:3, :], both[1, 0:3, :], jnp.zeros((2, LANES), f32)], axis=0)
    scale_row = jnp.concatenate(
        [both[j // 3, 3 + j % 3 : 4 + j % 3, :] for j in range(6)], axis=1
    )
    shift_row = jnp.concatenate(
        [both[j // 3, 6 + j % 3 : 7 + j % 3, :] for j in range(6)], axis=1
    )
    scale_row = scale_row / stat_ref[2:3, :]
    shift_row = shift_row / stat_ref[2:3, :]

    def feature(c, carry):
        rows = rows_of(c, 128, 128)
        batch_hat = (widen(feat_ref[rows, :]) - stat_ref[0:1, :]) * stat_ref[1:2, :]
        value = grad[rows, :] - shift_row - batch_hat * scale_row
        gctx[rows, :] = (
            cols_ref[rows, 3:4] * (vec_ref[0:1, :] * stat_ref[1:2, :]) * value
        ).astype(bf16)
        return carry

    lax.fori_loop(0, 4, feature, 0)
    feat_local = pltpu.make_async_copy(gctx, feat_o, text_keep.at[1])
    feat_local.start()

    in_a.finish()
    side_a.finish()
    for a in (down_a, up_a, out_a, in_a, side_a):
        a.drain()

    def text_drain(k, carry):
        text_copy(k, me).wait_send()
        return carry

    lax.fori_loop(1, 16, text_drain, 0)
    for copy in paired:
        copy.wait_send()
    for k in range(2):
        text_pairs[k].wait_recv()
        text_local[k].wait()
    feat_local.wait()
    looked_local.wait()


def backward_call(lens, feat, row, made, vocab):
    (
        w_in, w_out, w_up, w_down, emb_t, ctx_t, first_t, act_t, dgelu, xh0, xh1, gp2, qkv, _,
        cols, lse, vec, _, _, last, slot, req, stat, twin,
    ) = made
    vm, hbm = pl.BlockSpec(memory_space=pltpu.VMEM), pl.BlockSpec(memory_space=pl.ANY)
    sm = pl.BlockSpec(memory_space=pltpu.SMEM)
    v = lambda *dims, dtype=bf16: pltpu.VMEM(dims, dtype)
    dma = pltpu.SemaphoreType.DMA
    parts = [(192, 384), (48, 1536), (48, 384), (48, 1152), (160, 384)]
    return pl.pallas_call(
        backward_kernel,
        name="backward",
        out_shape=(
            shape(BLOCK, 768, dtype=bf16), shape(BLOCK, 768, dtype=bf16), shape(vocab, 768), shape(160, 768), shape(48, 2304),
            shape(48, 768), shape(48, 3072), shape(192, 768), shape(8, LANES),
        ),
        in_specs=[sm] + [vm] * 10 + [hbm] * 13,
        out_specs=tuple([hbm] * 8 + [vm]),
        scratch_shapes=[
            v(768, 2304), v(768, 768), v(4, 256, 1024), v(4, 256, 768), v(4, 768, 256),
            v(4, BLOCK, 256), v(768, 1024), v(768, 1024),
            v(BLOCK, 768, dtype=f32), v(BLOCK, 768, dtype=f32),
            v(BLOCK, 2304),
            v(BLOCK, 768), v(BLOCK, 384), v(BLOCK, 3072), v(BLOCK, 1536), v(BLOCK, 768),
            v(BLOCK, 384), v(BLOCK, 768), v(BLOCK, 2304), v(BLOCK, 1152),
            v(BLOCK, 768), v(BLOCK, 384),
            *(v(16 * r, c) for r, c in parts),
            *(v(8, r, c) for r, c in parts),
            *(v(4, r, c) for r, c in parts),
            *(v(4, r, c) for r, c in parts),
            *(v(r, c, dtype=f32) for r, c in parts),
            v(16 * CAP, 768), v(16 * CAP, 384), v(16 * CAP, 384), v(16 * CAP, 384),
            v(8, 16 * CAP, dtype=f32), v(BLOCK, BLOCK, dtype=f32),
            v(16, 768, dtype=f32), v(8, 2304, dtype=f32), v(8, 3072, dtype=f32),
            v(24, 768, dtype=f32), v(24, 768, dtype=f32), v(16, 16, LANES, dtype=f32),
            v(16, 16, LANES, dtype=f32), v(2, 16, LANES, dtype=f32),
            dma((9,)), dma((4,)), dma((3, 4)), dma((10,)), dma((10,)),
            dma((5, 17)), dma((5, 8)), dma((5, 4)), dma((5, 4)), dma((5,)), dma((5,)),
            dma((16,)), dma((16,)), dma((16,)), dma((16,)), dma((4,)),
        ],
        compiler_params=pltpu.CompilerParams(
            collective_id=1, has_side_effects=True, vmem_limit_bytes=62 * 2**20
        ),
    )(
        lens, feat, row, twin, cols, lse, vec, last, slot, req, stat,
        w_in, w_out, w_up, w_down, emb_t, ctx_t, first_t, act_t, dgelu, xh0, xh1, gp2, qkv,
    )


def dense_rows(text_ids, text_table):
    shards, vocab = lax.axis_size("shard"), text_table.shape[0]
    ring = [(k, (k + 1) % shards) for k in range(shards)]
    local = jnp.arange(vocab, dtype=jnp.int32)

    def step(k, carry):
        piece, rows = carry
        owner = lax.rem(lax.axis_index("shard") + shards - k, shards)
        hit = (text_ids - owner * vocab)[:, None] == local[None, :]
        return lax.ppermute(piece, "shard", ring), rows + mm(hit.astype(bf16), piece)

    rows = jnp.zeros((text_ids.shape[0], text_table.shape[1]), f32)
    return lax.fori_loop(0, shards, step, (text_table, rows))[1].astype(bf16)


def dense_sums(text_ids, looked, vocab):
    shards = lax.axis_size("shard")
    ring = [(k, (k + 1) % shards) for k in range(shards)]
    local = jnp.arange(vocab, dtype=jnp.int32)

    def step(k, total):
        owner = lax.rem(lax.axis_index("shard") + 2 * shards - 1 - k, shards)
        hit = local[:, None] == (text_ids - owner * vocab)[None, :]
        return lax.ppermute(total, "shard", ring) + mm(hit.astype(bf16), looked)

    total = lax.fori_loop(0, shards, step, jnp.zeros((vocab, looked.shape[1]), f32))
    return total + lax.ppermute(total, "rep", [(0, 1), (1, 0)])


def once(condition, body, value):
    return lax.while_loop(
        lambda state: state[0],
        lambda state: (jnp.zeros((), bool), body(state[1])),
        (condition, value),
    )[1]


def fast(*args):
    (
        region_features, text_ids, boxes, segment_ids, document_lengths, cotangent,
        batch_gain, batch_bias, text_table, side_table, embed_gain, embed_bias,
        in_weight, in_bias, out_weight, out_bias, first_gain, first_bias,
        up_weight, up_bias, down_weight, down_bias, second_gain, second_bias,
    ) = args
    vocab = text_table.shape[0]
    col = pack_indices(text_ids, boxes, segment_ids, vocab)
    row = col.T
    vec = [
        v.reshape(1, -1)
        for v in (
            batch_gain, batch_bias, embed_gain, embed_bias, out_bias, first_gain, first_bias,
            down_bias, second_gain, second_bias, in_bias, up_bias,
        )
    ]
    operands = (
        document_lengths, region_features, col, row, vec, cotangent, text_table,
        side_table, in_weight, out_weight, up_weight, down_weight,
    )
    made = forward_call(*operands)
    crowded = made[-2][3, 0] > CAP
    made = once(
        crowded,
        lambda _: tuple(forward_call(*operands, dense_rows(text_ids, text_table))),
        tuple(made),
    )
    feature_grad, looked, g_text, g_side, g_in, g_out, g_up, g_down, pieces = backward_call(
        document_lengths, region_features, row, made, vocab
    )
    g_text = once(crowded, lambda total: total + dense_sums(text_ids, looked, vocab), g_text)
    out_rows, feature_grad, g_text, g_side, g_in, g_out, g_up, g_down = place(
        made[13], feature_grad, g_text, g_side, g_in, g_out, g_up, g_down
    )
    pieces = pieces.reshape(-1)
    cut = lambda k: pieces[k * 48 : (k + 1) * 48]
    return (
        out_rows, feature_grad, cut(0), cut(1), g_text, g_side, cut(2), cut(3), g_in,
        pieces[480:576], g_out, cut(4), cut(5), cut(6), g_up, pieces[576:768], g_down, cut(7),
        cut(8), cut(9),
    )


def place_kernel(*refs):
    count = (len(refs) - 2) // 3
    sources, targets, held = refs[:count], refs[count : 2 * count], refs[2 * count : 3 * count]
    load_sem, store_sem = refs[-2:]
    loads = [
        pltpu.make_async_copy(sources[k], held[k], load_sem.at[k]) for k in range(count)
    ]
    stores = [
        pltpu.make_async_copy(held[k], targets[k], store_sem.at[k]) for k in range(count)
    ]
    for copy in loads:
        copy.start()
    for load, store in zip(loads, stores):
        load.wait()
        store.start()
    for copy in stores:
        copy.wait()


def place(*arrays):
    hbm = pl.BlockSpec(memory_space=pl.ANY)
    count = len(arrays)
    return pl.pallas_call(
        place_kernel,
        name="place",
        out_shape=tuple(shape(*a.shape, dtype=a.dtype) for a in arrays),
        in_specs=[hbm] * count,
        out_specs=tuple([hbm] * count),
        scratch_shapes=[
            *(pltpu.VMEM(a.shape, a.dtype) for a in arrays),
            pltpu.SemaphoreType.DMA((count,)),
            pltpu.SemaphoreType.DMA((count,)),
        ],
        compiler_params=pltpu.CompilerParams(vmem_limit_bytes=32 * 2**20),
    )(*arrays)


def fits(mesh):
    return dict(mesh.shape) == {"rep": 2, "shard": 16}


def solution(mesh):
    in_specs = (
        P(("rep", "shard"), None),
        P(("rep", "shard")),
        P(("rep", "shard"), None),
        P(("rep", "shard")),
        P(("rep", "shard"), None),
        P(("rep", "shard"), None),
        P("shard"),
        P("shard"),
        P("shard", None),
        P("shard", None),
        P("shard"),
        P("shard"),
        P("shard", None),
        P("shard"),
        P("shard", None),
        P("shard"),
        P("shard"),
        P("shard"),
        P("shard", None),
        P("shard"),
        P("shard", None),
        P("shard"),
        P("shard"),
        P("shard"),
    )
    out_specs = (
        P(("rep", "shard"), None),
        P(("rep", "shard"), None),
        P("shard"),
        P("shard"),
        P("shard", None),
        P("shard", None),
        P("shard"),
        P("shard"),
        P("shard", None),
        P("shard"),
        P("shard", None),
        P("shard"),
        P("shard"),
        P("shard"),
        P("shard", None),
        P("shard"),
        P("shard", None),
        P("shard"),
        P("shard"),
        P("shard"),
    )
    return jax.shard_map(
        fast if fits(mesh) else general, mesh=mesh, in_specs=in_specs, out_specs=out_specs, check_vma=False
    )
```
